32 devices in a mesh: dp: 2 (over core), modes: 16 (over z, y, x).
Axes of the slice: x: 2, y: 2, z: 4, core: 2. Of those that a mesh axis runs over, the one named last changes fastest.
Arguments:
- x_in: bfloat16 [32768, 512], P(('dp', 'modes')), may hold values from -6 to 6
- cotangent: bfloat16 [32768, 512], P(('dp', 'modes')), may hold values from -6 to 6
- block_grid: int32 [512], P(('dp', 'modes')), may hold values from 8 to 32, as said below
- keep_modes: int32 [3], replicated, may hold values from 6 to 32, as said below
- norm1_gain: float32 [2, 512], replicated, may hold values from 0.5 to 1.5
- norm1_bias: float32 [2, 512], replicated, may hold values from -1.8 to 1.8
- mix_w1: bfloat16 [2, 2, 8, 64, 64], replicated, may hold values from -0.5 to 0.5
- mix_b1: float32 [2, 2, 512], replicated, may hold values from -3 to 3
- mix_w2: bfloat16 [2, 2, 8, 64, 64], replicated, may hold values from -0.5 to 0.5
- mix_b2: float32 [2, 2, 512], replicated, may hold values from -1.8 to 1.8
- norm2_gain: float32 [2, 512], replicated, may hold values from 0.5 to 1.5
- norm2_bias: float32 [2, 512], replicated, may hold values from -1.8 to 1.8
- fc1: bfloat16 [2, 512, 512], replicated, may hold values from -0.25 to 0.25
- fc1_bias: float32 [2, 512], replicated, may hold values from -1.8 to 1.8
- fc2: bfloat16 [2, 512, 512], replicated, may hold values from -0.375 to 0.375
- fc2_bias: float32 [2, 512], replicated, may hold values from -1.8 to 1.8
Outputs:
- out: bfloat16 [32768, 512], P(('dp', 'modes'))
- x_grad: bfloat16 [32768, 512], P(('dp', 'modes'))
- norm1_gain_grad: float32 [2, 512], replicated
- norm1_bias_grad: float32 [2, 512], replicated
- mix_w1_grad: float32 [2, 2, 8, 64, 64], replicated
- mix_b1_grad: float32 [2, 2, 512], replicated
- mix_w2_grad: float32 [2, 2, 8, 64, 64], replicated
- mix_b2_grad: float32 [2, 2, 512], replicated
- norm2_gain_grad: float32 [2, 512], replicated
- norm2_bias_grad: float32 [2, 512], replicated
- fc1_grad: float32 [2, 512, 512], replicated
- fc1_bias_grad: float32 [2, 512], replicated
- fc2_grad: float32 [2, 512, 512], replicated
- fc2_bias_grad: float32 [2, 512], replicated
The draws below stay inside these ranges and needn't reach their ends.
Inputs may be any that keep to these rules, and one draw needn't show every extreme that they name: `block_grid`: each slab's 16 entries are all 32, or four quarters of 4 entries, each quarter all 16 or all 8; some slab is all 32 and some quarter is all 8. `keep_modes`: entry 0 is 8 minus a quarter of it (rounded down), entry 2 is 32, entry 1 lies between 16 minus a quarter of it (rounded down) and 16.
All inputs are finite; a program needn't handle non-finite values.
Results may differ from the reference program's by a relative error of at most 0.019.
Values may be sent and summed in bfloat16 or wider, within the bound.
No kernel may reach another device: no remote copies, remote signals or barrier semaphores. Data moves between devices by JAX's collectives and lax.ppermute only.
A program may use at most 192 MiB of HBM per device.

```python
import jax
import jax.numpy as jnp
from jax import lax

D = 512
FF = 512
BLOCKS = 8
BS = 64
GS = 8
GM = 16
GL = 32
NBLK = 16
SLAB = 1024
LAYERS = 2
SLABS_ALL = 32
ROWS = 32768


def draw_block_grid(key, part):
    key = jax.random.fold_in(key, 5)
    kinds_key, quarter_key, pick_key = jax.random.split(key, 3)
    kinds = jax.random.randint(kinds_key, (SLABS_ALL,), 0, 3)
    quarters = jax.random.randint(quarter_key, (SLABS_ALL, 4), 0, 2)
    whole_at = jax.random.randint(pick_key, (), 0, SLABS_ALL)
    slab_ids = jnp.arange(SLABS_ALL)
    small_at = (whole_at + 1) % SLABS_ALL
    kinds = jnp.where(slab_ids == whole_at, 0, kinds)
    kinds = jnp.where(slab_ids == small_at, 1, kinds)
    first = (slab_ids == small_at)[:, None] & (jnp.arange(4)[None, :] == 0)
    quarters = jnp.where(first, 1, quarters)
    grid = jnp.where(kinds[:, None] == 0, GL, jnp.where(quarters == 0, GM, GS))
    return jnp.repeat(grid, NBLK // 4, axis=1).reshape(-1).astype(jnp.int32)


def draw_keep_modes(key, part):
    key = jax.random.fold_in(key, 9)
    middle = GM - jax.random.randint(key, (), 0, GM // 4 + 1)
    return jnp.stack([jnp.int32(GS - GS // 4), middle.astype(jnp.int32), jnp.int32(GL)]).astype(jnp.int32)


def shard_levels(own_key, dims, pieces, least, largest):
    def one(position, blocks):
        heights = jax.random.uniform(jax.random.fold_in(jax.random.fold_in(own_key, 6), position), (blocks,), jnp.float32, least / len(pieces), largest / len(pieces))
        return jnp.repeat(jnp.exp(heights), dims[position] // blocks).reshape((-1,) + (1,) * (len(dims) - position - 1))

    factor_of = one(*pieces[0])
    for cut in pieces[1:]:
        factor_of = factor_of * one(*cut)
    return factor_of


def gaussian(stream_key, shape, scale, most, cuts=(), kind=jnp.bfloat16):
    loudness = shard_levels(stream_key, shape, cuts, -0.22, 0.18) if cuts else 1.0
    entries = jax.random.normal(stream_key, shape, jnp.float32) * scale * loudness
    return jnp.minimum(jnp.maximum(entries, -most), most).astype(kind)


def setup_inputs(seed: int = 0) -> dict:
    keys = jax.random.split(jax.random.key(seed), 17)
    return {
        "x_in": gaussian(keys[0], (ROWS, D), 1.0, 6.0, ((0, 32),)),
        "cotangent": gaussian(keys[1], (ROWS, D), 1.0, 6.0, ((0, 32),)),
        "block_grid": draw_block_grid(jax.random.fold_in(keys[16], 71), 0),
        "keep_modes": draw_keep_modes(jax.random.fold_in(keys[16], 71), 0),
        "norm1_gain": jnp.clip(1.0 + 0.1 * jax.random.normal(keys[4], (LAYERS, D), jnp.float32), 0.5, 1.5),
        "norm1_bias": gaussian(keys[5], (LAYERS, D), 0.3, 1.8, (), jnp.float32),
        "mix_w1": gaussian(keys[6], (LAYERS, 2, BLOCKS, BS, BS), (2 * BS) ** -0.5, 0.5),
        "mix_b1": gaussian(keys[7], (LAYERS, 2, D), 0.5, 3.0, (), jnp.float32),
        "mix_w2": gaussian(keys[8], (LAYERS, 2, BLOCKS, BS, BS), (2 * BS) ** -0.5, 0.5),
        "mix_b2": gaussian(keys[9], (LAYERS, 2, D), 0.3, 1.8, (), jnp.float32),
        "norm2_gain": jnp.clip(1.0 + 0.1 * jax.random.normal(keys[10], (LAYERS, D), jnp.float32), 0.5, 1.5),
        "norm2_bias": gaussian(keys[11], (LAYERS, D), 0.3, 1.8, (), jnp.float32),
        "fc1": gaussian(keys[12], (LAYERS, D, FF), D ** -0.5, 0.25),
        "fc1_bias": gaussian(keys[13], (LAYERS, FF), 0.3, 1.8, (), jnp.float32),
        "fc2": gaussian(keys[14], (LAYERS, FF, D), (FF // 2) ** -0.5, 0.375),
        "fc2_bias": gaussian(keys[15], (LAYERS, D), 0.3, 1.8, (), jnp.float32),
    }


@jax.custom_vjp
def low(v):
    return lax.optimization_barrier(v.astype(jnp.bfloat16)).astype(jnp.float32)

@jax.custom_vjp
def low_back(v):
    return v

def low_keep(v):
    return (low(v), None)

def low_pass(kept, grad):
    return (grad,)

def back_keep(v):
    return (v, None)

def back_low(kept, grad):
    return (low(grad),)
low.defvjp(low_keep, low_pass)
low_back.defvjp(back_keep, back_low)
HIGH = lax.Precision.HIGHEST

def dft_tables(grid_blocks, keep, slab_rows):
    rows = jnp.arange(slab_rows, dtype=jnp.int32)
    count = grid_blocks.shape[0]
    blk = rows // (slab_rows // count)
    match = (blk[:, None] == jnp.arange(count, dtype=jnp.int32)[None, :]).astype(jnp.int32)
    grid = lax.optimization_barrier(jnp.sum(match * grid_blocks.astype(jnp.int32)[None, :], axis=1)).astype(jnp.int32)
    span = grid * grid
    start = rows // span * span
    local = rows - start
    prow = local // grid
    pcol = local % grid
    keep_now = jnp.where(grid == GS, keep[0], jnp.where(grid == GM, keep[1], keep[2])).astype(jnp.int32)
    used = (prow < keep_now) & (pcol < keep_now)
    same = start[:, None] == start[None, :]
    phase = (prow[:, None] * prow[None, :] + pcol[:, None] * pcol[None, :]) % grid[:, None]
    sidef = grid.astype(jnp.float32)[:, None]
    angle = phase.astype(jnp.float32) * (2.0 * jnp.pi) / sidef
    live = same & used[:, None]
    table_re = jnp.where(live, jnp.cos(angle) / sidef, jnp.float32(0.0))
    table_im = jnp.where(live, -jnp.sin(angle) / sidef, jnp.float32(0.0))
    return (table_re, table_im)

def layer_norm(x, gain, shift):
    mean = lax.optimization_barrier(jnp.mean(x, -1, keepdims=True))
    cent = x - mean
    var = lax.optimization_barrier(jnp.mean(cent * cent, -1, keepdims=True))
    return cent * lax.rsqrt(var + 1e-05) * gain + shift

def shrink(v):
    return v - 0.05 * v * lax.rsqrt(v * v + 0.0025)

def spectral(table, x):
    slabs = table.shape[0]
    out = jnp.einsum('srp,spd->srd', table, x.reshape(slabs, table.shape[2], -1), precision=HIGH)
    return out.reshape(x.shape)

def synth(table, x):
    slabs = table.shape[0]
    out = jnp.einsum('srp,srd->spd', table, x.reshape(slabs, table.shape[1], -1), precision=HIGH)
    return out.reshape(x.shape)

def block_mix(real, imag, weight, bias):
    n = real.shape[0]
    part_re = real.reshape(n, BLOCKS, -1)
    part_im = imag.reshape(n, BLOCKS, -1)

    def prod(a, w):
        return jnp.einsum('nkc,kcd->nkd', a, w, precision=HIGH)
    out_re = prod(part_re, weight[0]) - prod(part_im, weight[1])
    out_im = prod(part_re, weight[1]) + prod(part_im, weight[0])
    return (out_re.reshape(n, -1) + bias[0], out_im.reshape(n, -1) + bias[1])

def forward(params, hidden, table_re, table_im):
    gain1, shift1, weight1, bias1, weight2, bias2, gain2, shift2, dense1, dbias1, dense2, dbias2 = params
    for layer in range(LAYERS):
        u = layer_norm(hidden, gain1[layer], shift1[layer])
        u_low = low(u)
        z_re = low_back(low(spectral(table_re, u_low)))
        z_im = low_back(low(spectral(table_im, u_low)))
        a_re, a_im = block_mix(z_re, z_im, weight1[layer], bias1[layer])
        o_re = low(jax.nn.gelu(low_back(a_re)))
        o_im = low(jax.nn.gelu(low_back(a_im)))
        e_re, e_im = block_mix(o_re, o_im, weight2[layer], bias2[layer])
        s_re = low_back(low(shrink(low_back(e_re))))
        s_im = low_back(low(shrink(low_back(e_im))))
        y = low_back(synth(table_re, s_re) + synth(table_im, s_im))
        mid = hidden + y + u
        v = low(layer_norm(mid, gain2[layer], shift2[layer]))
        pre = low_back(jnp.dot(v, dense1[layer], precision=HIGH) + dbias1[layer])
        act = low(jax.nn.gelu(pre))
        branch = low_back(jnp.dot(act, dense2[layer], precision=HIGH))
        hidden = mid + branch + dbias2[layer]
    return hidden

def reference(x_in, cotangent, block_grid, keep_modes, norm1_gain, norm1_bias, mix_w1, mix_b1, mix_w2, mix_b2, norm2_gain, norm2_bias, fc1, fc1_bias, fc2, fc2_bias):
    params = tuple((p.astype(jnp.float32) for p in (norm1_gain, norm1_bias, mix_w1, mix_b1, mix_w2, mix_b2, norm2_gain, norm2_bias, fc1, fc1_bias, fc2, fc2_bias)))
    groups = SLABS_ALL // 4
    inputs = x_in.reshape(groups, 4 * SLAB, D)
    cots = cotangent.reshape(groups, 4 * SLAB, D)
    grids = block_grid.reshape(groups, 4, NBLK)
    keep = keep_modes.astype(jnp.int32)

    def step(acc, item):
        xg, cg, gg = item
        table_re, table_im = jax.vmap(lambda g: dft_tables(g, keep, SLAB))(gg)
        table_re = low(table_re)
        table_im = low(table_im)
        out, pull = jax.vjp(lambda ps, xx: forward(ps, xx, table_re, table_im), params, xg.astype(jnp.float32))
        dparams, dx = pull(cg.astype(jnp.float32))
        acc = jax.tree.map(lambda a, b: a + b, acc, dparams)
        return (acc, (out.astype(jnp.bfloat16), dx.astype(jnp.bfloat16)))
    zeros = jax.tree.map(jnp.zeros_like, params)
    sums, (outs, grads) = lax.scan(step, zeros, (inputs, cots, grids))
    return (outs.reshape(ROWS, D), grads.reshape(ROWS, D), sums[0], sums[1], sums[2], sums[3], sums[4], sums[5], sums[6], sums[7], sums[8], sums[9], sums[10], sums[11])
```

```python
import math
from functools import partial

import jax
import jax.numpy as jnp
from jax import lax
from jax.experimental import pallas as pl
from jax.experimental.pallas import tpu as pltpu
from jax.sharding import PartitionSpec as P

LAYERS = 2
NBLK = 16
F32 = jnp.float32
BF = jnp.bfloat16
C0 = math.sqrt(2.0 / math.pi)
C1 = 0.044715 * C0
PER = 1296
RT = 256
CH = 64


def nn(a, b):
    return jnp.dot(a, b, preferred_element_type=F32)


def nt(a, b):
    return lax.dot_general(a, b, (((1,), (1,)), ((), ())), preferred_element_type=F32)


def tn(a, b):
    return lax.dot_general(a, b, (((0,), (0,)), ((), ())), preferred_element_type=F32)


def gelu_pair(x):
    x2 = x * x
    p = 0.5 + 0.5 * jnp.tanh(x * (C0 + C1 * x2))
    y = x * p
    return y, p + y * (1.0 - p) * (2.0 * C0 + (6.0 * C1) * x2)


def cos_sin(t):
    x = t - 0.5
    w = (2.0 * math.pi * x) ** 2
    c = jnp.full_like(w, 1.0 / math.factorial(16))
    s = jnp.full_like(w, -1.0 / math.factorial(15))
    for k in range(7, -1, -1):
        c = c * w + (-1.0) ** k / math.factorial(2 * k)
        if k < 7:
            s = s * w + (-1.0) ** k / math.factorial(2 * k + 1)
    return -c, -s * (2.0 * math.pi * x)


def pick(values, block):
    out = jnp.zeros(block.shape, jnp.int32)
    for j in range(NBLK):
        out = jnp.where(block == j, values[j], out)
    return out


def split(index, grid):
    span = grid * grid
    start = index & ~(span - 1)
    local = index & (span - 1)
    lg = jnp.where(grid == 8, 3, jnp.where(grid == 16, 4, 5))
    return start, lax.shift_right_logical(local, lg), local & (grid - 1)


def build_tables(grid_ref, keep_ref, cre, cim, m1, m2, m3):
    rows = cre.shape[0]
    unit = rows // NBLK
    vals = [grid_ref[j] for j in range(NBLK)]
    keep = [keep_ref[j] for j in range(3)]
    lane = lax.broadcasted_iota(jnp.int32, (8, rows), 1)
    gc = pick(vals, lane // unit)
    start_c, p_c, q_c = split(lane, gc)
    ginv = 1.0 / gc.astype(F32)
    sub = lax.broadcasted_iota(jnp.int32, (8, rows), 0)
    bcs = []
    for j in range(4):
        q_r = (sub + 8 * j) & (gc - 1)
        t = ((q_r * q_c) & (gc - 1)).astype(F32) * ginv
        bcs.append(cos_sin(t))

    def step(i, carry):
        blk = sub + 8 * i
        r = blk * 8
        gb = jnp.full((8, rows), 0, jnp.int32) + grid_ref[(64 * i) // unit]
        start_b, p_b, _ = split(r, gb)
        t = ((p_b * p_c) & (gc - 1)).astype(F32) * ginv
        ac, as_ = cos_sin(t)
        same = jnp.where(start_b == start_c, ginv, 0.0)
        ac = ac * same
        as_ = as_ * same
        for j in range(8):
            bc, bs = bcs[j % 4]
            a1 = ac[j : j + 1, :]
            a2 = as_[j : j + 1, :]
            if j % 2 == 0:
                bc2, bs2 = bcs[(j + 1) % 4]
                b1 = ac[j + 1 : j + 2, :]
                b2 = as_[j + 1 : j + 2, :]
                re = jnp.concatenate([a1 * bc - a2 * bs, b1 * bc2 - b2 * bs2], 0)
                im = jnp.concatenate([-(a2 * bc + a1 * bs), -(b2 * bc2 + b1 * bs2)], 0)
                dst = pl.ds(pl.multiple_of(i * 64 + j * 8, 16), 16)
                cre[dst, :] = re.astype(BF)
                cim[dst, :] = im.astype(BF)
        return carry

    lax.fori_loop(0, rows // 64, step, 0)

    def mask(i, carry):
        r = lax.broadcasted_iota(jnp.int32, (64, 128), 0) + 64 * i
        gb = jnp.full((64, 128), 0, jnp.int32) + grid_ref[(64 * i) // unit]
        _, p, q = split(r, gb)
        k = jnp.where(gb == 8, keep[0], jnp.where(gb == 16, keep[1], keep[2]))
        m = jnp.where((p < k) & (q < k), 1.0, 0.0)
        dst = pl.ds(pl.multiple_of(i * 64, 64), 64)
        m1[dst, :] = m
        m2[dst, :] = m * 0.05
        m3[dst, :] = m * (0.05 * 0.0025)
        return carry

    lax.fori_loop(0, rows // 64, mask, 0)


def build_mix(w_ref, out_ref):
    i = lax.broadcasted_iota(jnp.int32, (64, 128), 0)
    j = lax.broadcasted_iota(jnp.int32, (64, 128), 1)
    dup = jnp.where((j & 63) == i, 1.0, 0.0).astype(BF)
    r = lax.broadcasted_iota(jnp.int32, (512, 128), 0)
    c = lax.broadcasted_iota(jnp.int32, (512, 128), 1)
    diag = ((r // 64) & 1) == (c // 64)
    for layer in range(LAYERS):
        re = jnp.where(diag, nn(w_ref[layer, 0], dup), 0.0)
        im = jnp.where(diag, nn(w_ref[layer, 1], dup), 0.0)
        for g in range(4):
            a = re[g * 128 : (g + 1) * 128].astype(BF)
            b = im[g * 128 : (g + 1) * 128]
            out_ref[layer, g, 0:128, 0:128] = a
            out_ref[layer, g, 128:256, 128:256] = a
            out_ref[layer, g, 0:128, 128:256] = b.astype(BF)
            out_ref[layer, g, 128:256, 0:128] = (-b).astype(BF)


def fold(x):
    return jnp.sum(x.reshape(x.shape[0] // 8, 8, x.shape[1]), 0)


def kernel(
    grid_ref, keep_ref, x_ref, cot_ref,
    n1g, n1b, w1, b1, w2, b2, n2g, n2b, fc1, fb1, fc2, fb2,
    out_ref, xg_ref, grads_ref,
    cre, cim, m1, m2, m3, w1g, w2g,
    xh1, rs1, hu, ul, z, o, da, ds, sr, si, xh2, rs2, v, act, dp,
    gm, gmid, acc,
):
    g_s, gy, gzr, gzi = hu, ul, sr, si
    rows = x_ref.shape[0]
    tiles = rows // RT
    build_tables(grid_ref, keep_ref, cre, cim, m1, m2, m3)
    build_mix(w1, w1g)
    build_mix(w2, w2g)
    acc[...] = jnp.zeros_like(acc)

    def tile(i):
        return pl.ds(pl.multiple_of(i * RT, RT), RT)

    def chunk(i, j):
        return pl.ds(pl.multiple_of(i * RT + j * CH, CH), CH)

    def add_to(layer, k, x):
        acc[layer, k] = acc[layer, k] + fold(x)

    def norm1(layer, dst, h):
        mean = jnp.mean(h, -1, keepdims=True)
        cent = h - mean
        rstd = lax.rsqrt(jnp.mean(cent * cent, -1, keepdims=True) + 1e-05)
        xh = cent * rstd
        u = xh * n1g[layer : layer + 1, :] + n1b[layer : layer + 1, :]
        xh1[layer, dst, :] = xh
        rs1[layer, dst, :] = jnp.broadcast_to(rstd, (CH, 128))
        ul[dst, :] = u.astype(BF)
        hu[dst, :] = h + u

    def enter(i, carry):
        for j in range(RT // CH):
            dst = chunk(i, j)
            norm1(0, dst, x_ref[dst, :].astype(F32))
        return carry

    lax.fori_loop(0, tiles, enter, 0)

    def mix_forward(layer):
        def body(i, carry):
            dst = tile(i)
            zr = nn(cre[dst, :], ul[...]).astype(BF)
            zi = nn(cim[dst, :], ul[...]).astype(BF)
            k1 = jnp.concatenate([m1[dst, :]] * 2, 1)
            k2 = jnp.concatenate([m2[dst, :]] * 2, 1)
            k3 = jnp.concatenate([m3[dst, :]] * 2, 1)
            for g in range(4):
                sl = slice(g * 128, (g + 1) * 128)
                gl = slice(g * 256, (g + 1) * 256)
                zg = jnp.concatenate([zr[:, sl], zi[:, sl]], 1)
                z[layer, dst, gl] = zg
                bias1 = jnp.concatenate([b1[layer, 0:1, sl], b1[layer, 1:2, sl]], 1)
                a = nn(zg, w1g[layer, g]) + bias1
                og, dag = gelu_pair(a)
                og = og.astype(BF)
                o[layer, dst, gl] = og
                da[layer, dst, gl] = dag.astype(BF)
                bias2 = jnp.concatenate([b2[layer, 0:1, sl], b2[layer, 1:2, sl]], 1)
                e = nn(og, w2g[layer, g]) + bias2
                r = lax.rsqrt(e * e + 0.0025)
                s = e * (k1 - k2 * r)
                ds[layer, dst, gl] = (k1 - k3 * (r * r * r)).astype(BF)
                sr[dst, sl] = s[:, 0:128].astype(BF)
                si[dst, sl] = s[:, 128:256].astype(BF)
            return carry

        lax.fori_loop(0, tiles, body, 0)

    def ff_forward(layer):
        def body(i, carry):
            dst = tile(i)
            y = nn(cre[dst, :], sr[...]) + nn(cim[dst, :], si[...])
            mids = []
            for j in range(RT // CH):
                cd = chunk(i, j)
                mid = y[j * CH : (j + 1) * CH] + hu[cd, :]
                mean = jnp.mean(mid, -1, keepdims=True)
                cent = mid - mean
                rstd = lax.rsqrt(jnp.mean(cent * cent, -1, keepdims=True) + 1e-05)
                xh = cent * rstd
                xh2[layer, cd, :] = xh
                rs2[layer, cd, :] = jnp.broadcast_to(rstd, (CH, 128))
                v[layer, cd, :] = (xh * n2g[layer : layer + 1, :] + n2b[layer : layer + 1, :]).astype(BF)
                hu[cd, :] = mid
            pre = nn(v[layer, dst, :], fc1[layer]) + fb1[layer : layer + 1, :]
            ac, dpre = gelu_pair(pre)
            act[layer, dst, :] = ac.astype(BF)
            dp[layer, dst, :] = dpre.astype(BF)
            br = nn(ac.astype(BF), fc2[layer])
            for j in range(RT // CH):
                cd = chunk(i, j)
                h = hu[cd, :] + (br[j * CH : (j + 1) * CH] + fb2[layer : layer + 1, :])
                if layer == LAYERS - 1:
                    out_ref[cd, :] = h.astype(BF)
                else:
                    norm1(layer + 1, cd, h)
            return carry

        lax.fori_loop(0, tiles, body, 0)

    for layer in range(LAYERS):
        mix_forward(layer)
        ff_forward(layer)

    def norm_back(gv, xh, rstd, gain):
        t = gv * gain
        mt = jnp.mean(t, -1, keepdims=True)
        mx = jnp.mean(t * xh, -1, keepdims=True)
        return rstd * (t - mt - xh * mx)

    def ff_backward(layer):
        def body(i, carry):
            dst = tile(i)
            if layer == LAYERS - 1:
                g = cot_ref[dst, :].astype(F32)
            else:
                g = g_s[dst, :]
            add_to(layer, 9, g)
            gmt = g.astype(BF)
            gm[dst, :] = gmt
            gact = nt(gmt, fc2[layer])
            gpre = gact * dp[layer, dst, :].astype(F32)
            add_to(layer, 8, gpre)
            gpt = gpre.astype(BF)
            dp[layer, dst, :] = gpt
            gv = nt(gpt, fc1[layer])
            for j in range(RT // CH):
                cd = chunk(i, j)
                gvc = gv[j * CH : (j + 1) * CH]
                xh = xh2[layer, cd, :]
                add_to(layer, 6, gvc * xh)
                add_to(layer, 7, gvc)
                rstd = jnp.concatenate([rs2[layer, cd, :]] * 4, 1)
                gmc = g[j * CH : (j + 1) * CH] + norm_back(gvc, xh, rstd, n2g[layer : layer + 1, :])
                gmid[cd, :] = gmc
                gy[cd, :] = gmc.astype(BF)
            return carry

        lax.fori_loop(0, tiles, body, 0)
        base = layer * PER
        for h in range(2):
            hs = slice(h * 256, (h + 1) * 256)
            grads_ref[base + h * 256 : base + (h + 1) * 256, :] = tn(v[layer, :, hs], dp[layer]).astype(BF)
            grads_ref[base + 512 + h * 256 : base + 512 + (h + 1) * 256, :] = tn(act[layer, :, hs], gm[...]).astype(BF)

    def mix_backward(layer):
        def body(i, carry):
            dst = tile(i)
            gsr = nn(cre[dst, :], gy[...])
            gsi = nn(cim[dst, :], gy[...])
            for g in range(4):
                sl = slice(g * 128, (g + 1) * 128)
                gl = slice(g * 256, (g + 1) * 256)
                gs = jnp.concatenate([gsr[:, sl], gsi[:, sl]], 1)
                gef = gs * ds[layer, dst, gl].astype(F32)
                fe = fold(gef)
                acc[layer, 4, :, sl] += fe[:, 0:128]
                acc[layer, 5, :, sl] += fe[:, 128:256]
                geb = gef.astype(BF)
                ds[layer, dst, gl] = geb
                gaf = nt(geb, w2g[layer, g]) * da[layer, dst, gl].astype(F32)
                fa = fold(gaf)
                acc[layer, 2, :, sl] += fa[:, 0:128]
                acc[layer, 3, :, sl] += fa[:, 128:256]
                gab = gaf.astype(BF)
                da[layer, dst, gl] = gab
                gz = nt(gab, w1g[layer, g]).astype(BF)
                gzr[dst, sl] = gz[:, 0:128]
                gzi[dst, sl] = gz[:, 128:256]
            return carry

        lax.fori_loop(0, tiles, body, 0)
        base = layer * PER + 1024
        low = lax.broadcasted_iota(jnp.int32, (64, 128), 1) < 64
        for left, right, off in ((o, ds, base + 128), (z, da, base)):
            for g in range(4):
                sl = slice(g * 128, (g + 1) * 128)
                gl = slice(g * 256, (g + 1) * 256)
                p = tn(left[layer, :, gl], right[layer, :, gl])
                re = p[0:128, 0:128] + p[128:256, 128:256]
                im = p[0:128, 128:256] - p[128:256, 0:128]
                grads_ref[off : off + 64, sl] = jnp.where(low, re[0:64], re[64:128]).astype(BF)
                grads_ref[off + 64 : off + 128, sl] = jnp.where(low, im[0:64], im[64:128]).astype(BF)

    def in_backward(layer):
        def body(i, carry):
            dst = tile(i)
            y = nn(cre[dst, :], gzr[...]) + nn(cim[dst, :], gzi[...])
            for j in range(RT // CH):
                cd = chunk(i, j)
                gmc = gmid[cd, :]
                gu = y[j * CH : (j + 1) * CH] + gmc
                xh = xh1[layer, cd, :]
                add_to(layer, 0, gu * xh)
                add_to(layer, 1, gu)
                rstd = jnp.concatenate([rs1[layer, cd, :]] * 4, 1)
                gh = gmc + norm_back(gu, xh, rstd, n1g[layer : layer + 1, :])
                if layer == 0:
                    xg_ref[cd, :] = gh.astype(BF)
                else:
                    g_s[cd, :] = gh
            return carry

        lax.fori_loop(0, tiles, body, 0)

    for layer in reversed(range(LAYERS)):
        ff_backward(layer)
        mix_backward(layer)
        in_backward(layer)

    for layer in range(LAYERS):
        t = jnp.sum(acc[layer], 1)
        t = jnp.concatenate([t, jnp.zeros((6, 512), F32)], 0)
        grads_ref[layer * PER + 1280 : layer * PER + 1296, :] = t.astype(BF)


def local_step(x_in, cotangent, block_grid, keep_modes, n1g, n1b, w1, b1, w2, b2, n2g, n2b, fc1, fb1, fc2, fb2):
    rows, d = x_in.shape
    vm = pl.BlockSpec(memory_space=pltpu.VMEM)
    sm = pl.BlockSpec(memory_space=pltpu.SMEM)
    w1r = w1.reshape(LAYERS, 2, 512, 64)
    w2r = w2.reshape(LAYERS, 2, 512, 64)
    scratch = [
        pltpu.VMEM((rows, rows), BF), pltpu.VMEM((rows, rows), BF),
        pltpu.VMEM((rows, 128), F32), pltpu.VMEM((rows, 128), F32), pltpu.VMEM((rows, 128), F32),
        pltpu.VMEM((LAYERS, 4, 256, 256), BF), pltpu.VMEM((LAYERS, 4, 256, 256), BF),
        pltpu.VMEM((LAYERS, rows, d), F32), pltpu.VMEM((LAYERS, rows, 128), F32),
        pltpu.VMEM((rows, d), F32), pltpu.VMEM((rows, d), BF),
        pltpu.VMEM((LAYERS, rows, 2 * d), BF), pltpu.VMEM((LAYERS, rows, 2 * d), BF),
        pltpu.VMEM((LAYERS, rows, 2 * d), BF), pltpu.VMEM((LAYERS, rows, 2 * d), BF),
        pltpu.VMEM((rows, d), BF), pltpu.VMEM((rows, d), BF),
        pltpu.VMEM((LAYERS, rows, d), F32), pltpu.VMEM((LAYERS, rows, 128), F32),
        pltpu.VMEM((LAYERS, rows, d), BF), pltpu.VMEM((LAYERS, rows, d), BF), pltpu.VMEM((LAYERS, rows, d), BF),
        pltpu.VMEM((rows, d), BF), pltpu.VMEM((rows, d), F32),
        pltpu.VMEM((LAYERS, 10, 8, d), F32),
    ]
    return pl.pallas_call(
        kernel,
        out_shape=(
            jax.ShapeDtypeStruct((rows, d), BF),
            jax.ShapeDtypeStruct((rows, d), BF),
            jax.ShapeDtypeStruct((LAYERS * PER, d), BF),
        ),
        in_specs=[sm, sm] + [vm] * 14,
        out_specs=(vm, vm, vm),
        scratch_shapes=scratch,
        compiler_params=pltpu.CompilerParams(vmem_limit_bytes=60 * 1024 * 1024),
        name="slab_step",
    )(block_grid, keep_modes, x_in, cotangent, n1g, n1b, w1r, b1, w2r, b2, n2g, n2b, fc1, fb1, fc2, fb2)


def unpack(flat):
    per = flat.reshape(LAYERS, PER, 512).astype(F32)
    fc1g = per[:, 0:512]
    fc2g = per[:, 512:1024]

    def mix(t):
        return t.reshape(LAYERS, 2, 64, 8, 64).transpose(0, 1, 3, 2, 4)

    vec = per[:, 1280:1296]
    return (
        vec[:, 0], vec[:, 1], mix(per[:, 1024:1152]), vec[:, 2:4], mix(per[:, 1152:1280]), vec[:, 4:6],
        vec[:, 6], vec[:, 7], fc1g, vec[:, 8], fc2g, vec[:, 9],
    )


AXES = ("dp", "modes")


def exchange(a, bit, count):
    return lax.ppermute(a, AXES, [(i, i ^ bit) for i in range(count)])


def all_sum(flat, count):
    me = lax.axis_index(AXES)
    bits = [count // 2] + [1 << k for k in range((count // 2).bit_length() - 1)]
    halves = []
    for bit in bits:
        if flat.shape[0] <= 162:
            got = exchange(flat, bit, count)
            flat = (flat.astype(F32) + got.astype(F32)).astype(BF)
            continue
        n = flat.shape[0] // 2
        high = (me & bit) != 0
        low_half, high_half = flat[:n], flat[n:]
        mine = jnp.where(high, high_half, low_half)
        got = exchange(jnp.where(high, low_half, high_half), bit, count)
        flat = (mine.astype(F32) + got.astype(F32)).astype(BF)
        halves.append((bit, high))
    for bit, high in reversed(halves):
        got = exchange(flat, bit, count)
        flat = jnp.where(high, jnp.concatenate([got, flat]), jnp.concatenate([flat, got]))
    return flat


def solution(mesh):
    count = mesh.shape["dp"] * mesh.shape["modes"]

    def on_device(*args):
        out, x_grad, flat = local_step(*args)
        return (out, x_grad) + unpack(all_sum(flat, count))

    rows = P(AXES, None)
    return jax.shard_map(
        on_device,
        mesh=mesh,
        in_specs=(rows, rows, P(AXES)) + (P(),) * 13,
        out_specs=(rows, rows) + (P(),) * 12,
        check_vma=False,
    )
```

```python
import math
from functools import partial

import jax
import jax.numpy as jnp
from jax import lax
from jax.experimental import pallas as pl
from jax.experimental.pallas import tpu as pltpu
from jax.sharding import PartitionSpec as P

LAYERS = 2
NBLK = 16
F32 = jnp.float32
BF = jnp.bfloat16
C0 = math.sqrt(2.0 / math.pi)
C1 = 0.044715 * C0
PER = 1344
RT = 256
ST = 256
NH = 512
CH = 64
CE = 32
CF = 16


def nn(a, b):
    return jnp.dot(a, b, preferred_element_type=F32)


def nt(a, b):
    return lax.dot_general(a, b, (((1,), (1,)), ((), ())), preferred_element_type=F32)


def tn(a, b):
    return lax.dot_general(a, b, (((0,), (0,)), ((), ())), preferred_element_type=F32)


def gelu_pair(x):
    x2 = x * x
    p = 0.5 + 0.5 * jnp.tanh(x * (C0 + C1 * x2))
    y = x * p
    return y, p + y * (1.0 - p) * (2.0 * C0 + (6.0 * C1) * x2)


def gelu_split(x):
    p = 0.5 + 0.5 * jnp.tanh(x * (C0 + C1 * (x * x)))
    y = (x * p).astype(BF)
    xb, pb, qb = x.astype(BF), p.astype(BF), (1.0 - p).astype(BF)
    return y, pb + y * qb * (2.0 * C0 + (6.0 * C1) * (xb * xb))


def cos_of(t):
    x = t - 0.5
    w = (2.0 * math.pi * x) ** 2
    c = jnp.full_like(w, 1.0 / math.factorial(16))
    for k in range(7, -1, -1):
        c = c * w + (-1.0) ** k / math.factorial(2 * k)
    return -c


def cos_sin(t):
    x = t - 0.5
    w = (2.0 * math.pi * x) ** 2
    c = jnp.full_like(w, 1.0 / math.factorial(16))
    s = jnp.full_like(w, -1.0 / math.factorial(15))
    for k in range(7, -1, -1):
        c = c * w + (-1.0) ** k / math.factorial(2 * k)
        if k < 7:
            s = s * w + (-1.0) ** k / math.factorial(2 * k + 1)
    return -c, -s * (2.0 * math.pi * x)


def pick(values, block):
    out = jnp.zeros(block.shape, jnp.int32)
    for j in range(NBLK):
        out = jnp.where(block == j, values[j], out)
    return out


def log_of(grid):
    return jnp.where(grid == 8, 3, jnp.where(grid == 16, 4, 5))


def slot_of(slot, grid):
    half = grid * grid // 2
    local = slot & (half - 1)
    pp = lax.shift_right_logical(local, log_of(grid))
    qq = local & (grid - 1)
    mid = lax.shift_right_logical(grid, 1)
    first = pp == 0
    special = first & ((qq == 0) | (qq == mid))
    p = jnp.where(first & (qq >= mid), mid, pp)
    q = jnp.where(first & (qq == mid), 0, qq)
    pm = jnp.where(special, p, (grid - p) & (grid - 1))
    qm = jnp.where(special, mid, (grid - q) & (grid - 1))
    return 2 * (slot - local), p, q, special, pm, qm


def build_tables(grid_ref, keep_ref, at, k1, k2, k3, nm, nb):
    rows = at.shape[1]
    slots = rows // 2
    unit = slots // NBLK
    vals = [grid_ref[j] for j in range(NBLK)]
    lane = lax.broadcasted_iota(jnp.int32, (8, rows), 1)
    sub = lax.broadcasted_iota(jnp.int32, (8, rows), 0)
    gc = pick(vals, lane // (2 * unit))
    span = gc * gc
    start_c = lane & ~(span - 1)
    local = lane & (span - 1)
    p_c = lax.shift_right_logical(local, log_of(gc))
    q_c = local & (gc - 1)
    ginv = 1.0 / gc.astype(F32)
    bcs = []
    for j in range(4):
        q_r = (sub + 8 * j) & (gc - 1)
        bcs.append(cos_sin(((q_r * q_c) & (gc - 1)).astype(F32) * ginv))

    def two(x):
        return jnp.concatenate([x, x], 0)

    gc2, start2, p2, q2, ginv2, sub2 = two(gc), two(start_c), two(p_c), two(q_c), two(ginv), lax.broadcasted_iota(jnp.int32, (16, rows), 0)

    def step(i, carry):
        slot = (sub + 8 * i) * 8
        gb = jnp.where(sub < 4, grid_ref[2 * i], grid_ref[2 * i + 1])
        half = gb * gb // 2
        loc = slot & (half - 1)
        p_b = lax.shift_right_logical(loc, log_of(gb))
        ac, as_ = cos_sin(((p_b * p_c) & (gc - 1)).astype(F32) * ginv)
        same = jnp.where(2 * (slot - loc) == start_c, ginv, 0.0)
        ac = ac * same
        as_ = as_ * same
        for j in range(0, 8, 2):
            re, im = [], []
            for d in range(2):
                bc, bs = bcs[(j + d) % 4]
                a1 = ac[j + d : j + d + 1, :]
                a2 = as_[j + d : j + d + 1, :]
                re.append(a1 * bc - a2 * bs)
                im.append(-(a2 * bc + a1 * bs))
            s0 = pl.multiple_of(i * 64 + j * 8, 16)
            at[pl.ds(s0, 16), :] = jnp.concatenate(re, 0).astype(BF)
            at[pl.ds(slots + s0, 16), :] = jnp.concatenate(im, 0).astype(BF)
            g = grid_ref[2 * i + j // 4]
            first = (s0 & (g * g // 2 - 1)) < g

            @pl.when(first)
            def _():
                gv = jnp.full((16, rows), 0, jnp.int32) + g
                start, p, q, special, pm, qm = slot_of(sub2 + s0, gv)
                live = jnp.where(start == start2, ginv2, 0.0)
                t = ((p * p2 + q * q2) & (gc2 - 1)).astype(F32) * ginv2
                tm = ((pm * p2 + qm * q2) & (gc2 - 1)).astype(F32) * ginv2
                quarter = jnp.where(t >= 0.75, t - 0.75, t + 0.25)
                at[pl.ds(s0, 16), :] = (cos_of(t) * live).astype(BF)
                at[pl.ds(slots + s0, 16), :] = (cos_of(jnp.where(special, tm, quarter)) * live).astype(BF)

        return carry

    lax.fori_loop(0, slots // 64, step, 0)

    def mask(i, carry):
        slot = lax.broadcasted_iota(jnp.int32, (unit, 128), 0) + unit * i
        g = jnp.full((unit, 128), 0, jnp.int32) + grid_ref[i]
        _, p, q, special, pm, qm = slot_of(slot, g)
        k = jnp.where(g == 8, keep_ref[0], jnp.where(g == 16, keep_ref[1], keep_ref[2]))
        plus = jnp.where((p < k) & (q < k), 1.0, 0.0)
        minus = jnp.where((pm < k) & (qm < k), 1.0, 0.0)
        n = jnp.where(special, 0.0, 1.0)
        dst = pl.ds(pl.multiple_of(i * unit, unit), unit)
        nm[dst, :] = n.astype(BF)
        nb[dst, :] = (1.0 - n).astype(BF)
        for sign, (m, im) in enumerate(((plus, plus * n), (minus, -minus * n))):
            for ref, f in ((k1, 1.0), (k2, 0.05), (k3, 0.05 * 0.0025)):
                ref[sign, dst, 0:128] = (m * f).astype(BF)
                ref[sign, dst, 128:256] = (im * f).astype(BF)
        return carry

    lax.fori_loop(0, NBLK, mask, 0)


def build_mix(w_ref, out_ref):
    i = lax.broadcasted_iota(jnp.int32, (64, 128), 0)
    j = lax.broadcasted_iota(jnp.int32, (64, 128), 1)
    dup = jnp.where((j & 63) == i, 1.0, 0.0).astype(BF)
    r = lax.broadcasted_iota(jnp.int32, (512, 128), 0)
    c = lax.broadcasted_iota(jnp.int32, (512, 128), 1)
    diag = ((r // 64) & 1) == (c // 64)
    for layer in range(LAYERS):
        re = jnp.where(diag, nn(w_ref[layer, 0], dup), 0.0)
        im = jnp.where(diag, nn(w_ref[layer, 1], dup), 0.0)
        for g in range(4):
            a = re[g * 128 : (g + 1) * 128].astype(BF)
            b = im[g * 128 : (g + 1) * 128]
            out_ref[layer, g, 0:128, 0:128] = a
            out_ref[layer, g, 128:256, 128:256] = a
            out_ref[layer, g, 0:128, 128:256] = b.astype(BF)
            out_ref[layer, g, 128:256, 0:128] = (-b).astype(BF)


def fold(x):
    return jnp.sum(x.reshape(x.shape[0] // 8, 8, x.shape[1]), 0)


def kernel(
    grid_ref, keep_ref, core_ref, x_ref, cot_ref,
    n1g, n1b, w1, b1, w2, b2, n2g, n2b, fc1, fb1, fc2, fb2,
    out_ref, xg_ref, grads_ref,
    at, st, k1, k2, k3, nm, nb, w1g, w2g,
    xh1, rs1, hu, ul, z, o, da, ds, pq, xh2, rs2, v, act, dp,
    gm, gmid, acc,
):
    g_s, gy = hu, ul
    rows = x_ref.shape[0]
    slots = rows // 2
    tiles = rows // RT
    stiles = slots // ST
    build_tables(grid_ref, keep_ref, at, k1, k2, k3, nm, nb)
    for i in range(4):
        st[:, i * 256 : (i + 1) * 256] = at[i * 256 : (i + 1) * 256, :].T
    build_mix(w1, w1g)
    build_mix(w2, w2g)
    acc[...] = jnp.zeros_like(acc)

    def tile(i):
        return slice(i * RT, (i + 1) * RT)

    def chunk(i, j):
        return slice(i * RT + j * CH, i * RT + (j + 1) * CH)

    def add_to(layer, k, x):
        acc[layer, k] = acc[layer, k] + fold(x)

    def norm1(layer, dst, h):
        mean = jnp.mean(h, -1, keepdims=True)
        cent = h - mean
        rstd = lax.rsqrt(jnp.mean(cent * cent, -1, keepdims=True) + 1e-05)
        xh = cent * rstd
        u = xh * n1g[layer : layer + 1, :] + n1b[layer : layer + 1, :]
        xh1[layer, dst, :] = xh.astype(BF)
        rs1[layer, dst, :] = jnp.broadcast_to(rstd, (CH, 128))
        ul[dst, :] = u.astype(BF)
        hu[dst, :] = h + u

    def enter():
        for i in range(tiles):
            for j in range(RT // CH):
                dst = chunk(i, j)
                norm1(0, dst, x_ref[dst, :].astype(F32))

    def block(f):
        pl.when(grid_ref[0] > 0)(f)

    enter()

    def lanes(x, times):
        return jnp.concatenate([x] * times, 1)

    def analyse(layer, t, p):
        sl = slice(t * ST, (t + 1) * ST)
        h = p % 2
        hs = slice(h * 256, (h + 1) * 256)
        if p < 2:
            zr = nn(at[sl, :], ul[:, hs]).astype(BF)
            for e in range(2):
                c0 = (2 * h + e) * 256
                z[layer, 0, sl, c0 : c0 + 128] = zr[:, e * 128 : e * 128 + 128]
        else:
            n, nbar = nm[sl, :], nb[sl, :]
            zi = nn(at[slots + t * ST : slots + (t + 1) * ST, :], ul[:, hs]).astype(BF)
            for e in range(2):
                c0 = (2 * h + e) * 256
                zie = zi[:, e * 128 : e * 128 + 128]
                zin = zie * n
                z[layer, 0, sl, c0 + 128 : c0 + 256] = zin
                z[layer, 1, sl, c0 + 128 : c0 + 256] = -zin
                z[layer, 1, sl, c0 : c0 + 128] = z[layer, 0, sl, c0 : c0 + 128] * n + zie * nbar

    def both(ref, layer, sl, gl):
        return ref[layer, :, sl, gl].reshape(2 * ST, 256)

    def put(ref, layer, sl, gl, x, c=None):
        if c is None:
            ref[layer, :, sl, gl] = x.reshape(2, ST, 256)
        else:
            r0 = sl.start + c % ST
            ref[layer, c // ST, r0 : r0 + CE, gl] = x

    def combine(dst, sl, cs, x, signed):
        n, nbar = nm[sl, :], nb[sl, :]
        rp, ip = x[0:ST, 0:128], x[0:ST, 128:256]
        rm, im = x[ST : 2 * ST, 0:128], x[ST : 2 * ST, 128:256]
        dst[sl, cs] = rp + rm * n
        q = ip + im if signed else (ip - im) * n
        dst[slots + sl.start : slots + sl.stop, cs] = q + rm * nbar

    def mix_forward(layer):
        def cut(k):
            t, g = k // 4, k % 4
            return slice(t * ST, (t + 1) * ST), slice(g * 128, (g + 1) * 128), slice(g * 256, (g + 1) * 256), g

        def dot_a(k):
            sl, cs, gl, g = cut(k)
            return nn(both(z, layer, sl, gl), w1g[layer, g])

        def gelu_a(k, a):
            sl, cs, gl, g = cut(k)
            bias = lanes2(b1[layer, 0:1, cs], b1[layer, 1:2, cs])
            ys = []
            for c in range(0, 2 * ST, CE):
                og, dag = gelu_split(a[c : c + CE] + bias)
                ys.append(og)
                put(o, layer, sl, gl, og, c)
                put(da, layer, sl, gl, dag, c)
            return nn(jnp.concatenate(ys, 0), w2g[layer, g])

        def shrink_e(k, ew):
            sl, cs, gl, g = cut(k)
            bias = lanes2(b2[layer, 0:1, cs], b2[layer, 1:2, cs])
            for c in range(0, ST, CE):
                rs = slice(sl.start + c, sl.start + c + CE)
                ss = []
                for sign in range(2):
                    e = ew[sign * ST + c : sign * ST + c + CE] + bias
                    r = lax.rsqrt(e * e + 0.0025)
                    c1 = k1[sign, rs, :]
                    ss.append((e - 0.05 * (e * r)).astype(BF) * c1)
                    r = r.astype(BF)
                    ds[layer, sign, rs, gl] = c1 - k3[sign, rs, :] * (r * r * r)
                n, nbar = nm[rs, :], nb[rs, :]
                rm = ss[1][:, 0:128]
                pq[rs, cs] = ss[0][:, 0:128] + rm * n
                pq[slots + rs.start : slots + rs.stop, cs] = ss[0][:, 128:256] + ss[1][:, 128:256] + rm * nbar

        steps = stiles * 4
        for p in range(4):
            analyse(layer, 0, p)
        a = dot_a(0)
        e_prev = None
        for k in range(steps):
            t, g = k // 4, k % 4
            if t + 1 < stiles:
                analyse(layer, t + 1, g)
            nxt = dot_a(k + 1) if k + 1 < steps else None
            e = gelu_a(k, a)
            if e_prev is not None:
                shrink_e(k - 1, e_prev)
            a, e_prev = nxt, e
        shrink_e(steps - 1, e_prev)

    def ff_forward(layer):
        def norm2(i, y):
            for j in range(RT // CH):
                cd = chunk(i, j)
                mid = y[j * CH : (j + 1) * CH] + hu[cd, :]
                mean = jnp.mean(mid, -1, keepdims=True)
                cent = mid - mean
                rstd = lax.rsqrt(jnp.mean(cent * cent, -1, keepdims=True) + 1e-05)
                xh = cent * rstd
                xh2[layer, cd, :] = xh.astype(BF)
                rs2[layer, cd, :] = jnp.broadcast_to(rstd, (CH, 128))
                v[layer, cd, :] = (xh * n2g[layer : layer + 1, :] + n2b[layer : layer + 1, :]).astype(BF)
                hu[cd, :] = mid
            return nn(v[layer, tile(i), :], fc1[layer])

        def gelu_f(i, pre):
            for j in range(0, RT, CF):
                cd = slice(i * RT + j, i * RT + j + CF)
                act[layer, cd, :], dp[layer, cd, :] = gelu_split(pre[j : j + CF] + fb1[layer : layer + 1, :])
            return nn(act[layer, tile(i), :], fc2[layer])

        def leave(i, br):
            for j in range(RT // CH):
                cd = chunk(i, j)
                h = hu[cd, :] + (br[j * CH : (j + 1) * CH] + fb2[layer : layer + 1, :])
                if layer == LAYERS - 1:
                    out_ref[cd, :] = h.astype(BF)
                else:
                    norm1(layer + 1, cd, h)

        def dot_y(i):
            return nn(st[tile(i), :], pq[...])

        y = dot_y(0)
        pre = None
        for i in range(tiles + 1):
            nxt = dot_y(i + 1) if i + 1 < tiles else None
            br = gelu_f(i - 1, pre) if i >= 1 else None
            pre = norm2(i, y) if i < tiles else None
            if i >= 1:
                leave(i - 1, br)
            y = nxt

    for layer in range(LAYERS):
        block(lambda: mix_forward(layer))
        block(lambda: ff_forward(layer))

    def norm_back(gv, xh, rstd, gain):
        t = gv * gain
        mt = jnp.mean(t, -1, keepdims=True)
        mx = jnp.mean(t * xh, -1, keepdims=True)
        return rstd * (t - mt - xh * mx)

    def with_sums(left, right):
        ones = jnp.ones((16, left.shape[0]), BF)
        return nn(jnp.concatenate([left.T, ones], 0), right)

    def ff_backward(layer):
        def load_g(rs):
            return cot_ref[rs, :].astype(F32) if layer == LAYERS - 1 else g_s[rs, :]

        def dot_a(i):
            dst = tile(i)
            gmt = cot_ref[dst, :] if layer == LAYERS - 1 else g_s[dst, :].astype(BF)
            gm[dst, :] = gmt
            return nt(gmt, fc2[layer])

        def mul(i, ga_):
            dst = tile(i)
            dp[layer, dst, :] = ga_.astype(BF) * dp[layer, dst, :]
            return nt(dp[layer, dst, :], fc1[layer])

        def leave(i, gv):
            for j in range(RT // CH):
                cd = chunk(i, j)
                gvc = gv[j * CH : (j + 1) * CH]
                xh = xh2[layer, cd, :].astype(F32)
                add_to(layer, 6, gvc * xh)
                add_to(layer, 7, gvc)
                rstd = lanes(rs2[layer, cd, :], 4)
                gmc = load_g(cd) + norm_back(gvc, xh, rstd, n2g[layer : layer + 1, :])
                gmid[cd, :] = gmc
                gy[cd, :] = gmc.astype(BF)

        cur = dot_a(0)
        prev = None
        for i in range(tiles + 1):
            nxt = dot_a(i + 1) if i + 1 < tiles else None
            gv = mul(i, cur) if i < tiles else None
            if i >= 1:
                leave(i - 1, prev)
            cur, prev = nxt, gv
        base = pl.multiple_of((layer ^ core_ref[0]) * PER, PER)
        for left, right, off, vec in ((v, dp[layer], 0, 8), (act, gm[...], 512, 9)):
            for h in range(2):
                hs = slice(h * 256, (h + 1) * 256)
                r = base + off + h * 256
                if h == 0:
                    p = with_sums(left[layer, :, hs], right)
                    acc[layer, vec, 0:1, :] = p[256:257]
                else:
                    p = tn(left[layer, :, hs], right)
                grads_ref[pl.ds(r, 256), :] = p[0:256].astype(BF)

    def mix_backward(layer):
        def cut(k):
            t, g = k // 4, k % 4
            return slice(t * ST, (t + 1) * ST), slice(g * 128, (g + 1) * 128), slice(g * 256, (g + 1) * 256), g

        def spectrum(t, h):
            hs = slice(h * 256, (h + 1) * 256)
            gr = nn(at[t * ST : (t + 1) * ST, :], gy[:, hs]).astype(BF)
            gi = nn(at[slots + t * ST : slots + (t + 1) * ST, :], gy[:, hs]).astype(BF)
            return gr, gi

        def dot_o(k, gr, gi):
            sl, cs, gl, g = cut(k)
            n, nbar = nm[sl, :], nb[sl, :]
            hs = slice(g % 2 * 128, g % 2 * 128 + 128)
            grc, gic = gr[:, hs], gi[:, hs]
            ds[layer, 0, sl, gl] = lanes2(grc, gic) * ds[layer, 0, sl, gl]
            ds[layer, 1, sl, gl] = lanes2(grc * n + gic * nbar, gic) * ds[layer, 1, sl, gl]
            return nt(both(ds, layer, sl, gl), w2g[layer, g])

        def dot_z(k, go):
            sl, cs, gl, g = cut(k)
            put(da, layer, sl, gl, go.astype(BF) * both(da, layer, sl, gl))
            return nt(both(da, layer, sl, gl), w1g[layer, g])

        def leave(k, gz):
            sl, cs, gl, g = cut(k)
            combine(pq, sl, cs, gz.astype(BF), False)

        steps = stiles * 4
        sp = {0: spectrum(0, 0)}
        go = dot_o(0, *sp[0])
        prev = None
        for k in range(steps + 1):
            if k % 2 == 0 and k + 2 < steps:
                sp[k // 2 + 1] = spectrum((k + 2) // 4, (k + 2) // 2 % 2)
            nxt = dot_o(k + 1, *sp[(k + 1) // 2]) if k + 1 < steps else None
            gz = dot_z(k, go) if k < steps else None
            if k >= 1:
                leave(k - 1, prev)
            go, prev = nxt, gz
        base = pl.multiple_of((layer ^ core_ref[0]) * PER, PER) + 1024
        low = lax.broadcasted_iota(jnp.int32, (64, 128), 1) < 64
        for left, right, off, vec in ((o, ds, base + 128, 4), (z, da, base, 2)):
            for g in range(4):
                cs = slice(g * 128, (g + 1) * 128)
                gl = slice(g * 256, (g + 1) * 256)
                lf = left[layer, :, :, gl].reshape(rows, 256)
                rt = right[layer, :, :, gl].reshape(rows, 256)
                p = with_sums(lf, rt)
                acc[layer, vec, 0:1, cs] = p[256:257, 0:128]
                acc[layer, vec + 1, 0:1, cs] = p[256:257, 128:256]
                re = p[0:128, 0:128] + p[128:256, 128:256]
                im = p[0:128, 128:256] - p[128:256, 0:128]
                grads_ref[pl.ds(off, 64), cs] = jnp.where(low, re[0:64], re[64:128]).astype(BF)
                grads_ref[pl.ds(off + 64, 64), cs] = jnp.where(low, im[0:64], im[64:128]).astype(BF)

    def in_backward(layer):
        def leave(i, y):
            for j in range(RT // CH):
                cd = chunk(i, j)
                gmc = gmid[cd, :]
                gu = y[j * CH : (j + 1) * CH] + gmc
                xh = xh1[layer, cd, :].astype(F32)
                add_to(layer, 0, gu * xh)
                add_to(layer, 1, gu)
                rstd = lanes(rs1[layer, cd, :], 4)
                gh = gmc + norm_back(gu, xh, rstd, n1g[layer : layer + 1, :])
                if layer == 0:
                    xg_ref[cd, :] = gh.astype(BF)
                else:
                    g_s[cd, :] = gh

        y = nn(st[tile(0), :], pq[...])
        for i in range(tiles):
            nxt = nn(st[tile(i + 1), :], pq[...]) if i + 1 < tiles else None
            leave(i, y)
            y = nxt

    for layer in reversed(range(LAYERS)):
        block(lambda: ff_backward(layer))
        block(lambda: mix_backward(layer))
        block(lambda: in_backward(layer))

    for layer in range(LAYERS):
        t = jnp.sum(acc[layer], 1)
        t = jnp.concatenate([t, jnp.zeros((PER - 1290, 512), F32)], 0)
        grads_ref[pl.ds(pl.multiple_of((layer ^ core_ref[0]) * PER, PER) + 1280, PER - 1280), :] = t.astype(BF)


def lanes2(a, b):
    return jnp.concatenate([a, b], 1)


def local_step(core, x_in, cotangent, block_grid, keep_modes, n1g, n1b, w1, b1, w2, b2, n2g, n2b, fc1, fb1, fc2, fb2):
    rows, d = x_in.shape
    slots = rows // 2
    vm = pl.BlockSpec(memory_space=pltpu.VMEM)
    sm = pl.BlockSpec(memory_space=pltpu.SMEM)
    w1r = w1.reshape(LAYERS, 2, 512, 64)
    w2r = w2.reshape(LAYERS, 2, 512, 64)
    scratch = [
        pltpu.VMEM((rows, rows), BF), pltpu.VMEM((rows, rows), BF),
        pltpu.VMEM((2, slots, 256), BF), pltpu.VMEM((2, slots, 256), BF), pltpu.VMEM((2, slots, 256), BF),
        pltpu.VMEM((slots, 128), BF), pltpu.VMEM((slots, 128), BF),
        pltpu.VMEM((LAYERS, 4, 256, 256), BF), pltpu.VMEM((LAYERS, 4, 256, 256), BF),
        pltpu.VMEM((LAYERS, rows, d), BF), pltpu.VMEM((LAYERS, rows, 128), F32),
        pltpu.VMEM((rows, d), F32), pltpu.VMEM((rows, d), BF),
        pltpu.VMEM((LAYERS, 2, slots, 2 * d), BF), pltpu.VMEM((LAYERS, 2, slots, 2 * d), BF),
        pltpu.VMEM((LAYERS, 2, slots, 2 * d), BF), pltpu.VMEM((LAYERS, 2, slots, 2 * d), BF),
        pltpu.VMEM((rows, d), BF),
        pltpu.VMEM((LAYERS, rows, d), BF), pltpu.VMEM((LAYERS, rows, 128), F32),
        pltpu.VMEM((LAYERS, rows, d), BF), pltpu.VMEM((LAYERS, rows, d), BF), pltpu.VMEM((LAYERS, rows, d), BF),
        pltpu.VMEM((rows, d), BF), pltpu.VMEM((rows, d), F32),
        pltpu.VMEM((LAYERS, 10, 8, d), F32),
    ]
    return pl.pallas_call(
        kernel,
        out_shape=(
            jax.ShapeDtypeStruct((rows, d), BF),
            jax.ShapeDtypeStruct((rows, d), BF),
            jax.ShapeDtypeStruct((LAYERS * PER, d), BF),
        ),
        in_specs=[sm, sm, sm] + [vm] * 14,
        out_specs=(vm, vm, vm),
        scratch_shapes=scratch,
        compiler_params=pltpu.CompilerParams(vmem_limit_bytes=64 * 1024 * 1024 - 65536),
        name="slab_step",
    )(block_grid, keep_modes, core, x_in, cotangent, n1g, n1b, w1r, b1, w2r, b2, n2g, n2b, fc1, fb1, fc2, fb2)


AXES = ("dp", "modes")


def spread(core_ref, mine, other, n1g, n1b, w1, b1, w2, b2, n2g, n2b, fc1, fb1, fc2, fb2):
    def write(layer, src):
        fc1[layer] = src[0:512, :].astype(F32)
        fc2[layer] = src[512:1024, :].astype(F32)
        for ref, base in ((w1, 1024), (w2, 1152)):
            for part in range(2):
                block = src[base + part * 64 : base + part * 64 + 64, :].astype(F32)
                for k in range(8):
                    ref[layer, part, k] = block[:, k * 64 : k * 64 + 64]
        vec = src[1280:1296, :].astype(F32)
        for row, ref in ((0, n1g), (1, n1b), (6, n2g), (7, n2b), (8, fb1), (9, fb2)):
            ref[layer : layer + 1, :] = vec[row : row + 1]
        b1[layer] = vec[2:4]
        b2[layer] = vec[4:6]

    @pl.when(core_ref[0] == 0)
    def _():
        write(0, mine)
        write(1, other)

    @pl.when(core_ref[0] != 0)
    def _():
        write(1, mine)
        write(0, other)


def unpack(core, mine, other, d):
    vm = pl.BlockSpec(memory_space=pltpu.VMEM)
    vec = jax.ShapeDtypeStruct((LAYERS, d), F32)
    pair = jax.ShapeDtypeStruct((LAYERS, 2, d), F32)
    mix = jax.ShapeDtypeStruct((LAYERS, 2, 8, 64, 64), F32)
    full = jax.ShapeDtypeStruct((LAYERS, d, d), F32)
    return pl.pallas_call(
        spread,
        out_shape=(vec, vec, mix, pair, mix, pair, vec, vec, full, vec, full, vec),
        in_specs=[pl.BlockSpec(memory_space=pltpu.SMEM), vm, vm],
        out_specs=(vm,) * 12,
        compiler_params=pltpu.CompilerParams(vmem_limit_bytes=32 * 1024 * 1024),
        name="spread",
    )(core, mine, other)


def exchange(a, bit, count):
    return lax.ppermute(a, AXES, [(i, i ^ bit) for i in range(count)])


def add(a, b):
    return (a.astype(F32) + b.astype(F32)).astype(BF)


def all_sum(flat, count):
    me = lax.axis_index(AXES)
    top = count // 2
    mine = add(flat[:PER], exchange(flat[PER:], top, count))
    bits = [1 << k for k in range(top.bit_length() - 1)]
    orders = [[bits[(c + k) % 3] for k in range(3)] for c in range(3)]
    third = PER // 3
    parts = [mine[c * third : (c + 1) * third] for c in range(3)]
    for k in range(3):
        moved = []
        for c in range(3):
            n = parts[c].shape[0] // 2
            high = (me & orders[c][k]) != 0
            keep = jnp.where(high, parts[c][n:], parts[c][:n])
            send = jnp.where(high, parts[c][:n], parts[c][n:])
            moved.append((keep, exchange(send, orders[c][k], count)))
        parts = [add(keep, got) for keep, got in moved]
    n = parts[0].shape[0]
    last = jnp.concatenate(parts)
    for bit in bits[3:]:
        last = add(last, exchange(last, bit, count))
    parts = [last[c * n : (c + 1) * n] for c in range(3)]
    for k in reversed(range(3)):
        gots = [exchange(parts[c], orders[c][k], count) for c in range(3)]
        for c in range(3):
            high = (me & orders[c][k]) != 0
            low_part = jnp.where(high, gots[c], parts[c])
            high_part = jnp.where(high, parts[c], gots[c])
            parts[c] = jnp.concatenate([low_part, high_part])
    mine = jnp.concatenate(parts)
    return mine, exchange(mine, top, count)


def solution(mesh):
    count = mesh.shape["dp"] * mesh.shape["modes"]

    def on_device(*args):
        core = lax.axis_index("dp").astype(jnp.int32).reshape(1)
        out, x_grad, flat = local_step(core, *args)
        mine, other = all_sum(flat, count)
        return (out, x_grad) + tuple(unpack(core, mine, other, flat.shape[1]))

    rows = P(AXES, None)
    return jax.shard_map(
        on_device,
        mesh=mesh,
        in_specs=(rows, rows, P(AXES)) + (P(),) * 13,
        out_specs=(rows, rows) + (P(),) * 12,
        check_vma=False,
    )
```

```python
import math
from functools import partial

import jax
import jax.numpy as jnp
from jax import lax
from jax.experimental import pallas as pl
from jax.experimental.pallas import tpu as pltpu
from jax.sharding import PartitionSpec as P

LAYERS = 2
NBLK = 16
F32 = jnp.float32
BF = jnp.bfloat16
C0 = math.sqrt(2.0 / math.pi)
C1 = 0.044715 * C0
PER = 1344
RT = 256
ST = 256
NH = 512
CH = 64
CE = 32
CF = 16


def nn(a, b):
    return jnp.dot(a, b, preferred_element_type=F32)


def nt(a, b):
    return lax.dot_general(a, b, (((1,), (1,)), ((), ())), preferred_element_type=F32)


def tn(a, b):
    return lax.dot_general(a, b, (((0,), (0,)), ((), ())), preferred_element_type=F32)


def gelu_pair(x):
    x2 = x * x
    p = 0.5 + 0.5 * jnp.tanh(x * (C0 + C1 * x2))
    y = x * p
    return y, p + y * (1.0 - p) * (2.0 * C0 + (6.0 * C1) * x2)


def gelu_split(x):
    p = 0.5 + 0.5 * jnp.tanh(x * (C0 + C1 * (x * x)))
    y = (x * p).astype(BF)
    xb, pb, qb = x.astype(BF), p.astype(BF), (1.0 - p).astype(BF)
    return y, pb + y * qb * (2.0 * C0 + (6.0 * C1) * (xb * xb))


def cos_of(t):
    x = t - 0.5
    w = (2.0 * math.pi * x) ** 2
    c = jnp.full_like(w, 1.0 / math.factorial(16))
    for k in range(7, -1, -1):
        c = c * w + (-1.0) ** k / math.factorial(2 * k)
    return -c


def cos_sin(t):
    x = t - 0.5
    w = (2.0 * math.pi * x) ** 2
    c = jnp.full_like(w, 1.0 / math.factorial(16))
    s = jnp.full_like(w, -1.0 / math.factorial(15))
    for k in range(7, -1, -1):
        c = c * w + (-1.0) ** k / math.factorial(2 * k)
        if k < 7:
            s = s * w + (-1.0) ** k / math.factorial(2 * k + 1)
    return -c, -s * (2.0 * math.pi * x)


def pick(values, block):
    out = jnp.zeros(block.shape, jnp.int32)
    for j in range(NBLK):
        out = jnp.where(block == j, values[j], out)
    return out


def log_of(grid):
    return jnp.where(grid == 8, 3, jnp.where(grid == 16, 4, 5))


def slot_of(slot, grid):
    half = grid * grid // 2
    local = slot & (half - 1)
    pp = lax.shift_right_logical(local, log_of(grid))
    qq = local & (grid - 1)
    mid = lax.shift_right_logical(grid, 1)
    first = pp == 0
    special = first & ((qq == 0) | (qq == mid))
    p = jnp.where(first & (qq >= mid), mid, pp)
    q = jnp.where(first & (qq == mid), 0, qq)
    pm = jnp.where(special, p, (grid - p) & (grid - 1))
    qm = jnp.where(special, mid, (grid - q) & (grid - 1))
    return 2 * (slot - local), p, q, special, pm, qm


def build_tables(grid_ref, keep_ref, at, k1, k2, k3, nm, nb):
    rows = at.shape[1]
    slots = rows // 2
    unit = slots // NBLK
    vals = [grid_ref[j] for j in range(NBLK)]
    lane = lax.broadcasted_iota(jnp.int32, (8, rows), 1)
    sub = lax.broadcasted_iota(jnp.int32, (8, rows), 0)
    gc = pick(vals, lane // (2 * unit))
    span = gc * gc
    start_c = lane & ~(span - 1)
    local = lane & (span - 1)
    p_c = lax.shift_right_logical(local, log_of(gc))
    q_c = local & (gc - 1)
    ginv = 1.0 / gc.astype(F32)
    bcs = []
    for j in range(4):
        q_r = (sub + 8 * j) & (gc - 1)
        bcs.append(cos_sin(((q_r * q_c) & (gc - 1)).astype(F32) * ginv))

    def two(x):
        return jnp.concatenate([x, x], 0)

    gc2, start2, p2, q2, ginv2, sub2 = two(gc), two(start_c), two(p_c), two(q_c), two(ginv), lax.broadcasted_iota(jnp.int32, (16, rows), 0)

    def step(i, carry):
        slot = (sub + 8 * i) * 8
        gb = jnp.where(sub < 4, grid_ref[2 * i], grid_ref[2 * i + 1])
        half = gb * gb // 2
        loc = slot & (half - 1)
        p_b = lax.shift_right_logical(loc, log_of(gb))
        ac, as_ = cos_sin(((p_b * p_c) & (gc - 1)).astype(F32) * ginv)
        same = jnp.where(2 * (slot - loc) == start_c, ginv, 0.0)
        ac = ac * same
        as_ = as_ * same
        for j in range(0, 8, 2):
            re, im = [], []
            for d in range(2):
                bc, bs = bcs[(j + d) % 4]
                a1 = ac[j + d : j + d + 1, :]
                a2 = as_[j + d : j + d + 1, :]
                re.append(a1 * bc - a2 * bs)
                im.append(-(a2 * bc + a1 * bs))
            s0 = pl.multiple_of(i * 64 + j * 8, 16)
            at[pl.ds(s0, 16), :] = jnp.concatenate(re, 0).astype(BF)
            at[pl.ds(slots + s0, 16), :] = jnp.concatenate(im, 0).astype(BF)
            g = grid_ref[2 * i + j // 4]
            first = (s0 & (g * g // 2 - 1)) < g

            @pl.when(first)
            def _():
                gv = jnp.full((16, rows), 0, jnp.int32) + g
                start, p, q, special, pm, qm = slot_of(sub2 + s0, gv)
                live = jnp.where(start == start2, ginv2, 0.0)
                t = ((p * p2 + q * q2) & (gc2 - 1)).astype(F32) * ginv2
                tm = ((pm * p2 + qm * q2) & (gc2 - 1)).astype(F32) * ginv2
                quarter = jnp.where(t >= 0.75, t - 0.75, t + 0.25)
                at[pl.ds(s0, 16), :] = (cos_of(t) * live).astype(BF)
                at[pl.ds(slots + s0, 16), :] = (cos_of(jnp.where(special, tm, quarter)) * live).astype(BF)

        return carry

    lax.fori_loop(0, slots // 64, step, 0)

    def mask(i, carry):
        slot = lax.broadcasted_iota(jnp.int32, (unit, 128), 0) + unit * i
        g = jnp.full((unit, 128), 0, jnp.int32) + grid_ref[i]
        _, p, q, special, pm, qm = slot_of(slot, g)
        k = jnp.where(g == 8, keep_ref[0], jnp.where(g == 16, keep_ref[1], keep_ref[2]))
        plus = jnp.where((p < k) & (q < k), 1.0, 0.0)
        minus = jnp.where((pm < k) & (qm < k), 1.0, 0.0)
        n = jnp.where(special, 0.0, 1.0)
        dst = pl.ds(pl.multiple_of(i * unit, unit), unit)
        nm[dst, :] = n.astype(BF)
        nb[dst, :] = (1.0 - n).astype(BF)
        for sign, (m, im) in enumerate(((plus, plus * n), (minus, -minus * n))):
            for ref, f in ((k1, 1.0), (k2, 0.05), (k3, 0.05 * 0.0025)):
                ref[sign, dst, 0:128] = (m * f).astype(BF)
                ref[sign, dst, 128:256] = (im * f).astype(BF)
        return carry

    lax.fori_loop(0, NBLK, mask, 0)


def build_mix(w_ref, out_ref):
    i = lax.broadcasted_iota(jnp.int32, (64, 128), 0)
    j = lax.broadcasted_iota(jnp.int32, (64, 128), 1)
    dup = jnp.where((j & 63) == i, 1.0, 0.0).astype(BF)
    r = lax.broadcasted_iota(jnp.int32, (512, 128), 0)
    c = lax.broadcasted_iota(jnp.int32, (512, 128), 1)
    diag = ((r // 64) & 1) == (c // 64)
    for layer in range(LAYERS):
        re = jnp.where(diag, nn(w_ref[layer, 0], dup), 0.0)
        im = jnp.where(diag, nn(w_ref[layer, 1], dup), 0.0)
        for g in range(4):
            a = re[g * 128 : (g + 1) * 128].astype(BF)
            b = im[g * 128 : (g + 1) * 128]
            out_ref[layer, g, 0:128, 0:128] = a
            out_ref[layer, g, 128:256, 128:256] = a
            out_ref[layer, g, 0:128, 128:256] = b.astype(BF)
            out_ref[layer, g, 128:256, 0:128] = (-b).astype(BF)


def min_layer(layer):
    return layer if isinstance(layer, int) else jnp.minimum(layer, LAYERS - 1)


def fold(x):
    return jnp.sum(x.reshape(x.shape[0] // 8, 8, x.shape[1]), 0)


def kernel(
    grid_ref, keep_ref, core_ref, x_hbm, cot_hbm,
    n1g, n1b, w1_hbm, b1, w2_hbm, b2, n2g, n2b, fc1_hbm, fb1, fc2_hbm, fb2,
    out_hbm, xg_hbm, mine_hbm, other_hbm,
    x_ref, cot_ref, w1, w2, fc1, fc2, out_ref, xg_ref, grads_ref, sems,
    at, st, k1, k2, k3, nm, nb, w1g, w2g,
    xh1, rs1, hu, ul, z, o, da, ds, pq, xh2, rs2, v, act, dp,
    gm, gmid, acc,
):
    g_s, gy = hu, ul

    def copy(k, src, dst):
        return pltpu.make_async_copy(src, dst, sems.at[k])

    loads = [
        copy(k, src, dst)
        for k, (src, dst) in enumerate(
            ((x_hbm, x_ref), (w1_hbm, w1), (w2_hbm, w2), (fc1_hbm, fc1), (fc2_hbm, fc2), (cot_hbm, cot_ref))
        )
    ]
    for c in loads:
        c.start()
    rows = x_ref.shape[0]
    slots = rows // 2
    tiles = rows // RT
    stiles = slots // ST
    build_tables(grid_ref, keep_ref, at, k1, k2, k3, nm, nb)
    for i in range(4):
        st[:, i * 256 : (i + 1) * 256] = at[i * 256 : (i + 1) * 256, :].T
    loads[1].wait()
    loads[2].wait()
    build_mix(w1, w1g)
    build_mix(w2, w2g)
    acc[...] = jnp.zeros_like(acc)

    def tile(i):
        return slice(i * RT, (i + 1) * RT)

    def chunk(i, j):
        return slice(i * RT + j * CH, i * RT + (j + 1) * CH)

    def add_to(layer, k, x):
        acc[layer, k] = acc[layer, k] + fold(x)

    def norm1(layer, dst, h):
        mean = jnp.mean(h, -1, keepdims=True)
        cent = h - mean
        rstd = lax.rsqrt(jnp.mean(cent * cent, -1, keepdims=True) + 1e-05)
        xh = cent * rstd
        u = xh * n1g[pl.ds(min_layer(layer), 1), :] + n1b[pl.ds(min_layer(layer), 1), :]
        xh1[layer, dst, :] = xh.astype(BF)
        rs1[layer, dst, :] = jnp.broadcast_to(rstd, (CH, 128))
        ul[dst, :] = u.astype(BF)
        hu[dst, :] = h + u

    def enter():
        for i in range(tiles):
            for j in range(RT // CH):
                dst = chunk(i, j)
                norm1(0, dst, x_ref[dst, :].astype(F32))

    def block(f):
        pl.when(grid_ref[0] > 0)(f)

    loads[0].wait()
    enter()
    loads[3].wait()
    loads[4].wait()
    loads[5].wait()

    def lanes(x, times):
        return jnp.concatenate([x] * times, 1)

    def analyse(layer, t, p):
        sl = slice(t * ST, (t + 1) * ST)
        h = p % 2
        hs = slice(h * 256, (h + 1) * 256)
        if p < 2:
            zr = nn(at[sl, :], ul[:, hs]).astype(BF)
            for e in range(2):
                c0 = (2 * h + e) * 256
                z[layer, 0, sl, c0 : c0 + 128] = zr[:, e * 128 : e * 128 + 128]
        else:
            n, nbar = nm[sl, :], nb[sl, :]
            zi = nn(at[slots + t * ST : slots + (t + 1) * ST, :], ul[:, hs]).astype(BF)
            for e in range(2):
                c0 = (2 * h + e) * 256
                zie = zi[:, e * 128 : e * 128 + 128]
                zin = zie * n
                z[layer, 0, sl, c0 + 128 : c0 + 256] = zin
                z[layer, 1, sl, c0 + 128 : c0 + 256] = -zin
                z[layer, 1, sl, c0 : c0 + 128] = z[layer, 0, sl, c0 : c0 + 128] * n + zie * nbar

    def both(ref, layer, sl, gl):
        return ref[layer, :, sl, gl].reshape(2 * ST, 256)

    def put(ref, layer, sl, gl, x, c=None):
        if c is None:
            ref[layer, :, sl, gl] = x.reshape(2, ST, 256)
        else:
            r0 = sl.start + c % ST
            ref[layer, c // ST, r0 : r0 + CE, gl] = x

    def combine(dst, sl, cs, x, signed):
        n, nbar = nm[sl, :], nb[sl, :]
        rp, ip = x[0:ST, 0:128], x[0:ST, 128:256]
        rm, im = x[ST : 2 * ST, 0:128], x[ST : 2 * ST, 128:256]
        dst[sl, cs] = rp + rm * n
        q = ip + im if signed else (ip - im) * n
        dst[slots + sl.start : slots + sl.stop, cs] = q + rm * nbar

    def mix_forward(layer):
        def cut(k):
            t, g = k // 4, k % 4
            return slice(t * ST, (t + 1) * ST), slice(g * 128, (g + 1) * 128), slice(g * 256, (g + 1) * 256), g

        def dot_a(k):
            sl, cs, gl, g = cut(k)
            return nn(both(z, layer, sl, gl), w1g[layer, g])

        def gelu_a(k, a):
            sl, cs, gl, g = cut(k)
            bias = lanes2(b1[layer, 0:1, cs], b1[layer, 1:2, cs])
            ys = []
            for c in range(0, 2 * ST, CE):
                og, dag = gelu_split(a[c : c + CE] + bias)
                ys.append(og)
                put(o, layer, sl, gl, og, c)
                put(da, layer, sl, gl, dag, c)
            return nn(jnp.concatenate(ys, 0), w2g[layer, g])

        def shrink_e(k, ew):
            sl, cs, gl, g = cut(k)
            bias = lanes2(b2[layer, 0:1, cs], b2[layer, 1:2, cs])
            for c in range(0, ST, CE):
                rs = slice(sl.start + c, sl.start + c + CE)
                ss = []
                for sign in range(2):
                    e = ew[sign * ST + c : sign * ST + c + CE] + bias
                    r = lax.rsqrt(e * e + 0.0025)
                    c1 = k1[sign, rs, :]
                    ss.append((e - 0.05 * (e * r)).astype(BF) * c1)
                    r = r.astype(BF)
                    ds[layer, sign, rs, gl] = c1 - k3[sign, rs, :] * (r * r * r)
                n, nbar = nm[rs, :], nb[rs, :]
                rm = ss[1][:, 0:128]
                pq[rs, cs] = ss[0][:, 0:128] + rm * n
                pq[slots + rs.start : slots + rs.stop, cs] = ss[0][:, 128:256] + ss[1][:, 128:256] + rm * nbar

        steps = stiles * 4
        for p in range(4):
            analyse(layer, 0, p)
        a = dot_a(0)
        e_prev = None
        for k in range(steps):
            t, g = k // 4, k % 4
            if t + 1 < stiles:
                analyse(layer, t + 1, g)
            nxt = dot_a(k + 1) if k + 1 < steps else None
            e = gelu_a(k, a)
            if e_prev is not None:
                shrink_e(k - 1, e_prev)
            a, e_prev = nxt, e
        shrink_e(steps - 1, e_prev)

    def ff_forward(layer):
        def norm2(i, y):
            for j in range(RT // CH):
                cd = chunk(i, j)
                mid = y[j * CH : (j + 1) * CH] + hu[cd, :]
                mean = jnp.mean(mid, -1, keepdims=True)
                cent = mid - mean
                rstd = lax.rsqrt(jnp.mean(cent * cent, -1, keepdims=True) + 1e-05)
                xh = cent * rstd
                xh2[layer, cd, :] = xh.astype(BF)
                rs2[layer, cd, :] = jnp.broadcast_to(rstd, (CH, 128))
                v[layer, cd, :] = (xh * n2g[pl.ds(layer, 1), :] + n2b[pl.ds(layer, 1), :]).astype(BF)
                hu[cd, :] = mid
            return nn(v[layer, tile(i), :], fc1[layer])

        def gelu_f(i, pre):
            for j in range(0, RT, CF):
                cd = slice(i * RT + j, i * RT + j + CF)
                act[layer, cd, :], dp[layer, cd, :] = gelu_split(pre[j : j + CF] + fb1[pl.ds(layer, 1), :])
            return nn(act[layer, tile(i), :], fc2[layer])

        def leave(i, br):
            for j in range(RT // CH):
                cd = chunk(i, j)
                h = hu[cd, :] + (br[j * CH : (j + 1) * CH] + fb2[pl.ds(layer, 1), :])
                out_ref[cd, :] = h.astype(BF)
                norm1(layer + 1, cd, h)

        def dot_y(i):
            return nn(st[tile(i), :], pq[...])

        y = dot_y(0)
        pre = None
        for i in range(tiles + 1):
            nxt = dot_y(i + 1) if i + 1 < tiles else None
            br = gelu_f(i - 1, pre) if i >= 1 else None
            pre = norm2(i, y) if i < tiles else None
            if i >= 1:
                leave(i - 1, br)
            y = nxt

    @partial(lax.fori_loop, 0, LAYERS, init_val=0)
    def _(layer, carry):
        block(lambda: mix_forward(layer))
        block(lambda: ff_forward(layer))
        return carry

    out_copy = copy(6, out_ref, out_hbm)
    out_copy.start()
    for i in range(tiles):
        g_s[tile(i), :] = cot_ref[tile(i), :].astype(F32)

    def norm_back(gv, xh, rstd, gain):
        t = gv * gain
        mt = jnp.mean(t, -1, keepdims=True)
        mx = jnp.mean(t * xh, -1, keepdims=True)
        return rstd * (t - mt - xh * mx)

    def with_sums(left, right):
        ones = jnp.ones((16, left.shape[0]), BF)
        return nn(jnp.concatenate([left.T, ones], 0), right)

    def ff_backward(layer):
        def load_g(rs):
            return g_s[rs, :]

        def dot_a(i):
            dst = tile(i)
            gmt = g_s[dst, :].astype(BF)
            gm[dst, :] = gmt
            return nt(gmt, fc2[layer])

        def mul(i, ga_):
            dst = tile(i)
            dp[layer, dst, :] = ga_.astype(BF) * dp[layer, dst, :]
            return nt(dp[layer, dst, :], fc1[layer])

        def leave(i, gv):
            for j in range(RT // CH):
                cd = chunk(i, j)
                gvc = gv[j * CH : (j + 1) * CH]
                xh = xh2[layer, cd, :].astype(F32)
                add_to(layer, 6, gvc * xh)
                add_to(layer, 7, gvc)
                rstd = lanes(rs2[layer, cd, :], 4)
                gmc = load_g(cd) + norm_back(gvc, xh, rstd, n2g[pl.ds(layer, 1), :])
                gmid[cd, :] = gmc
                gy[cd, :] = gmc.astype(BF)

        cur = dot_a(0)
        prev = None
        for i in range(tiles + 1):
            nxt = dot_a(i + 1) if i + 1 < tiles else None
            gv = mul(i, cur) if i < tiles else None
            if i >= 1:
                leave(i - 1, prev)
            cur, prev = nxt, gv
        base = pl.multiple_of((layer ^ core_ref[0]) * PER, PER)
        for left, right, off, vec in ((v, dp[layer], 0, 8), (act, gm[...], 512, 9)):
            for h in range(2):
                hs = slice(h * 256, (h + 1) * 256)
                r = base + off + h * 256
                if h == 0:
                    p = with_sums(left[layer, :, hs], right)
                    acc[layer, vec, 0:1, :] = p[256:257]
                else:
                    p = tn(left[layer, :, hs], right)
                grads_ref[pl.ds(r, 256), :] = p[0:256].astype(BF)

    def mix_backward(layer):
        def cut(k):
            t, g = k // 4, k % 4
            return slice(t * ST, (t + 1) * ST), slice(g * 128, (g + 1) * 128), slice(g * 256, (g + 1) * 256), g

        def spectrum(t, h):
            hs = slice(h * 256, (h + 1) * 256)
            gr = nn(at[t * ST : (t + 1) * ST, :], gy[:, hs]).astype(BF)
            gi = nn(at[slots + t * ST : slots + (t + 1) * ST, :], gy[:, hs]).astype(BF)
            return gr, gi

        def dot_o(k, gr, gi):
            sl, cs, gl, g = cut(k)
            n, nbar = nm[sl, :], nb[sl, :]
            hs = slice(g % 2 * 128, g % 2 * 128 + 128)
            grc, gic = gr[:, hs], gi[:, hs]
            ds[layer, 0, sl, gl] = lanes2(grc, gic) * ds[layer, 0, sl, gl]
            ds[layer, 1, sl, gl] = lanes2(grc * n + gic * nbar, gic) * ds[layer, 1, sl, gl]
            return nt(both(ds, layer, sl, gl), w2g[layer, g])

        def dot_z(k, go):
            sl, cs, gl, g = cut(k)
            put(da, layer, sl, gl, go.astype(BF) * both(da, layer, sl, gl))
            return nt(both(da, layer, sl, gl), w1g[layer, g])

        def leave(k, gz):
            sl, cs, gl, g = cut(k)
            combine(pq, sl, cs, gz.astype(BF), False)

        steps = stiles * 4
        sp = {0: spectrum(0, 0)}
        go = dot_o(0, *sp[0])
        prev = None
        for k in range(steps + 1):
            if k % 2 == 0 and k + 2 < steps:
                sp[k // 2 + 1] = spectrum((k + 2) // 4, (k + 2) // 2 % 2)
            nxt = dot_o(k + 1, *sp[(k + 1) // 2]) if k + 1 < steps else None
            gz = dot_z(k, go) if k < steps else None
            if k >= 1:
                leave(k - 1, prev)
            go, prev = nxt, gz
        base = pl.multiple_of((layer ^ core_ref[0]) * PER, PER) + 1024
        low = lax.broadcasted_iota(jnp.int32, (64, 128), 1) < 64
        for left, right, off, vec in ((o, ds, base + 128, 4), (z, da, base, 2)):
            for g in range(4):
                cs = slice(g * 128, (g + 1) * 128)
                gl = slice(g * 256, (g + 1) * 256)
                lf = left[layer, :, :, gl].reshape(rows, 256)
                rt = right[layer, :, :, gl].reshape(rows, 256)
                p = with_sums(lf, rt)
                acc[layer, vec, 0:1, cs] = p[256:257, 0:128]
                acc[layer, vec + 1, 0:1, cs] = p[256:257, 128:256]
                re = p[0:128, 0:128] + p[128:256, 128:256]
                im = p[0:128, 128:256] - p[128:256, 0:128]
                grads_ref[pl.ds(off, 64), cs] = jnp.where(low, re[0:64], re[64:128]).astype(BF)
                grads_ref[pl.ds(off + 64, 64), cs] = jnp.where(low, im[0:64], im[64:128]).astype(BF)

    def in_backward(layer):
        def leave(i, y):
            for j in range(RT // CH):
                cd = chunk(i, j)
                gmc = gmid[cd, :]
                gu = y[j * CH : (j + 1) * CH] + gmc
                xh = xh1[layer, cd, :].astype(F32)
                add_to(layer, 0, gu * xh)
                add_to(layer, 1, gu)
                rstd = lanes(rs1[layer, cd, :], 4)
                gh = gmc + norm_back(gu, xh, rstd, n1g[pl.ds(min_layer(layer), 1), :])
                xg_ref[cd, :] = gh.astype(BF)
                g_s[cd, :] = gh

        y = nn(st[tile(0), :], pq[...])
        for i in range(tiles):
            nxt = nn(st[tile(i + 1), :], pq[...]) if i + 1 < tiles else None
            leave(i, y)
            y = nxt

    @partial(lax.fori_loop, 0, LAYERS, init_val=0)
    def _(step, carry):
        layer = LAYERS - 1 - step
        block(lambda: ff_backward(layer))
        block(lambda: mix_backward(layer))
        block(lambda: in_backward(layer))
        return carry

    for layer in range(LAYERS):
        t = jnp.sum(acc[layer], 1)
        t = jnp.concatenate([t, jnp.zeros((PER - 1290, 512), F32)], 0)
        grads_ref[pl.ds(pl.multiple_of((layer ^ core_ref[0]) * PER, PER) + 1280, PER - 1280), :] = t.astype(BF)
    stores = [copy(7, xg_ref, xg_hbm), copy(8, grads_ref.at[pl.ds(PER, PER)], other_hbm), copy(9, grads_ref.at[pl.ds(0, PER)], mine_hbm)]
    for c in stores:
        c.start()
    out_copy.wait()
    for c in stores:
        c.wait()


def lanes2(a, b):
    return jnp.concatenate([a, b], 1)


def local_step(core, x_in, cotangent, block_grid, keep_modes, n1g, n1b, w1, b1, w2, b2, n2g, n2b, fc1, fb1, fc2, fb2):
    rows, d = x_in.shape
    slots = rows // 2
    vm = pl.BlockSpec(memory_space=pltpu.VMEM)
    sm = pl.BlockSpec(memory_space=pltpu.SMEM)
    hbm = pl.BlockSpec(memory_space=pl.ANY)
    w1r = w1.reshape(LAYERS, 2, 512, 64)
    w2r = w2.reshape(LAYERS, 2, 512, 64)
    scratch = [
        pltpu.VMEM((rows, d), BF), pltpu.VMEM((rows, d), BF),
        pltpu.VMEM(w1r.shape, BF), pltpu.VMEM(w2r.shape, BF), pltpu.VMEM(fc1.shape, BF), pltpu.VMEM(fc2.shape, BF),
        pltpu.VMEM((rows, d), BF), pltpu.VMEM((rows, d), BF), pltpu.VMEM((LAYERS * PER, d), BF),
        pltpu.SemaphoreType.DMA((10,)),
        pltpu.VMEM((rows, rows), BF), pltpu.VMEM((rows, rows), BF),
        pltpu.VMEM((2, slots, 256), BF), pltpu.VMEM((2, slots, 256), BF), pltpu.VMEM((2, slots, 256), BF),
        pltpu.VMEM((slots, 128), BF), pltpu.VMEM((slots, 128), BF),
        pltpu.VMEM((LAYERS, 4, 256, 256), BF), pltpu.VMEM((LAYERS, 4, 256, 256), BF),
        pltpu.VMEM((LAYERS + 1, rows, d), BF), pltpu.VMEM((LAYERS + 1, rows, 128), F32),
        pltpu.VMEM((rows, d), F32), pltpu.VMEM((rows, d), BF),
        pltpu.VMEM((LAYERS, 2, slots, 2 * d), BF), pltpu.VMEM((LAYERS, 2, slots, 2 * d), BF),
        pltpu.VMEM((LAYERS, 2, slots, 2 * d), BF), pltpu.VMEM((LAYERS, 2, slots, 2 * d), BF),
        pltpu.VMEM((rows, d), BF),
        pltpu.VMEM((LAYERS, rows, d), BF), pltpu.VMEM((LAYERS, rows, 128), F32),
        pltpu.VMEM((LAYERS, rows, d), BF), pltpu.VMEM((LAYERS, rows, d), BF), pltpu.VMEM((LAYERS, rows, d), BF),
        pltpu.VMEM((rows, d), BF), pltpu.VMEM((rows, d), F32),
        pltpu.VMEM((LAYERS, 10, 8, d), F32),
    ]
    return pl.pallas_call(
        kernel,
        out_shape=(
            jax.ShapeDtypeStruct((rows, d), BF),
            jax.ShapeDtypeStruct((rows, d), BF),
            jax.ShapeDtypeStruct((PER, d), BF),
            jax.ShapeDtypeStruct((PER, d), BF),
        ),
        in_specs=[sm, sm, sm, hbm, hbm, vm, vm, hbm, vm, hbm, vm, vm, vm, hbm, vm, hbm, vm],
        out_specs=(hbm,) * 4,
        scratch_shapes=scratch,
        compiler_params=pltpu.CompilerParams(vmem_limit_bytes=64 * 1024 * 1024 - 65536),
        name="slab_step",
    )(block_grid, keep_modes, core, x_in, cotangent, n1g, n1b, w1r, b1, w2r, b2, n2g, n2b, fc1, fb1, fc2, fb2)


AXES = ("dp", "modes")


def spread(core_ref, mine, other, n1g, n1b, w1, b1, w2, b2, n2g, n2b, fc1, fb1, fc2, fb2):
    def write(layer, src):
        fc1[layer] = src[0:512, :].astype(F32)
        fc2[layer] = src[512:1024, :].astype(F32)
        for ref, base in ((w1, 1024), (w2, 1152)):
            for part in range(2):
                block = src[base + part * 64 : base + part * 64 + 64, :].astype(F32)
                for k in range(8):
                    ref[layer, part, k] = block[:, k * 64 : k * 64 + 64]
        vec = src[1280:1296, :].astype(F32)
        for row, ref in ((0, n1g), (1, n1b), (6, n2g), (7, n2b), (8, fb1), (9, fb2)):
            ref[layer : layer + 1, :] = vec[row : row + 1]
        b1[layer] = vec[2:4]
        b2[layer] = vec[4:6]

    @pl.when(core_ref[0] == 0)
    def _():
        write(0, mine)
        write(1, other)

    @pl.when(core_ref[0] != 0)
    def _():
        write(1, mine)
        write(0, other)


def unpack(core, mine, other, d):
    vm = pl.BlockSpec(memory_space=pltpu.VMEM)
    vec = jax.ShapeDtypeStruct((LAYERS, d), F32)
    pair = jax.ShapeDtypeStruct((LAYERS, 2, d), F32)
    mix = jax.ShapeDtypeStruct((LAYERS, 2, 8, 64, 64), F32)
    full = jax.ShapeDtypeStruct((LAYERS, d, d), F32)
    return pl.pallas_call(
        spread,
        out_shape=(vec, vec, mix, pair, mix, pair, vec, vec, full, vec, full, vec),
        in_specs=[pl.BlockSpec(memory_space=pltpu.SMEM), vm, vm],
        out_specs=(vm,) * 12,
        compiler_params=pltpu.CompilerParams(vmem_limit_bytes=32 * 1024 * 1024),
        name="spread",
    )(core, mine, other)


def exchange(a, bit, count):
    return lax.ppermute(a, AXES, [(i, i ^ bit) for i in range(count)])


def add(a, b):
    return (a.astype(F32) + b.astype(F32)).astype(BF)


def all_sum(mine, other, count):
    me = lax.axis_index(AXES)
    top = count // 2
    mine = add(mine, exchange(other, top, count))
    bits = [1 << k for k in range(top.bit_length() - 1)]
    orders = [[bits[(c + k) % 3] for k in range(3)] for c in range(3)]
    third = PER // 3
    parts = [mine[c * third : (c + 1) * third] for c in range(3)]
    for k in range(3):
        moved = []
        for c in range(3):
            n = parts[c].shape[0] // 2
            high = (me & orders[c][k]) != 0
            keep = jnp.where(high, parts[c][n:], parts[c][:n])
            send = jnp.where(high, parts[c][:n], parts[c][n:])
            moved.append((keep, exchange(send, orders[c][k], count)))
        parts = [add(keep, got) for keep, got in moved]
    n = parts[0].shape[0]
    last = jnp.concatenate(parts)
    for bit in bits[3:]:
        last = add(last, exchange(last, bit, count))
    parts = [last[c * n : (c + 1) * n] for c in range(3)]
    for k in reversed(range(3)):
        gots = [exchange(parts[c], orders[c][k], count) for c in range(3)]
        for c in range(3):
            high = (me & orders[c][k]) != 0
            low_part = jnp.where(high, gots[c], parts[c])
            high_part = jnp.where(high, parts[c], gots[c])
            parts[c] = jnp.concatenate([low_part, high_part])
    mine = jnp.concatenate(parts)
    return mine, exchange(mine, top, count)


def solution(mesh):
    count = mesh.shape["dp"] * mesh.shape["modes"]

    def on_device(*args):
        core = lax.axis_index("dp").astype(jnp.int32).reshape(1)
        out, x_grad, mine, other = local_step(core, *args)
        mine, other = all_sum(mine, other, count)
        return (out, x_grad) + tuple(unpack(core, mine, other, mine.shape[1]))

    rows = P(AXES, None)
    return jax.shard_map(
        on_device,
        mesh=mesh,
        in_specs=(rows, rows, P(AXES)) + (P(),) * 13,
        out_specs=(rows, rows) + (P(),) * 12,
        check_vma=False,
    )
```

```python
import math
from functools import partial

import jax
import jax.numpy as jnp
from jax import lax
from jax.experimental import pallas as pl
from jax.experimental.pallas import tpu as pltpu
from jax.sharding import PartitionSpec as P

LAYERS = 2
NBLK = 16
F32 = jnp.float32
BF = jnp.bfloat16
C0 = math.sqrt(2.0 / math.pi)
C1 = 0.044715 * C0
PER = 1344
RT = 256
ST = 256
NH = 512
CH = 64
CE = 32
CF = 16


def nn(a, b):
    return jnp.dot(a, b, preferred_element_type=F32)


def nt(a, b):
    return lax.dot_general(a, b, (((1,), (1,)), ((), ())), preferred_element_type=F32)


def tn(a, b):
    return lax.dot_general(a, b, (((0,), (0,)), ((), ())), preferred_element_type=F32)


def gelu_pair(x):
    x2 = x * x
    p = 0.5 + 0.5 * jnp.tanh(x * (C0 + C1 * x2))
    y = x * p
    return y, p + y * (1.0 - p) * (2.0 * C0 + (6.0 * C1) * x2)


def gelu_split(x):
    p = 0.5 + 0.5 * jnp.tanh(x * (C0 + C1 * (x * x)))
    y = (x * p).astype(BF)
    xb, pb, qb = x.astype(BF), p.astype(BF), (1.0 - p).astype(BF)
    return y, pb + y * qb * (2.0 * C0 + (6.0 * C1) * (xb * xb))


def cos_of(t):
    x = t - 0.5
    w = (2.0 * math.pi * x) ** 2
    c = jnp.full_like(w, 1.0 / math.factorial(16))
    for k in range(7, -1, -1):
        c = c * w + (-1.0) ** k / math.factorial(2 * k)
    return -c


def cos_sin(t):
    x = t - 0.5
    w = (2.0 * math.pi * x) ** 2
    c = jnp.full_like(w, 1.0 / math.factorial(16))
    s = jnp.full_like(w, -1.0 / math.factorial(15))
    for k in range(7, -1, -1):
        c = c * w + (-1.0) ** k / math.factorial(2 * k)
        if k < 7:
            s = s * w + (-1.0) ** k / math.factorial(2 * k + 1)
    return -c, -s * (2.0 * math.pi * x)


def pick(values, block):
    out = jnp.zeros(block.shape, jnp.int32)
    for j in range(NBLK):
        out = jnp.where(block == j, values[j], out)
    return out


def log_of(grid):
    return jnp.where(grid == 8, 3, jnp.where(grid == 16, 4, 5))


def slot_of(slot, grid):
    half = grid * grid // 2
    local = slot & (half - 1)
    pp = lax.shift_right_logical(local, log_of(grid))
    qq = local & (grid - 1)
    mid = lax.shift_right_logical(grid, 1)
    first = pp == 0
    special = first & ((qq == 0) | (qq == mid))
    p = jnp.where(first & (qq >= mid), mid, pp)
    q = jnp.where(first & (qq == mid), 0, qq)
    pm = jnp.where(special, p, (grid - p) & (grid - 1))
    qm = jnp.where(special, mid, (grid - q) & (grid - 1))
    return 2 * (slot - local), p, q, special, pm, qm


def build_tables(grid_ref, keep_ref, at, k1, k3, nm, nb):
    rows = at.shape[1]
    slots = rows // 2
    unit = slots // NBLK
    vals = [grid_ref[j] for j in range(NBLK)]
    lane = lax.broadcasted_iota(jnp.int32, (8, rows), 1)
    sub = lax.broadcasted_iota(jnp.int32, (8, rows), 0)
    gc = pick(vals, lane // (2 * unit))
    span = gc * gc
    start_c = lane & ~(span - 1)
    local = lane & (span - 1)
    p_c = lax.shift_right_logical(local, log_of(gc))
    q_c = local & (gc - 1)
    ginv = 1.0 / gc.astype(F32)
    bcs = []
    for j in range(4):
        q_r = (sub + 8 * j) & (gc - 1)
        bcs.append(cos_sin(((q_r * q_c) & (gc - 1)).astype(F32) * ginv))

    def two(x):
        return jnp.concatenate([x, x], 0)

    gc2, start2, p2, q2, ginv2, sub2 = two(gc), two(start_c), two(p_c), two(q_c), two(ginv), lax.broadcasted_iota(jnp.int32, (16, rows), 0)

    def step(i, carry):
        slot = (sub + 8 * i) * 8
        gb = jnp.where(sub < 4, grid_ref[2 * i], grid_ref[2 * i + 1])
        half = gb * gb // 2
        loc = slot & (half - 1)
        p_b = lax.shift_right_logical(loc, log_of(gb))
        ac, as_ = cos_sin(((p_b * p_c) & (gc - 1)).astype(F32) * ginv)
        same = jnp.where(2 * (slot - loc) == start_c, ginv, 0.0)
        ac = ac * same
        as_ = as_ * same
        for j in range(0, 8, 2):
            re, im = [], []
            for d in range(2):
                bc, bs = bcs[(j + d) % 4]
                a1 = ac[j + d : j + d + 1, :]
                a2 = as_[j + d : j + d + 1, :]
                re.append(a1 * bc - a2 * bs)
                im.append(-(a2 * bc + a1 * bs))
            s0 = pl.multiple_of(i * 64 + j * 8, 16)
            at[pl.ds(s0, 16), :] = jnp.concatenate(re, 0).astype(BF)
            at[pl.ds(slots + s0, 16), :] = jnp.concatenate(im, 0).astype(BF)
            g = grid_ref[2 * i + j // 4]
            first = (s0 & (g * g // 2 - 1)) < g

            @pl.when(first)
            def _():
                gv = jnp.full((16, rows), 0, jnp.int32) + g
                start, p, q, special, pm, qm = slot_of(sub2 + s0, gv)
                live = jnp.where(start == start2, ginv2, 0.0)
                t = ((p * p2 + q * q2) & (gc2 - 1)).astype(F32) * ginv2
                tm = ((pm * p2 + qm * q2) & (gc2 - 1)).astype(F32) * ginv2
                quarter = jnp.where(t >= 0.75, t - 0.75, t + 0.25)
                at[pl.ds(s0, 16), :] = (cos_of(t) * live).astype(BF)
                at[pl.ds(slots + s0, 16), :] = (cos_of(jnp.where(special, tm, quarter)) * live).astype(BF)

        return carry

    lax.fori_loop(0, slots // 64, step, 0)

    def mask(i, carry):
        slot = lax.broadcasted_iota(jnp.int32, (unit, 128), 0) + unit * i
        g = jnp.full((unit, 128), 0, jnp.int32) + grid_ref[i]
        _, p, q, special, pm, qm = slot_of(slot, g)
        k = jnp.where(g == 8, keep_ref[0], jnp.where(g == 16, keep_ref[1], keep_ref[2]))
        plus = jnp.where((p < k) & (q < k), 1.0, 0.0)
        minus = jnp.where((pm < k) & (qm < k), 1.0, 0.0)
        n = jnp.where(special, 0.0, 1.0)
        dst = pl.ds(pl.multiple_of(i * unit, unit), unit)
        nm[dst, :] = n.astype(BF)
        nb[dst, :] = (1.0 - n).astype(BF)
        for sign, (m, im) in enumerate(((plus, plus * n), (minus, -minus * n))):
            for ref, f in ((k1, 1.0), (k3, 0.05 * 0.0025)):
                ref[sign, dst, 0:128] = (m * f).astype(BF)
                ref[sign, dst, 128:256] = (im * f).astype(BF)
        return carry

    lax.fori_loop(0, NBLK, mask, 0)


def build_mix(w_ref, out_ref):
    i = lax.broadcasted_iota(jnp.int32, (64, 128), 0)
    j = lax.broadcasted_iota(jnp.int32, (64, 128), 1)
    dup = jnp.where((j & 63) == i, 1.0, 0.0).astype(BF)
    r = lax.broadcasted_iota(jnp.int32, (512, 128), 0)
    c = lax.broadcasted_iota(jnp.int32, (512, 128), 1)
    diag = ((r // 64) & 1) == (c // 64)
    for layer in range(LAYERS):
        re = jnp.where(diag, nn(w_ref[layer, 0], dup), 0.0)
        im = jnp.where(diag, nn(w_ref[layer, 1], dup), 0.0)
        for g in range(4):
            a = re[g * 128 : (g + 1) * 128].astype(BF)
            b = im[g * 128 : (g + 1) * 128]
            out_ref[layer, g, 0:128, 0:128] = a
            out_ref[layer, g, 128:256, 128:256] = a
            out_ref[layer, g, 0:128, 128:256] = b.astype(BF)
            out_ref[layer, g, 128:256, 0:128] = (-b).astype(BF)


def min_layer(layer):
    return layer if isinstance(layer, int) else jnp.minimum(layer, LAYERS - 1)


def fold(x):
    return jnp.sum(x.reshape(x.shape[0] // 8, 8, x.shape[1]), 0)


def kernel(
    grid_ref, keep_ref, core_ref, x_hbm, cot_hbm,
    n1g, n1b, w1_hbm, b1, w2_hbm, b2, n2g, n2b, fc1_hbm, fb1, fc2_hbm, fb2,
    out_hbm, xg_hbm, mine_hbm, other_hbm,
    x_ref, cot_ref, w1, w2, fc1, fc2, out_ref, grads_ref, sems,
    at, st, k1, k3, nm, nb, w1g, w2g,
    xh1, rs1, hu, ul, z, o, da, ds, pq, xh2, rs2, v, act, dp,
    gmid, acc,
):
    g_s, gy, gm, xg_ref = hu, ul, x_ref, cot_ref

    def copy(k, src, dst):
        return pltpu.make_async_copy(src, dst, sems.at[k])

    loads = [
        copy(k, src, dst)
        for k, (src, dst) in enumerate(
            ((x_hbm, x_ref), (w1_hbm, w1), (w2_hbm, w2), (fc1_hbm, fc1), (fc2_hbm, fc2), (cot_hbm, cot_ref))
        )
    ]
    for c in loads:
        c.start()
    rows = x_ref.shape[0]
    slots = rows // 2
    tiles = rows // RT
    stiles = slots // ST
    build_tables(grid_ref, keep_ref, at, k1, k3, nm, nb)
    for i in range(4):
        st[:, i * 256 : (i + 1) * 256] = at[i * 256 : (i + 1) * 256, :].T
    loads[1].wait()
    loads[2].wait()
    build_mix(w1, w1g)
    build_mix(w2, w2g)
    acc[...] = jnp.zeros_like(acc)

    def tile(i):
        return slice(i * RT, (i + 1) * RT)

    def chunk(i, j):
        return slice(i * RT + j * CH, i * RT + (j + 1) * CH)

    def add_to(layer, k, x):
        acc[layer, k] = acc[layer, k] + fold(x)

    def norm1(layer, dst, h):
        mean = jnp.mean(h, -1, keepdims=True)
        cent = h - mean
        rstd = lax.rsqrt(jnp.mean(cent * cent, -1, keepdims=True) + 1e-05)
        xh = cent * rstd
        u = xh * n1g[pl.ds(min_layer(layer), 1), :] + n1b[pl.ds(min_layer(layer), 1), :]
        xh1[layer, dst, :] = xh.astype(BF)
        rs1[layer, dst, :] = jnp.broadcast_to(rstd, (CH, 128))
        ul[dst, :] = u.astype(BF)
        hu[dst, :] = h + u

    def enter():
        for i in range(tiles):
            for j in range(RT // CH):
                dst = chunk(i, j)
                norm1(0, dst, x_ref[dst, :].astype(F32))

    def block(f):
        f()

    loads[0].wait()
    enter()
    loads[3].wait()
    loads[4].wait()
    loads[5].wait()

    def lanes(x, times):
        return jnp.concatenate([x] * times, 1)

    def analyse(layer, t, p):
        sl = slice(t * ST, (t + 1) * ST)
        h = p % 2
        hs = slice(h * 256, (h + 1) * 256)
        if p < 2:
            zr = nn(at[sl, :], ul[:, hs]).astype(BF)
            for e in range(2):
                c0 = (2 * h + e) * 256
                z[layer, 0, sl, c0 : c0 + 128] = zr[:, e * 128 : e * 128 + 128]
        else:
            n, nbar = nm[sl, :], nb[sl, :]
            zi = nn(at[slots + t * ST : slots + (t + 1) * ST, :], ul[:, hs]).astype(BF)
            for e in range(2):
                c0 = (2 * h + e) * 256
                zie = zi[:, e * 128 : e * 128 + 128]
                zin = zie * n
                z[layer, 0, sl, c0 + 128 : c0 + 256] = zin
                z[layer, 1, sl, c0 + 128 : c0 + 256] = -zin
                z[layer, 1, sl, c0 : c0 + 128] = z[layer, 0, sl, c0 : c0 + 128] * n + zie * nbar

    def both(ref, layer, sl, gl):
        return ref[layer, :, sl, gl].reshape(2 * ST, 256)

    def put(ref, layer, sl, gl, x, c=None):
        if c is None:
            ref[layer, :, sl, gl] = x.reshape(2, ST, 256)
        else:
            r0 = sl.start + c % ST
            ref[layer, c // ST, r0 : r0 + CE, gl] = x

    def combine(dst, sl, cs, x, signed):
        n, nbar = nm[sl, :], nb[sl, :]
        rp, ip = x[0:ST, 0:128], x[0:ST, 128:256]
        rm, im = x[ST : 2 * ST, 0:128], x[ST : 2 * ST, 128:256]
        dst[sl, cs] = rp + rm * n
        q = ip + im if signed else (ip - im) * n
        dst[slots + sl.start : slots + sl.stop, cs] = q + rm * nbar

    def mix_forward(layer):
        def cut(k):
            t, g = k // 4, k % 4
            return slice(t * ST, (t + 1) * ST), slice(g * 128, (g + 1) * 128), slice(g * 256, (g + 1) * 256), g

        def dot_a(k):
            sl, cs, gl, g = cut(k)
            return nn(both(z, layer, sl, gl), w1g[layer, g])

        def gelu_a(k, a):
            sl, cs, gl, g = cut(k)
            bias = lanes2(b1[layer, 0:1, cs], b1[layer, 1:2, cs])
            ys = []
            for c in range(0, 2 * ST, CE):
                og, dag = gelu_split(a[c : c + CE] + bias)
                ys.append(og)
                put(o, layer, sl, gl, og, c)
                put(da, layer, sl, gl, dag, c)
            return nn(jnp.concatenate(ys, 0), w2g[layer, g])

        def shrink_e(k, ew):
            sl, cs, gl, g = cut(k)
            bias = lanes2(b2[layer, 0:1, cs], b2[layer, 1:2, cs])
            for c in range(0, ST, CE):
                rs = slice(sl.start + c, sl.start + c + CE)
                ss = []
                for sign in range(2):
                    e = ew[sign * ST + c : sign * ST + c + CE] + bias
                    r = lax.rsqrt(e * e + 0.0025)
                    c1 = k1[sign, rs, :]
                    ss.append((e - 0.05 * (e * r)).astype(BF) * c1)
                    r = r.astype(BF)
                    ds[layer, sign, rs, gl] = c1 - k3[sign, rs, :] * (r * r * r)
                n, nbar = nm[rs, :], nb[rs, :]
                rm = ss[1][:, 0:128]
                pq[rs, cs] = ss[0][:, 0:128] + rm * n
                pq[slots + rs.start : slots + rs.stop, cs] = ss[0][:, 128:256] + ss[1][:, 128:256] + rm * nbar

        steps = stiles * 4
        for p in range(4):
            analyse(layer, 0, p)
        a = dot_a(0)
        e_prev = None
        for k in range(steps):
            t, g = k // 4, k % 4
            if t + 1 < stiles:
                analyse(layer, t + 1, g)
            nxt = dot_a(k + 1) if k + 1 < steps else None
            e = gelu_a(k, a)
            if e_prev is not None:
                shrink_e(k - 1, e_prev)
            a, e_prev = nxt, e
        shrink_e(steps - 1, e_prev)

    def ff_forward(layer):
        def norm2(i, y):
            for j in range(RT // CH):
                cd = chunk(i, j)
                mid = y[j * CH : (j + 1) * CH] + hu[cd, :]
                mean = jnp.mean(mid, -1, keepdims=True)
                cent = mid - mean
                rstd = lax.rsqrt(jnp.mean(cent * cent, -1, keepdims=True) + 1e-05)
                xh = cent * rstd
                xh2[layer, cd, :] = xh.astype(BF)
                rs2[layer, cd, :] = jnp.broadcast_to(rstd, (CH, 128))
                v[layer, cd, :] = (xh * n2g[pl.ds(layer, 1), :] + n2b[pl.ds(layer, 1), :]).astype(BF)
                hu[cd, :] = mid
            return nn(v[layer, tile(i), :], fc1[layer])

        def gelu_f(i, pre):
            for j in range(0, RT, CF):
                cd = slice(i * RT + j, i * RT + j + CF)
                act[layer, cd, :], dp[layer, cd, :] = gelu_split(pre[j : j + CF] + fb1[pl.ds(layer, 1), :])
            return nn(act[layer, tile(i), :], fc2[layer])

        def leave(i, br):
            for j in range(RT // CH):
                cd = chunk(i, j)
                h = hu[cd, :] + (br[j * CH : (j + 1) * CH] + fb2[pl.ds(layer, 1), :])
                out_ref[cd, :] = h.astype(BF)
                norm1(layer + 1, cd, h)

        def dot_y(i):
            return nn(st[tile(i), :], pq[...])

        y = dot_y(0)
        pre = None
        for i in range(tiles + 1):
            nxt = dot_y(i + 1) if i + 1 < tiles else None
            br = gelu_f(i - 1, pre) if i >= 1 else None
            pre = norm2(i, y) if i < tiles else None
            if i >= 1:
                leave(i - 1, br)
            y = nxt

    @partial(lax.fori_loop, 0, LAYERS, init_val=0)
    def _(layer, carry):
        block(lambda: mix_forward(layer))
        block(lambda: ff_forward(layer))
        return carry

    out_copy = copy(6, out_ref, out_hbm)
    out_copy.start()
    for i in range(tiles):
        g_s[tile(i), :] = cot_ref[tile(i), :].astype(F32)

    def norm_back(gv, xh, rstd, gain):
        t = gv * gain
        mt = jnp.mean(t, -1, keepdims=True)
        mx = jnp.mean(t * xh, -1, keepdims=True)
        return rstd * (t - mt - xh * mx)

    def with_sums(left, right):
        ones = jnp.ones((16, left.shape[0]), BF)
        return nn(jnp.concatenate([left.T, ones], 0), right)

    def ff_backward(layer):
        def load_g(rs):
            return g_s[rs, :]

        def dot_a(i):
            dst = tile(i)
            gmt = g_s[dst, :].astype(BF)
            gm[dst, :] = gmt
            return nt(gmt, fc2[layer])

        def mul(i, ga_):
            dst = tile(i)
            dp[layer, dst, :] = ga_.astype(BF) * dp[layer, dst, :]
            return nt(dp[layer, dst, :], fc1[layer])

        def leave(i, gv):
            for j in range(RT // CH):
                cd = chunk(i, j)
                gvc = gv[j * CH : (j + 1) * CH]
                xh = xh2[layer, cd, :].astype(F32)
                add_to(layer, 6, gvc * xh)
                add_to(layer, 7, gvc)
                rstd = lanes(rs2[layer, cd, :], 4)
                gmc = load_g(cd) + norm_back(gvc, xh, rstd, n2g[pl.ds(layer, 1), :])
                gmid[cd, :] = gmc
                gy[cd, :] = gmc.astype(BF)

        cur = dot_a(0)
        prev = None
        for i in range(tiles + 1):
            nxt = dot_a(i + 1) if i + 1 < tiles else None
            gv = mul(i, cur) if i < tiles else None
            if i >= 1:
                leave(i - 1, prev)
            cur, prev = nxt, gv
        base = pl.multiple_of((layer ^ core_ref[0]) * PER, PER)
        for left, right, off, vec in ((v, dp[layer], 0, 8), (act, gm[...], 512, 9)):
            for h in range(2):
                hs = slice(h * 256, (h + 1) * 256)
                r = base + off + h * 256
                if h == 0:
                    p = with_sums(left[layer, :, hs], right)
                    acc[layer, vec, 0:1, :] = p[256:257]
                else:
                    p = tn(left[layer, :, hs], right)
                grads_ref[pl.ds(r, 256), :] = p[0:256].astype(BF)

    def mix_backward(layer):
        def cut(k):
            t, g = k // 4, k % 4
            return slice(t * ST, (t + 1) * ST), slice(g * 128, (g + 1) * 128), slice(g * 256, (g + 1) * 256), g

        def spectrum(t, h):
            hs = slice(h * 256, (h + 1) * 256)
            gr = nn(at[t * ST : (t + 1) * ST, :], gy[:, hs]).astype(BF)
            gi = nn(at[slots + t * ST : slots + (t + 1) * ST, :], gy[:, hs]).astype(BF)
            return gr, gi

        def dot_o(k, gr, gi):
            sl, cs, gl, g = cut(k)
            n, nbar = nm[sl, :], nb[sl, :]
            hs = slice(g % 2 * 128, g % 2 * 128 + 128)
            grc, gic = gr[:, hs], gi[:, hs]
            ds[layer, 0, sl, gl] = lanes2(grc, gic) * ds[layer, 0, sl, gl]
            ds[layer, 1, sl, gl] = lanes2(grc * n + gic * nbar, gic) * ds[layer, 1, sl, gl]
            return nt(both(ds, layer, sl, gl), w2g[layer, g])

        def dot_z(k, go):
            sl, cs, gl, g = cut(k)
            put(da, layer, sl, gl, go.astype(BF) * both(da, layer, sl, gl))
            return nt(both(da, layer, sl, gl), w1g[layer, g])

        def leave(k, gz):
            sl, cs, gl, g = cut(k)
            combine(pq, sl, cs, gz.astype(BF), False)

        steps = stiles * 4
        sp = {0: spectrum(0, 0)}
        go = dot_o(0, *sp[0])
        prev = None
        for k in range(steps + 1):
            if k % 2 == 0 and k + 2 < steps:
                sp[k // 2 + 1] = spectrum((k + 2) // 4, (k + 2) // 2 % 2)
            nxt = dot_o(k + 1, *sp[(k + 1) // 2]) if k + 1 < steps else None
            gz = dot_z(k, go) if k < steps else None
            if k >= 1:
                leave(k - 1, prev)
            go, prev = nxt, gz
        base = pl.multiple_of((layer ^ core_ref[0]) * PER, PER) + 1024
        low = lax.broadcasted_iota(jnp.int32, (64, 128), 1) < 64
        for left, right, off, vec in ((o, ds, base + 128, 4), (z, da, base, 2)):
            for g in range(4):
                cs = slice(g * 128, (g + 1) * 128)
                gl = slice(g * 256, (g + 1) * 256)
                lf = left[layer, :, :, gl].reshape(rows, 256)
                rt = right[layer, :, :, gl].reshape(rows, 256)
                p = with_sums(lf, rt)
                acc[layer, vec, 0:1, cs] = p[256:257, 0:128]
                acc[layer, vec + 1, 0:1, cs] = p[256:257, 128:256]
                re = p[0:128, 0:128] + p[128:256, 128:256]
                im = p[0:128, 128:256] - p[128:256, 0:128]
                grads_ref[pl.ds(off, 64), cs] = jnp.where(low, re[0:64], re[64:128]).astype(BF)
                grads_ref[pl.ds(off + 64, 64), cs] = jnp.where(low, im[0:64], im[64:128]).astype(BF)

    def in_backward(layer):
        def leave(i, y):
            for j in range(RT // CH):
                cd = chunk(i, j)
                gmc = gmid[cd, :]
                gu = y[j * CH : (j + 1) * CH] + gmc
                xh = xh1[layer, cd, :].astype(F32)
                add_to(layer, 0, gu * xh)
                add_to(layer, 1, gu)
                rstd = lanes(rs1[layer, cd, :], 4)
                gh = gmc + norm_back(gu, xh, rstd, n1g[pl.ds(min_layer(layer), 1), :])
                xg_ref[cd, :] = gh.astype(BF)
                g_s[cd, :] = gh

        y = nn(st[tile(0), :], pq[...])
        for i in range(tiles):
            nxt = nn(st[tile(i + 1), :], pq[...]) if i + 1 < tiles else None
            leave(i, y)
            y = nxt

    @partial(lax.fori_loop, 0, LAYERS, init_val=0)
    def _(step, carry):
        layer = LAYERS - 1 - step
        block(lambda: ff_backward(layer))
        block(lambda: mix_backward(layer))
        block(lambda: in_backward(layer))
        return carry

    def vectors(layer):
        t = jnp.sum(acc[layer], 1)
        t = jnp.concatenate([t, jnp.zeros((PER - 1290, 512), F32)], 0)
        grads_ref[pl.ds(pl.multiple_of((layer ^ core_ref[0]) * PER, PER) + 1280, PER - 1280), :] = t.astype(BF)

    vectors(1)
    mine_copy = copy(8, grads_ref.at[pl.ds(0, PER)], mine_hbm)
    other_copy = copy(9, grads_ref.at[pl.ds(PER, PER)], other_hbm)
    xg_copy = copy(7, xg_ref, xg_hbm)
    vectors(0)
    other_copy.start()
    mine_copy.start()
    xg_copy.start()
    out_copy.wait()
    other_copy.wait()
    mine_copy.wait()
    xg_copy.wait()


def lanes2(a, b):
    return jnp.concatenate([a, b], 1)


def local_step(core, x_in, cotangent, block_grid, keep_modes, n1g, n1b, w1, b1, w2, b2, n2g, n2b, fc1, fb1, fc2, fb2):
    rows, d = x_in.shape
    slots = rows // 2
    vm = pl.BlockSpec(memory_space=pltpu.VMEM)
    sm = pl.BlockSpec(memory_space=pltpu.SMEM)
    hbm = pl.BlockSpec(memory_space=pl.ANY)
    w1r = w1.reshape(LAYERS, 2, 512, 64)
    w2r = w2.reshape(LAYERS, 2, 512, 64)
    scratch = [
        pltpu.VMEM((rows, d), BF), pltpu.VMEM((rows, d), BF),
        pltpu.VMEM(w1r.shape, BF), pltpu.VMEM(w2r.shape, BF), pltpu.VMEM(fc1.shape, BF), pltpu.VMEM(fc2.shape, BF),
        pltpu.VMEM((rows, d), BF), pltpu.VMEM((LAYERS * PER, d), BF),
        pltpu.SemaphoreType.DMA((10,)),
        pltpu.VMEM((rows, rows), BF), pltpu.VMEM((rows, rows), BF),
        pltpu.VMEM((2, slots, 256), BF), pltpu.VMEM((2, slots, 256), BF),
        pltpu.VMEM((slots, 128), BF), pltpu.VMEM((slots, 128), BF),
        pltpu.VMEM((LAYERS, 4, 256, 256), BF), pltpu.VMEM((LAYERS, 4, 256, 256), BF),
        pltpu.VMEM((LAYERS + 1, rows, d), BF), pltpu.VMEM((LAYERS + 1, rows, 128), F32),
        pltpu.VMEM((rows, d), F32), pltpu.VMEM((rows, d), BF),
        pltpu.VMEM((LAYERS, 2, slots, 2 * d), BF), pltpu.VMEM((LAYERS, 2, slots, 2 * d), BF),
        pltpu.VMEM((LAYERS, 2, slots, 2 * d), BF), pltpu.VMEM((LAYERS, 2, slots, 2 * d), BF),
        pltpu.VMEM((rows, d), BF),
        pltpu.VMEM((LAYERS, rows, d), BF), pltpu.VMEM((LAYERS, rows, 128), F32),
        pltpu.VMEM((LAYERS, rows, d), BF), pltpu.VMEM((LAYERS, rows, d), BF), pltpu.VMEM((LAYERS, rows, d), BF),
        pltpu.VMEM((rows, d), F32),
        pltpu.VMEM((LAYERS, 10, 8, d), F32),
    ]
    return pl.pallas_call(
        kernel,
        out_shape=(
            jax.ShapeDtypeStruct((rows, d), BF),
            jax.ShapeDtypeStruct((rows, d), BF),
            jax.ShapeDtypeStruct((PER, d), BF),
            jax.ShapeDtypeStruct((PER, d), BF),
        ),
        in_specs=[sm, sm, sm, hbm, hbm, vm, vm, hbm, vm, hbm, vm, vm, vm, hbm, vm, hbm, vm],
        out_specs=(hbm,) * 4,
        scratch_shapes=scratch,
        compiler_params=pltpu.CompilerParams(vmem_limit_bytes=58 * 1024 * 1024),
        name="slab_step",
    )(block_grid, keep_modes, core, x_in, cotangent, n1g, n1b, w1r, b1, w2r, b2, n2g, n2b, fc1, fb1, fc2, fb2)


AXES = ("dp", "modes")


def spread_layer(layer, src, outs, bufs, sems):
    fc1, fc2, w1, w2 = bufs
    fc1[...] = src[0:512, :].astype(F32)
    copies = [pltpu.make_async_copy(buf, out.at[layer], sems.at[k]) for k, (buf, out) in enumerate(zip(bufs, outs))]
    copies[0].start()
    fc2[...] = src[512:1024, :].astype(F32)
    copies[1].start()
    for k, (ref, base) in enumerate(((w1, 1024), (w2, 1152))):
        for part in range(2):
            block = src[base + part * 64 : base + part * 64 + 64, :].astype(F32)
            for j in range(8):
                ref[part, j] = block[:, j * 64 : j * 64 + 64]
        copies[2 + k].start()
    return copies


def spread_mine(core_ref, mine, fc1_out, fc2_out, w1_out, w2_out, fc1, fc2, w1, w2, sems):
    for c in spread_layer(core_ref[0], mine, (fc1_out, fc2_out, w1_out, w2_out), (fc1, fc2, w1, w2), sems):
        c.wait()


def spread_other(
    core_ref, mine, other, fc1_in, fc2_in, w1_in, w2_in,
    fc1_out, fc2_out, w1_out, w2_out, n1g, n1b, b1, b2, n2g, n2b, fb1, fb2, fc1, fc2, w1, w2, sems,
):
    copies = spread_layer(1 - core_ref[0], other, (fc1_out, fc2_out, w1_out, w2_out), (fc1, fc2, w1, w2), sems)
    here = mine[1280:1296, :].astype(F32)
    there = other[1280:1296, :].astype(F32)
    for layer in range(LAYERS):
        vec = jnp.where(core_ref[0] == layer, here, there)
        for row, ref in ((0, n1g), (1, n1b), (6, n2g), (7, n2b), (8, fb1), (9, fb2)):
            ref[layer : layer + 1, :] = vec[row : row + 1]
        b1[layer] = vec[2:4]
        b2[layer] = vec[4:6]
    for c in copies:
        c.wait()


def unpack_shapes(d):
    mix = jax.ShapeDtypeStruct((LAYERS, 2, 8, 64, 64), F32)
    full = jax.ShapeDtypeStruct((LAYERS, d, d), F32)
    big = (full, full, mix, mix)
    scratch = [pltpu.VMEM(s.shape[1:], F32) for s in big] + [pltpu.SemaphoreType.DMA((4,))]
    return big, scratch


def unpack_mine(core, mine, d):
    vm = pl.BlockSpec(memory_space=pltpu.VMEM)
    hbm = pl.BlockSpec(memory_space=pl.ANY)
    big, scratch = unpack_shapes(d)
    return pl.pallas_call(
        spread_mine,
        out_shape=big,
        in_specs=[pl.BlockSpec(memory_space=pltpu.SMEM), vm],
        out_specs=(hbm,) * 4,
        scratch_shapes=scratch,
        compiler_params=pltpu.CompilerParams(vmem_limit_bytes=16 * 1024 * 1024),
        cost_estimate=pl.CostEstimate(flops=1 << 20, bytes_accessed=4 << 20, transcendentals=0),
        name="spread_mine",
    )(core, mine)


def unpack(core, mine, other, d, big_in=None):
    vm = pl.BlockSpec(memory_space=pltpu.VMEM)
    hbm = pl.BlockSpec(memory_space=pl.ANY)
    big, scratch = unpack_shapes(d)
    vec = jax.ShapeDtypeStruct((LAYERS, d), F32)
    pair = jax.ShapeDtypeStruct((LAYERS, 2, d), F32)
    if big_in is None:
        big_in = unpack_mine(core, mine, d)
    fc1, fc2, w1, w2, n1g, n1b, b1, b2, n2g, n2b, fb1, fb2 = pl.pallas_call(
        spread_other,
        out_shape=big + (vec, vec, pair, pair, vec, vec, vec, vec),
        in_specs=[pl.BlockSpec(memory_space=pltpu.SMEM), vm, vm] + [hbm] * 4,
        out_specs=(hbm,) * 4 + (vm,) * 8,
        scratch_shapes=scratch,
        input_output_aliases={3: 0, 4: 1, 5: 2, 6: 3},
        compiler_params=pltpu.CompilerParams(vmem_limit_bytes=16 * 1024 * 1024),
        name="spread_other",
    )(core, mine, other, *big_in)
    return n1g, n1b, w1, b1, w2, b2, n2g, n2b, fc1, fb1, fc2, fb2


def exchange(a, bit, count):
    return lax.ppermute(a, AXES, [(i, i ^ bit) for i in range(count)])


def add(a, b):
    return (a.astype(F32) + b.astype(F32)).astype(BF)


def all_sum(mine, other, count):
    me = lax.axis_index(AXES)
    top = count // 2
    mine = add(mine, exchange(other, top, count))
    bits = [1 << k for k in range(top.bit_length() - 1)]
    orders = [[bits[(c + k) % 3] for k in range(3)] for c in range(3)]
    third = PER // 3
    parts = [mine[c * third : (c + 1) * third] for c in range(3)]
    for k in range(3):
        moved = []
        for c in range(3):
            n = parts[c].shape[0] // 2
            high = (me & orders[c][k]) != 0
            keep = jnp.where(high, parts[c][n:], parts[c][:n])
            send = jnp.where(high, parts[c][:n], parts[c][n:])
            moved.append((keep, exchange(send, orders[c][k], count)))
        parts = [add(keep, got) for keep, got in moved]
    n = parts[0].shape[0]
    last = jnp.concatenate(parts)
    for bit in bits[3:]:
        last = add(last, exchange(last, bit, count))
    parts = [last[c * n : (c + 1) * n] for c in range(3)]
    for k in reversed(range(3)):
        gots = [exchange(parts[c], orders[c][k], count) for c in range(3)]
        for c in range(3):
            high = (me & orders[c][k]) != 0
            low_part = jnp.where(high, gots[c], parts[c])
            high_part = jnp.where(high, parts[c], gots[c])
            parts[c] = jnp.concatenate([low_part, high_part])
    mine = jnp.concatenate(parts)
    return mine, exchange(mine, top, count)


def solution(mesh):
    count = mesh.shape["dp"] * mesh.shape["modes"]

    def on_device(*args):
        core = lax.axis_index("dp").astype(jnp.int32).reshape(1)
        out, x_grad, mine, other = local_step(core, *args)
        mine, other = all_sum(mine, other, count)
        return (out, x_grad) + tuple(unpack(core, mine, other, mine.shape[1]))

    rows = P(AXES, None)
    return jax.shard_map(
        on_device,
        mesh=mesh,
        in_specs=(rows, rows, P(AXES)) + (P(),) * 13,
        out_specs=(rows, rows) + (P(),) * 12,
        check_vma=False,
    )
```

```python
import math
from functools import partial

import jax
import jax.numpy as jnp
from jax import lax
from jax.experimental import pallas as pl
from jax.experimental.pallas import tpu as pltpu
from jax.sharding import PartitionSpec as P

LAYERS = 2
NBLK = 16
F32 = jnp.float32
BF = jnp.bfloat16
C0 = math.sqrt(2.0 / math.pi)
C1 = 0.044715 * C0
PER = 1344
RT = 256
ST = 256
NH = 512
CH = 64
CE = 32
CF = 16


def nn(a, b):
    return jnp.dot(a, b, preferred_element_type=F32)


def nt(a, b):
    return lax.dot_general(a, b, (((1,), (1,)), ((), ())), preferred_element_type=F32)


def tn(a, b):
    return lax.dot_general(a, b, (((0,), (0,)), ((), ())), preferred_element_type=F32)


def gelu_pair(x):
    x2 = x * x
    p = 0.5 + 0.5 * jnp.tanh(x * (C0 + C1 * x2))
    y = x * p
    return y, p + y * (1.0 - p) * (2.0 * C0 + (6.0 * C1) * x2)


def gelu_split(x):
    p = 0.5 + 0.5 * jnp.tanh(x * (C0 + C1 * (x * x)))
    y = (x * p).astype(BF)
    xb, pb, qb = x.astype(BF), p.astype(BF), (1.0 - p).astype(BF)
    return y, pb + y * qb * (2.0 * C0 + (6.0 * C1) * (xb * xb))


def cos_of(t):
    x = t - 0.5
    w = (2.0 * math.pi * x) ** 2
    c = jnp.full_like(w, 1.0 / math.factorial(16))
    for k in range(7, -1, -1):
        c = c * w + (-1.0) ** k / math.factorial(2 * k)
    return -c


def cos_sin(t):
    x = t - 0.5
    w = (2.0 * math.pi * x) ** 2
    c = jnp.full_like(w, 1.0 / math.factorial(16))
    s = jnp.full_like(w, -1.0 / math.factorial(15))
    for k in range(7, -1, -1):
        c = c * w + (-1.0) ** k / math.factorial(2 * k)
        if k < 7:
            s = s * w + (-1.0) ** k / math.factorial(2 * k + 1)
    return -c, -s * (2.0 * math.pi * x)


def pick(values, block):
    out = jnp.zeros(block.shape, jnp.int32)
    for j in range(NBLK):
        out = jnp.where(block == j, values[j], out)
    return out


def log_of(grid):
    return jnp.where(grid == 8, 3, jnp.where(grid == 16, 4, 5))


def slot_of(slot, grid):
    half = grid * grid // 2
    local = slot & (half - 1)
    pp = lax.shift_right_logical(local, log_of(grid))
    qq = local & (grid - 1)
    mid = lax.shift_right_logical(grid, 1)
    first = pp == 0
    special = first & ((qq == 0) | (qq == mid))
    p = jnp.where(first & (qq >= mid), mid, pp)
    q = jnp.where(first & (qq == mid), 0, qq)
    pm = jnp.where(special, p, (grid - p) & (grid - 1))
    qm = jnp.where(special, mid, (grid - q) & (grid - 1))
    return 2 * (slot - local), p, q, special, pm, qm


def build_tables(grid_ref, keep_ref, at, k1, k3, nm, nb):
    rows = at.shape[1]
    slots = rows // 2
    unit = slots // NBLK
    vals = [grid_ref[j] for j in range(NBLK)]
    lane = lax.broadcasted_iota(jnp.int32, (8, rows), 1)
    sub = lax.broadcasted_iota(jnp.int32, (8, rows), 0)
    gc = pick(vals, lane // (2 * unit))
    span = gc * gc
    start_c = lane & ~(span - 1)
    local = lane & (span - 1)
    p_c = lax.shift_right_logical(local, log_of(gc))
    q_c = local & (gc - 1)
    ginv = 1.0 / gc.astype(F32)
    bcs = []
    for j in range(4):
        q_r = (sub + 8 * j) & (gc - 1)
        bcs.append(cos_sin(((q_r * q_c) & (gc - 1)).astype(F32) * ginv))

    def two(x):
        return jnp.concatenate([x, x], 0)

    gc2, start2, p2, q2, ginv2, sub2 = two(gc), two(start_c), two(p_c), two(q_c), two(ginv), lax.broadcasted_iota(jnp.int32, (16, rows), 0)

    def step(i, carry):
        slot = (sub + 8 * i) * 8
        gb = jnp.where(sub < 4, grid_ref[2 * i], grid_ref[2 * i + 1])
        half = gb * gb // 2
        loc = slot & (half - 1)
        p_b = lax.shift_right_logical(loc, log_of(gb))
        ac, as_ = cos_sin(((p_b * p_c) & (gc - 1)).astype(F32) * ginv)
        same = jnp.where(2 * (slot - loc) == start_c, ginv, 0.0)
        ac = ac * same
        as_ = as_ * same
        for j in range(0, 8, 2):
            re, im = [], []
            for d in range(2):
                bc, bs = bcs[(j + d) % 4]
                a1 = ac[j + d : j + d + 1, :]
                a2 = as_[j + d : j + d + 1, :]
                re.append(a1 * bc - a2 * bs)
                im.append(-(a2 * bc + a1 * bs))
            s0 = pl.multiple_of(i * 64 + j * 8, 16)
            at[pl.ds(s0, 16), :] = jnp.concatenate(re, 0).astype(BF)
            at[pl.ds(slots + s0, 16), :] = jnp.concatenate(im, 0).astype(BF)
            g = grid_ref[2 * i + j // 4]
            first = (s0 & (g * g // 2 - 1)) < g

            @pl.when(first)
            def _():
                gv = jnp.full((16, rows), 0, jnp.int32) + g
                start, p, q, special, pm, qm = slot_of(sub2 + s0, gv)
                live = jnp.where(start == start2, ginv2, 0.0)
                t = ((p * p2 + q * q2) & (gc2 - 1)).astype(F32) * ginv2
                tm = ((pm * p2 + qm * q2) & (gc2 - 1)).astype(F32) * ginv2
                quarter = jnp.where(t >= 0.75, t - 0.75, t + 0.25)
                at[pl.ds(s0, 16), :] = (cos_of(t) * live).astype(BF)
                at[pl.ds(slots + s0, 16), :] = (cos_of(jnp.where(special, tm, quarter)) * live).astype(BF)

        return carry

    lax.fori_loop(0, slots // 64, step, 0)

    def mask(i, carry):
        slot = lax.broadcasted_iota(jnp.int32, (unit, 128), 0) + unit * i
        g = jnp.full((unit, 128), 0, jnp.int32) + grid_ref[i]
        _, p, q, special, pm, qm = slot_of(slot, g)
        k = jnp.where(g == 8, keep_ref[0], jnp.where(g == 16, keep_ref[1], keep_ref[2]))
        plus = jnp.where((p < k) & (q < k), 1.0, 0.0)
        minus = jnp.where((pm < k) & (qm < k), 1.0, 0.0)
        n = jnp.where(special, 0.0, 1.0)
        dst = pl.ds(pl.multiple_of(i * unit, unit), unit)
        nm[dst, :] = n.astype(BF)
        nb[dst, :] = (1.0 - n).astype(BF)
        for sign, (m, im) in enumerate(((plus, plus * n), (minus, -minus * n))):
            for ref, f in ((k1, 1.0), (k3, 0.05 * 0.0025)):
                ref[sign, dst, 0:128] = (m * f).astype(BF)
                ref[sign, dst, 128:256] = (im * f).astype(BF)
        return carry

    lax.fori_loop(0, NBLK, mask, 0)


def build_mix(w_ref, out_ref):
    i = lax.broadcasted_iota(jnp.int32, (64, 128), 0)
    j = lax.broadcasted_iota(jnp.int32, (64, 128), 1)
    dup = jnp.where((j & 63) == i, 1.0, 0.0).astype(BF)
    r = lax.broadcasted_iota(jnp.int32, (512, 128), 0)
    c = lax.broadcasted_iota(jnp.int32, (512, 128), 1)
    diag = ((r // 64) & 1) == (c // 64)
    for layer in range(LAYERS):
        re = jnp.where(diag, nn(w_ref[layer, 0], dup), 0.0)
        im = jnp.where(diag, nn(w_ref[layer, 1], dup), 0.0)
        for g in range(4):
            a = re[g * 128 : (g + 1) * 128].astype(BF)
            b = im[g * 128 : (g + 1) * 128]
            out_ref[layer, g, 0:128, 0:128] = a
            out_ref[layer, g, 128:256, 128:256] = a
            out_ref[layer, g, 0:128, 128:256] = b.astype(BF)
            out_ref[layer, g, 128:256, 0:128] = (-b).astype(BF)


def min_layer(layer):
    return layer if isinstance(layer, int) else jnp.minimum(layer, LAYERS - 1)


def fold(x):
    return jnp.sum(x.reshape(x.shape[0] // 8, 8, x.shape[1]), 0)


def kernel(
    grid_ref, keep_ref, core_ref, x_hbm, cot_hbm,
    n1g, n1b, w1_hbm, b1, w2_hbm, b2, n2g, n2b, fc1_hbm, fb1, fc2_hbm, fb2,
    out_hbm, xg_hbm, m0, m1, m2, t0, t1, t2,
    x_ref, cot_ref, w1, w2, fc1, fc2, out_ref, grads_ref, sems,
    at, st, k1, k3, nm, nb, w1g, w2g,
    xh1, rs1, hu, ul, z, o, da, ds, pq, xh2, rs2, v, act, dp,
    gmid, acc,
):
    g_s, gy, gm, xg_ref = hu, ul, x_ref, cot_ref

    def copy(k, src, dst):
        return pltpu.make_async_copy(src, dst, sems.at[k])

    loads = [
        copy(k, src, dst)
        for k, (src, dst) in enumerate(
            ((x_hbm, x_ref), (w1_hbm, w1), (w2_hbm, w2), (fc1_hbm, fc1), (fc2_hbm, fc2), (cot_hbm, cot_ref))
        )
    ]
    for c in loads:
        c.start()
    rows = x_ref.shape[0]
    slots = rows // 2
    tiles = rows // RT
    stiles = slots // ST
    build_tables(grid_ref, keep_ref, at, k1, k3, nm, nb)
    for i in range(4):
        st[:, i * 256 : (i + 1) * 256] = at[i * 256 : (i + 1) * 256, :].T
    loads[1].wait()
    loads[2].wait()
    build_mix(w1, w1g)
    build_mix(w2, w2g)
    acc[...] = jnp.zeros_like(acc)

    def tile(i):
        return slice(i * RT, (i + 1) * RT)

    def chunk(i, j):
        return slice(i * RT + j * CH, i * RT + (j + 1) * CH)

    def add_to(layer, k, x):
        acc[layer, k] = acc[layer, k] + fold(x)

    def norm1(layer, dst, h):
        mean = jnp.mean(h, -1, keepdims=True)
        cent = h - mean
        rstd = lax.rsqrt(jnp.mean(cent * cent, -1, keepdims=True) + 1e-05)
        xh = cent * rstd
        u = xh * n1g[pl.ds(min_layer(layer), 1), :] + n1b[pl.ds(min_layer(layer), 1), :]
        xh1[layer, dst, :] = xh.astype(BF)
        rs1[layer, dst, :] = jnp.broadcast_to(rstd, (CH, 128))
        ul[dst, :] = u.astype(BF)
        hu[dst, :] = h + u

    def enter():
        for i in range(tiles):
            for j in range(RT // CH):
                dst = chunk(i, j)
                norm1(0, dst, x_ref[dst, :].astype(F32))

    def block(f):
        f()

    loads[0].wait()
    enter()
    loads[3].wait()
    loads[4].wait()
    loads[5].wait()

    def lanes(x, times):
        return jnp.concatenate([x] * times, 1)

    def analyse(layer, t, p):
        sl = slice(t * ST, (t + 1) * ST)
        h = p % 2
        hs = slice(h * 256, (h + 1) * 256)
        if p < 2:
            zr = nn(at[sl, :], ul[:, hs]).astype(BF)
            for e in range(2):
                c0 = (2 * h + e) * 256
                z[layer, 0, sl, c0 : c0 + 128] = zr[:, e * 128 : e * 128 + 128]
        else:
            n, nbar = nm[sl, :], nb[sl, :]
            zi = nn(at[slots + t * ST : slots + (t + 1) * ST, :], ul[:, hs]).astype(BF)
            for e in range(2):
                c0 = (2 * h + e) * 256
                zie = zi[:, e * 128 : e * 128 + 128]
                zin = zie * n
                z[layer, 0, sl, c0 + 128 : c0 + 256] = zin
                z[layer, 1, sl, c0 + 128 : c0 + 256] = -zin
                z[layer, 1, sl, c0 : c0 + 128] = z[layer, 0, sl, c0 : c0 + 128] * n + zie * nbar

    def both(ref, layer, sl, gl):
        return ref[layer, :, sl, gl].reshape(2 * ST, 256)

    def put(ref, layer, sl, gl, x, c=None):
        if c is None:
            ref[layer, :, sl, gl] = x.reshape(2, ST, 256)
        else:
            r0 = sl.start + c % ST
            ref[layer, c // ST, r0 : r0 + CE, gl] = x

    def combine(dst, sl, cs, x, signed):
        n, nbar = nm[sl, :], nb[sl, :]
        rp, ip = x[0:ST, 0:128], x[0:ST, 128:256]
        rm, im = x[ST : 2 * ST, 0:128], x[ST : 2 * ST, 128:256]
        dst[sl, cs] = rp + rm * n
        q = ip + im if signed else (ip - im) * n
        dst[slots + sl.start : slots + sl.stop, cs] = q + rm * nbar

    def mix_forward(layer):
        def cut(k):
            t, g = k // 4, k % 4
            return slice(t * ST, (t + 1) * ST), slice(g * 128, (g + 1) * 128), slice(g * 256, (g + 1) * 256), g

        def dot_a(k):
            sl, cs, gl, g = cut(k)
            return nn(both(z, layer, sl, gl), w1g[layer, g])

        def gelu_a(k, a):
            sl, cs, gl, g = cut(k)
            bias = lanes2(b1[layer, 0:1, cs], b1[layer, 1:2, cs])
            ys = []
            for c in range(0, 2 * ST, CE):
                og, dag = gelu_split(a[c : c + CE] + bias)
                ys.append(og)
                put(o, layer, sl, gl, og, c)
                put(da, layer, sl, gl, dag, c)
            return nn(jnp.concatenate(ys, 0), w2g[layer, g])

        def shrink_e(k, ew):
            sl, cs, gl, g = cut(k)
            bias = lanes2(b2[layer, 0:1, cs], b2[layer, 1:2, cs])
            for c in range(0, ST, CE):
                rs = slice(sl.start + c, sl.start + c + CE)
                ss = []
                for sign in range(2):
                    e = ew[sign * ST + c : sign * ST + c + CE] + bias
                    r = lax.rsqrt(e * e + 0.0025)
                    c1 = k1[sign, rs, :]
                    ss.append((e - 0.05 * (e * r)).astype(BF) * c1)
                    r = r.astype(BF)
                    ds[layer, sign, rs, gl] = c1 - k3[sign, rs, :] * (r * r * r)
                n, nbar = nm[rs, :], nb[rs, :]
                rm = ss[1][:, 0:128]
                pq[rs, cs] = ss[0][:, 0:128] + rm * n
                pq[slots + rs.start : slots + rs.stop, cs] = ss[0][:, 128:256] + ss[1][:, 128:256] + rm * nbar

        steps = stiles * 4
        for p in range(4):
            analyse(layer, 0, p)
        a = dot_a(0)
        e_prev = None
        for k in range(steps):
            t, g = k // 4, k % 4
            if t + 1 < stiles:
                analyse(layer, t + 1, g)
            nxt = dot_a(k + 1) if k + 1 < steps else None
            e = gelu_a(k, a)
            if e_prev is not None:
                shrink_e(k - 1, e_prev)
            a, e_prev = nxt, e
        shrink_e(steps - 1, e_prev)

    def ff_forward(layer):
        def norm2(i, y):
            for j in range(RT // CH):
                cd = chunk(i, j)
                mid = y[j * CH : (j + 1) * CH] + hu[cd, :]
                mean = jnp.mean(mid, -1, keepdims=True)
                cent = mid - mean
                rstd = lax.rsqrt(jnp.mean(cent * cent, -1, keepdims=True) + 1e-05)
                xh = cent * rstd
                xh2[layer, cd, :] = xh.astype(BF)
                rs2[layer, cd, :] = jnp.broadcast_to(rstd, (CH, 128))
                v[layer, cd, :] = (xh * n2g[pl.ds(layer, 1), :] + n2b[pl.ds(layer, 1), :]).astype(BF)
                hu[cd, :] = mid
            return nn(v[layer, tile(i), :], fc1[layer])

        def gelu_f(i, pre):
            for j in range(0, RT, CF):
                cd = slice(i * RT + j, i * RT + j + CF)
                act[layer, cd, :], dp[layer, cd, :] = gelu_split(pre[j : j + CF] + fb1[pl.ds(layer, 1), :])
            return nn(act[layer, tile(i), :], fc2[layer])

        def leave(i, br):
            for j in range(RT // CH):
                cd = chunk(i, j)
                h = hu[cd, :] + (br[j * CH : (j + 1) * CH] + fb2[pl.ds(layer, 1), :])
                out_ref[cd, :] = h.astype(BF)
                norm1(layer + 1, cd, h)

        def dot_y(i):
            return nn(st[tile(i), :], pq[...])

        y = dot_y(0)
        pre = None
        for i in range(tiles + 1):
            nxt = dot_y(i + 1) if i + 1 < tiles else None
            br = gelu_f(i - 1, pre) if i >= 1 else None
            pre = norm2(i, y) if i < tiles else None
            if i >= 1:
                leave(i - 1, br)
            y = nxt

    @partial(lax.fori_loop, 0, LAYERS, init_val=0)
    def _(layer, carry):
        block(lambda: mix_forward(layer))
        block(lambda: ff_forward(layer))
        return carry

    out_copy = copy(6, out_ref, out_hbm)
    out_copy.start()
    for i in range(tiles):
        g_s[tile(i), :] = cot_ref[tile(i), :].astype(F32)

    def norm_back(gv, xh, rstd, gain):
        t = gv * gain
        mt = jnp.mean(t, -1, keepdims=True)
        mx = jnp.mean(t * xh, -1, keepdims=True)
        return rstd * (t - mt - xh * mx)

    def with_sums(left, right):
        ones = jnp.ones((16, left.shape[0]), BF)
        return nn(jnp.concatenate([left.T, ones], 0), right)

    def ff_backward(layer):
        def load_g(rs):
            return g_s[rs, :]

        def dot_a(i):
            dst = tile(i)
            gmt = g_s[dst, :].astype(BF)
            gm[dst, :] = gmt
            return nt(gmt, fc2[layer])

        def mul(i, ga_):
            dst = tile(i)
            dp[layer, dst, :] = ga_.astype(BF) * dp[layer, dst, :]
            return nt(dp[layer, dst, :], fc1[layer])

        def leave(i, gv):
            for j in range(RT // CH):
                cd = chunk(i, j)
                gvc = gv[j * CH : (j + 1) * CH]
                xh = xh2[layer, cd, :].astype(F32)
                add_to(layer, 6, gvc * xh)
                add_to(layer, 7, gvc)
                rstd = lanes(rs2[layer, cd, :], 4)
                gmc = load_g(cd) + norm_back(gvc, xh, rstd, n2g[pl.ds(layer, 1), :])
                gmid[cd, :] = gmc
                gy[cd, :] = gmc.astype(BF)

        cur = dot_a(0)
        prev = None
        for i in range(tiles + 1):
            nxt = dot_a(i + 1) if i + 1 < tiles else None
            gv = mul(i, cur) if i < tiles else None
            if i >= 1:
                leave(i - 1, prev)
            cur, prev = nxt, gv
        base = pl.multiple_of((layer ^ core_ref[0]) * PER, PER)
        for left, right, off, vec in ((v, dp[layer], 0, 8), (act, gm[...], 512, 9)):
            for h in range(2):
                hs = slice(h * 256, (h + 1) * 256)
                r = base + off + h * 256
                if h == 0:
                    p = with_sums(left[layer, :, hs], right)
                    acc[layer, vec, 0:1, :] = p[256:257]
                else:
                    p = tn(left[layer, :, hs], right)
                grads_ref[pl.ds(r, 256), :] = p[0:256].astype(BF)

    def mix_backward(layer):
        def cut(k):
            t, g = k // 4, k % 4
            return slice(t * ST, (t + 1) * ST), slice(g * 128, (g + 1) * 128), slice(g * 256, (g + 1) * 256), g

        def spectrum(t, h):
            hs = slice(h * 256, (h + 1) * 256)
            gr = nn(at[t * ST : (t + 1) * ST, :], gy[:, hs]).astype(BF)
            gi = nn(at[slots + t * ST : slots + (t + 1) * ST, :], gy[:, hs]).astype(BF)
            return gr, gi

        def dot_o(k, gr, gi):
            sl, cs, gl, g = cut(k)
            n, nbar = nm[sl, :], nb[sl, :]
            hs = slice(g % 2 * 128, g % 2 * 128 + 128)
            grc, gic = gr[:, hs], gi[:, hs]
            ds[layer, 0, sl, gl] = lanes2(grc, gic) * ds[layer, 0, sl, gl]
            ds[layer, 1, sl, gl] = lanes2(grc * n + gic * nbar, gic) * ds[layer, 1, sl, gl]
            return nt(both(ds, layer, sl, gl), w2g[layer, g])

        def dot_z(k, go):
            sl, cs, gl, g = cut(k)
            put(da, layer, sl, gl, go.astype(BF) * both(da, layer, sl, gl))
            return nt(both(da, layer, sl, gl), w1g[layer, g])

        def leave(k, gz):
            sl, cs, gl, g = cut(k)
            combine(pq, sl, cs, gz.astype(BF), False)

        steps = stiles * 4
        sp = {0: spectrum(0, 0)}
        go = dot_o(0, *sp[0])
        prev = None
        for k in range(steps + 1):
            if k % 2 == 0 and k + 2 < steps:
                sp[k // 2 + 1] = spectrum((k + 2) // 4, (k + 2) // 2 % 2)
            nxt = dot_o(k + 1, *sp[(k + 1) // 2]) if k + 1 < steps else None
            gz = dot_z(k, go) if k < steps else None
            if k >= 1:
                leave(k - 1, prev)
            go, prev = nxt, gz
        base = pl.multiple_of((layer ^ core_ref[0]) * PER, PER) + 1024
        low = lax.broadcasted_iota(jnp.int32, (64, 128), 1) < 64
        for left, right, off, vec in ((o, ds, base + 128, 4), (z, da, base, 2)):
            for g in range(4):
                cs = slice(g * 128, (g + 1) * 128)
                gl = slice(g * 256, (g + 1) * 256)
                lf = left[layer, :, :, gl].reshape(rows, 256)
                rt = right[layer, :, :, gl].reshape(rows, 256)
                p = with_sums(lf, rt)
                acc[layer, vec, 0:1, cs] = p[256:257, 0:128]
                acc[layer, vec + 1, 0:1, cs] = p[256:257, 128:256]
                re = p[0:128, 0:128] + p[128:256, 128:256]
                im = p[0:128, 128:256] - p[128:256, 0:128]
                grads_ref[pl.ds(off, 64), cs] = jnp.where(low, re[0:64], re[64:128]).astype(BF)
                grads_ref[pl.ds(off + 64, 64), cs] = jnp.where(low, im[0:64], im[64:128]).astype(BF)

    def in_backward(layer):
        def leave(i, y):
            for j in range(RT // CH):
                cd = chunk(i, j)
                gmc = gmid[cd, :]
                gu = y[j * CH : (j + 1) * CH] + gmc
                xh = xh1[layer, cd, :].astype(F32)
                add_to(layer, 0, gu * xh)
                add_to(layer, 1, gu)
                rstd = lanes(rs1[layer, cd, :], 4)
                gh = gmc + norm_back(gu, xh, rstd, n1g[pl.ds(min_layer(layer), 1), :])
                xg_ref[cd, :] = gh.astype(BF)
                g_s[cd, :] = gh

        y = nn(st[tile(0), :], pq[...])
        for i in range(tiles):
            nxt = nn(st[tile(i + 1), :], pq[...]) if i + 1 < tiles else None
            leave(i, y)
            y = nxt

    @partial(lax.fori_loop, 0, LAYERS, init_val=0)
    def _(step, carry):
        layer = LAYERS - 1 - step
        block(lambda: ff_backward(layer))
        block(lambda: mix_backward(layer))
        block(lambda: in_backward(layer))
        return carry

    def vectors(layer):
        t = jnp.sum(acc[layer], 1)
        t = jnp.concatenate([t, jnp.zeros((PER - 1290, 512), F32)], 0)
        grads_ref[pl.ds(pl.multiple_of((layer ^ core_ref[0]) * PER, PER) + 1280, PER - 1280), :] = t.astype(BF)

    vectors(1)
    sends = [
        copy(8 + k, grads_ref.at[pl.ds(row, PER // 3)], dst)
        for k, (row, dst) in enumerate(
            (((3 * half + c) * (PER // 3), dst) for half, refs in ((1, (t0, t1, t2)), (0, (m0, m1, m2))) for c, dst in enumerate(refs))
        )
    ]
    xg_copy = copy(7, xg_ref, xg_hbm)
    vectors(0)
    for c in sends:
        c.start()
    xg_copy.start()
    out_copy.wait()
    for c in sends:
        c.wait()
    xg_copy.wait()


def lanes2(a, b):
    return jnp.concatenate([a, b], 1)


def local_step(core, x_in, cotangent, block_grid, keep_modes, n1g, n1b, w1, b1, w2, b2, n2g, n2b, fc1, fb1, fc2, fb2):
    rows, d = x_in.shape
    slots = rows // 2
    vm = pl.BlockSpec(memory_space=pltpu.VMEM)
    sm = pl.BlockSpec(memory_space=pltpu.SMEM)
    hbm = pl.BlockSpec(memory_space=pl.ANY)
    w1r = w1.reshape(LAYERS, 2, 512, 64)
    w2r = w2.reshape(LAYERS, 2, 512, 64)
    scratch = [
        pltpu.VMEM((rows, d), BF), pltpu.VMEM((rows, d), BF),
        pltpu.VMEM(w1r.shape, BF), pltpu.VMEM(w2r.shape, BF), pltpu.VMEM(fc1.shape, BF), pltpu.VMEM(fc2.shape, BF),
        pltpu.VMEM((rows, d), BF), pltpu.VMEM((LAYERS * PER, d), BF),
        pltpu.SemaphoreType.DMA((14,)),
        pltpu.VMEM((rows, rows), BF), pltpu.VMEM((rows, rows), BF),
        pltpu.VMEM((2, slots, 256), BF), pltpu.VMEM((2, slots, 256), BF),
        pltpu.VMEM((slots, 128), BF), pltpu.VMEM((slots, 128), BF),
        pltpu.VMEM((LAYERS, 4, 256, 256), BF), pltpu.VMEM((LAYERS, 4, 256, 256), BF),
        pltpu.VMEM((LAYERS + 1, rows, d), BF), pltpu.VMEM((LAYERS + 1, rows, 128), F32),
        pltpu.VMEM((rows, d), F32), pltpu.VMEM((rows, d), BF),
        pltpu.VMEM((LAYERS, 2, slots, 2 * d), BF), pltpu.VMEM((LAYERS, 2, slots, 2 * d), BF),
        pltpu.VMEM((LAYERS, 2, slots, 2 * d), BF), pltpu.VMEM((LAYERS, 2, slots, 2 * d), BF),
        pltpu.VMEM((rows, d), BF),
        pltpu.VMEM((LAYERS, rows, d), BF), pltpu.VMEM((LAYERS, rows, 128), F32),
        pltpu.VMEM((LAYERS, rows, d), BF), pltpu.VMEM((LAYERS, rows, d), BF), pltpu.VMEM((LAYERS, rows, d), BF),
        pltpu.VMEM((rows, d), F32),
        pltpu.VMEM((LAYERS, 10, 8, d), F32),
    ]
    return pl.pallas_call(
        kernel,
        out_shape=(
            jax.ShapeDtypeStruct((rows, d), BF),
            jax.ShapeDtypeStruct((rows, d), BF),
        )
        + (jax.ShapeDtypeStruct((PER // 3, d), BF),) * 6,
        in_specs=[sm, sm, sm, hbm, hbm, vm, vm, hbm, vm, hbm, vm, vm, vm, hbm, vm, hbm, vm],
        out_specs=(hbm,) * 8,
        scratch_shapes=scratch,
        compiler_params=pltpu.CompilerParams(vmem_limit_bytes=58 * 1024 * 1024),
        name="slab_step",
    )(block_grid, keep_modes, core, x_in, cotangent, n1g, n1b, w1r, b1, w2r, b2, n2g, n2b, fc1, fb1, fc2, fb2)


AXES = ("dp", "modes")


def spread_layer(layer, parts, outs, bufs, sems):
    fc1, fc2, w1, w2 = bufs
    p0, p1, p2 = parts
    n = PER // 3
    copies = [pltpu.make_async_copy(buf, out.at[layer], sems.at[k]) for k, (buf, out) in enumerate(zip(bufs, outs))]
    fc1[0:n, :] = p0[...].astype(F32)
    fc1[n:512, :] = p1[0 : 512 - n, :].astype(F32)
    copies[0].start()
    fc2[0 : 2 * n - 512, :] = p1[512 - n : n, :].astype(F32)
    fc2[2 * n - 512 : 512, :] = p2[0 : 1024 - 2 * n, :].astype(F32)
    copies[1].start()
    for k, (ref, base) in enumerate(((w1, 1024 - 2 * n), (w2, 1152 - 2 * n))):
        for part in range(2):
            block = p2[base + part * 64 : base + part * 64 + 64, :].astype(F32)
            for j in range(8):
                ref[part, j] = block[:, j * 64 : j * 64 + 64]
        copies[2 + k].start()
    return copies


def spread_mine(core_ref, a0, a1, a2, fc1_out, fc2_out, w1_out, w2_out, fc1, fc2, w1, w2, sems):
    for c in spread_layer(core_ref[0], (a0, a1, a2), (fc1_out, fc2_out, w1_out, w2_out), (fc1, fc2, w1, w2), sems):
        c.wait()


def spread_other(
    core_ref, a0, a1, a2, c0, c1, c2, fc1_in, fc2_in, w1_in, w2_in,
    fc1_out, fc2_out, w1_out, w2_out, n1g, n1b, b1, b2, n2g, n2b, fb1, fb2, fc1, fc2, w1, w2, sems,
):
    copies = spread_layer(1 - core_ref[0], (c0, c1, c2), (fc1_out, fc2_out, w1_out, w2_out), (fc1, fc2, w1, w2), sems)
    row = 1280 - 2 * (PER // 3)
    here = a2[row : row + 16, :].astype(F32)
    there = c2[row : row + 16, :].astype(F32)
    for layer in range(LAYERS):
        vec = jnp.where(core_ref[0] == layer, here, there)
        for row, ref in ((0, n1g), (1, n1b), (6, n2g), (7, n2b), (8, fb1), (9, fb2)):
            ref[layer : layer + 1, :] = vec[row : row + 1]
        b1[layer] = vec[2:4]
        b2[layer] = vec[4:6]
    for c in copies:
        c.wait()


def unpack_shapes(d):
    mix = jax.ShapeDtypeStruct((LAYERS, 2, 8, 64, 64), F32)
    full = jax.ShapeDtypeStruct((LAYERS, d, d), F32)
    big = (full, full, mix, mix)
    scratch = [pltpu.VMEM(s.shape[1:], F32) for s in big] + [pltpu.SemaphoreType.DMA((4,))]
    return big, scratch


def unpack_mine(core, mine, d):
    vm = pl.BlockSpec(memory_space=pltpu.VMEM)
    hbm = pl.BlockSpec(memory_space=pl.ANY)
    big, scratch = unpack_shapes(d)
    return pl.pallas_call(
        spread_mine,
        out_shape=big,
        in_specs=[pl.BlockSpec(memory_space=pltpu.SMEM), vm, vm, vm],
        out_specs=(hbm,) * 4,
        scratch_shapes=scratch,
        compiler_params=pltpu.CompilerParams(vmem_limit_bytes=16 * 1024 * 1024),
        cost_estimate=pl.CostEstimate(flops=1 << 20, bytes_accessed=4 << 20, transcendentals=0),
        name="spread_mine",
    )(core, *mine)


def unpack(core, mine, other, d, big_in=None):
    vm = pl.BlockSpec(memory_space=pltpu.VMEM)
    hbm = pl.BlockSpec(memory_space=pl.ANY)
    big, scratch = unpack_shapes(d)
    vec = jax.ShapeDtypeStruct((LAYERS, d), F32)
    pair = jax.ShapeDtypeStruct((LAYERS, 2, d), F32)
    if big_in is None:
        big_in = unpack_mine(core, mine, d)
    fc1, fc2, w1, w2, n1g, n1b, b1, b2, n2g, n2b, fb1, fb2 = pl.pallas_call(
        spread_other,
        out_shape=big + (vec, vec, pair, pair, vec, vec, vec, vec),
        in_specs=[pl.BlockSpec(memory_space=pltpu.SMEM)] + [vm] * 6 + [hbm] * 4,
        out_specs=(hbm,) * 4 + (vm,) * 8,
        scratch_shapes=scratch,
        input_output_aliases={7: 0, 8: 1, 9: 2, 10: 3},
        compiler_params=pltpu.CompilerParams(vmem_limit_bytes=16 * 1024 * 1024),
        name="spread_other",
    )(core, *mine, *other, *big_in)
    return n1g, n1b, w1, b1, w2, b2, n2g, n2b, fc1, fb1, fc2, fb2


def exchange(a, bit, count):
    return lax.ppermute(a, AXES, [(i, i ^ bit) for i in range(count)])


def add(a, b):
    return (a.astype(F32) + b.astype(F32)).astype(BF)


def all_sum(mine, other, count):
    me = lax.axis_index(AXES)
    top = count // 2
    bits = [1 << k for k in range(top.bit_length() - 1)]
    orders = [[bits[(c + k) % 3] for k in range(3)] for c in range(3)]
    gots = [exchange(t, top, count) for t in other]
    parts = [add(m, got) for m, got in zip(mine, gots)]
    for k in range(3):
        moved = []
        for c in range(3):
            n = parts[c].shape[0] // 2
            high = (me & orders[c][k]) != 0
            keep = jnp.where(high, parts[c][n:], parts[c][:n])
            send = jnp.where(high, parts[c][:n], parts[c][n:])
            moved.append((keep, exchange(send, orders[c][k], count)))
        parts = [add(keep, got) for keep, got in moved]
    n = parts[0].shape[0]
    last = jnp.concatenate(parts)
    for bit in bits[3:]:
        last = add(last, exchange(last, bit, count))
    parts = [last[c * n : (c + 1) * n] for c in range(3)]
    for k in reversed(range(3)):
        gots = [exchange(parts[c], orders[c][k], count) for c in range(3)]
        for c in range(3):
            high = (me & orders[c][k]) != 0
            low_part = jnp.where(high, gots[c], parts[c])
            high_part = jnp.where(high, parts[c], gots[c])
            parts[c] = jnp.concatenate([low_part, high_part])
    return parts, [exchange(p, top, count) for p in parts]


def solution(mesh):
    count = mesh.shape["dp"] * mesh.shape["modes"]

    def on_device(*args):
        core = lax.axis_index("dp").astype(jnp.int32).reshape(1)
        out, x_grad, *parts = local_step(core, *args)
        mine, other = all_sum(parts[:3], parts[3:], count)
        return (out, x_grad) + tuple(unpack(core, mine, other, out.shape[1]))

    rows = P(AXES, None)
    return jax.shard_map(
        on_device,
        mesh=mesh,
        in_specs=(rows, rows, P(AXES)) + (P(),) * 13,
        out_specs=(rows, rows) + (P(),) * 12,
        check_vma=False,
    )
```

```python
import math
from functools import partial

import jax
import jax.numpy as jnp
from jax import lax
from jax.experimental import pallas as pl
from jax.experimental.pallas import tpu as pltpu
from jax.sharding import PartitionSpec as P

LAYERS = 2
NBLK = 16
F32 = jnp.float32
BF = jnp.bfloat16
C0 = math.sqrt(2.0 / math.pi)
C1 = 0.044715 * C0
PER = 1344
RT = 256
ST = 256
NH = 512
CH = 64
CE = 32
CF = 16


def nn(a, b):
    return jnp.dot(a, b, preferred_element_type=F32)


def nt(a, b):
    return lax.dot_general(a, b, (((1,), (1,)), ((), ())), preferred_element_type=F32)


def tn(a, b):
    return lax.dot_general(a, b, (((0,), (0,)), ((), ())), preferred_element_type=F32)


def gelu_pair(x):
    x2 = x * x
    p = 0.5 + 0.5 * jnp.tanh(x * (C0 + C1 * x2))
    y = x * p
    return y, p + y * (1.0 - p) * (2.0 * C0 + (6.0 * C1) * x2)


def gelu_split(x):
    p = 0.5 + 0.5 * jnp.tanh(x * (C0 + C1 * (x * x)))
    y = (x * p).astype(BF)
    xb, pb, qb = x.astype(BF), p.astype(BF), (1.0 - p).astype(BF)
    return y, pb + y * qb * (2.0 * C0 + (6.0 * C1) * (xb * xb))


def cos_of(t):
    x = t - 0.5
    w = (2.0 * math.pi * x) ** 2
    c = jnp.full_like(w, 1.0 / math.factorial(16))
    for k in range(7, -1, -1):
        c = c * w + (-1.0) ** k / math.factorial(2 * k)
    return -c


def cos_sin(t):
    x = t - 0.5
    w = (2.0 * math.pi * x) ** 2
    c = jnp.full_like(w, 1.0 / math.factorial(16))
    s = jnp.full_like(w, -1.0 / math.factorial(15))
    for k in range(7, -1, -1):
        c = c * w + (-1.0) ** k / math.factorial(2 * k)
        if k < 7:
            s = s * w + (-1.0) ** k / math.factorial(2 * k + 1)
    return -c, -s * (2.0 * math.pi * x)


def pick(values, block):
    out = jnp.zeros(block.shape, jnp.int32)
    for j in range(NBLK):
        out = jnp.where(block == j, values[j], out)
    return out


def log_of(grid):
    return jnp.where(grid == 8, 3, jnp.where(grid == 16, 4, 5))


def slot_of(slot, grid):
    half = grid * grid // 2
    local = slot & (half - 1)
    pp = lax.shift_right_logical(local, log_of(grid))
    qq = local & (grid - 1)
    mid = lax.shift_right_logical(grid, 1)
    first = pp == 0
    special = first & ((qq == 0) | (qq == mid))
    p = jnp.where(first & (qq >= mid), mid, pp)
    q = jnp.where(first & (qq == mid), 0, qq)
    pm = jnp.where(special, p, (grid - p) & (grid - 1))
    qm = jnp.where(special, mid, (grid - q) & (grid - 1))
    return 2 * (slot - local), p, q, special, pm, qm


def build_tables(grid_ref, keep_ref, at, k1, k3, nm, nb):
    rows = at.shape[1]
    slots = rows // 2
    unit = slots // NBLK
    vals = [grid_ref[j] for j in range(NBLK)]
    lane = lax.broadcasted_iota(jnp.int32, (8, rows), 1)
    sub = lax.broadcasted_iota(jnp.int32, (8, rows), 0)
    gc = pick(vals, lane // (2 * unit))
    span = gc * gc
    start_c = lane & ~(span - 1)
    local = lane & (span - 1)
    p_c = lax.shift_right_logical(local, log_of(gc))
    q_c = local & (gc - 1)
    ginv = 1.0 / gc.astype(F32)
    bcs = []
    for j in range(4):
        q_r = (sub + 8 * j) & (gc - 1)
        bcs.append(cos_sin(((q_r * q_c) & (gc - 1)).astype(F32) * ginv))

    def two(x):
        return jnp.concatenate([x, x], 0)

    gc2, start2, p2, q2, ginv2, sub2 = two(gc), two(start_c), two(p_c), two(q_c), two(ginv), lax.broadcasted_iota(jnp.int32, (16, rows), 0)

    def step(i, carry):
        slot = (sub + 8 * i) * 8
        gb = jnp.where(sub < 4, grid_ref[2 * i], grid_ref[2 * i + 1])
        half = gb * gb // 2
        loc = slot & (half - 1)
        p_b = lax.shift_right_logical(loc, log_of(gb))
        ac, as_ = cos_sin(((p_b * p_c) & (gc - 1)).astype(F32) * ginv)
        same = jnp.where(2 * (slot - loc) == start_c, ginv, 0.0)
        ac = ac * same
        as_ = as_ * same
        for j in range(0, 8, 2):
            re, im = [], []
            for d in range(2):
                bc, bs = bcs[(j + d) % 4]
                a1 = ac[j + d : j + d + 1, :]
                a2 = as_[j + d : j + d + 1, :]
                re.append(a1 * bc - a2 * bs)
                im.append(-(a2 * bc + a1 * bs))
            s0 = pl.multiple_of(i * 64 + j * 8, 16)
            at[pl.ds(s0, 16), :] = jnp.concatenate(re, 0).astype(BF)
            at[pl.ds(slots + s0, 16), :] = jnp.concatenate(im, 0).astype(BF)
            g = grid_ref[2 * i + j // 4]
            first = (s0 & (g * g // 2 - 1)) < g

            @pl.when(first)
            def _():
                gv = jnp.full((16, rows), 0, jnp.int32) + g
                start, p, q, special, pm, qm = slot_of(sub2 + s0, gv)
                live = jnp.where(start == start2, ginv2, 0.0)
                t = ((p * p2 + q * q2) & (gc2 - 1)).astype(F32) * ginv2
                tm = ((pm * p2 + qm * q2) & (gc2 - 1)).astype(F32) * ginv2
                quarter = jnp.where(t >= 0.75, t - 0.75, t + 0.25)
                at[pl.ds(s0, 16), :] = (cos_of(t) * live).astype(BF)
                at[pl.ds(slots + s0, 16), :] = (cos_of(jnp.where(special, tm, quarter)) * live).astype(BF)

        return carry

    lax.fori_loop(0, slots // 64, step, 0)

    def mask(i, carry):
        slot = lax.broadcasted_iota(jnp.int32, (unit, 128), 0) + unit * i
        g = jnp.full((unit, 128), 0, jnp.int32) + grid_ref[i]
        _, p, q, special, pm, qm = slot_of(slot, g)
        k = jnp.where(g == 8, keep_ref[0], jnp.where(g == 16, keep_ref[1], keep_ref[2]))
        plus = jnp.where((p < k) & (q < k), 1.0, 0.0)
        minus = jnp.where((pm < k) & (qm < k), 1.0, 0.0)
        n = jnp.where(special, 0.0, 1.0)
        dst = pl.ds(pl.multiple_of(i * unit, unit), unit)
        nm[dst, :] = n.astype(BF)
        nb[dst, :] = (1.0 - n).astype(BF)
        for sign, (m, im) in enumerate(((plus, plus * n), (minus, -minus * n))):
            for ref, f in ((k1, 1.0), (k3, 0.05 * 0.0025)):
                ref[sign, dst, 0:128] = (m * f).astype(BF)
                ref[sign, dst, 128:256] = (im * f).astype(BF)
        return carry

    lax.fori_loop(0, NBLK, mask, 0)


def build_mix(w_ref, out_ref):
    i = lax.broadcasted_iota(jnp.int32, (64, 128), 0)
    j = lax.broadcasted_iota(jnp.int32, (64, 128), 1)
    dup = jnp.where((j & 63) == i, 1.0, 0.0).astype(BF)
    r = lax.broadcasted_iota(jnp.int32, (512, 128), 0)
    c = lax.broadcasted_iota(jnp.int32, (512, 128), 1)
    diag = ((r // 64) & 1) == (c // 64)
    for layer in range(LAYERS):
        re = jnp.where(diag, nn(w_ref[layer, 0], dup), 0.0)
        im = jnp.where(diag, nn(w_ref[layer, 1], dup), 0.0)
        for g in range(4):
            a = re[g * 128 : (g + 1) * 128].astype(BF)
            b = im[g * 128 : (g + 1) * 128]
            out_ref[layer, g, 0:128, 0:128] = a
            out_ref[layer, g, 128:256, 128:256] = a
            out_ref[layer, g, 0:128, 128:256] = b.astype(BF)
            out_ref[layer, g, 128:256, 0:128] = (-b).astype(BF)


def min_layer(layer):
    return layer if isinstance(layer, int) else jnp.minimum(layer, LAYERS - 1)


def fold(x):
    return jnp.sum(x.reshape(x.shape[0] // 8, 8, x.shape[1]), 0)


def kernel(
    grid_ref, keep_ref, core_ref, x_hbm, cot_hbm,
    n1g, n1b, w1_hbm, b1, w2_hbm, b2, n2g, n2b, fc1_hbm, fb1, fc2_hbm, fb2,
    out_hbm, xg_hbm, m0, m1, m2, t0, t1, t2,
    x_ref, cot_ref, w1, w2, fc1, fc2, out_ref, grads_ref, sems,
    at, st, k1, k3, nm, nb, w1g, w2g,
    xh1, rs1, hu, ul, z, o, da, ds, pq, xh2, rs2, v, act, dp,
    gmid, acc,
):
    g_s, gy, gm, xg_ref = hu, ul, x_ref, cot_ref

    def copy(k, src, dst):
        return pltpu.make_async_copy(src, dst, sems.at[k])

    loads = [
        copy(k, src, dst)
        for k, (src, dst) in enumerate(
            ((x_hbm, x_ref), (w1_hbm, w1), (w2_hbm, w2), (fc1_hbm, fc1), (fc2_hbm, fc2), (cot_hbm, cot_ref))
        )
    ]
    for c in loads:
        c.start()
    rows = x_ref.shape[0]
    slots = rows // 2
    tiles = rows // RT
    stiles = slots // ST
    build_tables(grid_ref, keep_ref, at, k1, k3, nm, nb)
    for i in range(4):
        st[:, i * 256 : (i + 1) * 256] = at[i * 256 : (i + 1) * 256, :].T
    loads[1].wait()
    loads[2].wait()
    build_mix(w1, w1g)
    build_mix(w2, w2g)
    acc[...] = jnp.zeros_like(acc)

    def tile(i):
        return slice(i * RT, (i + 1) * RT)

    def chunk(i, j):
        return slice(i * RT + j * CH, i * RT + (j + 1) * CH)

    def add_to(layer, k, x):
        acc[layer, k] = acc[layer, k] + fold(x)

    def norm1(layer, dst, h):
        mean = jnp.mean(h, -1, keepdims=True)
        cent = h - mean
        rstd = lax.rsqrt(jnp.mean(cent * cent, -1, keepdims=True) + 1e-05)
        xh = cent * rstd
        u = xh * n1g[pl.ds(min_layer(layer), 1), :] + n1b[pl.ds(min_layer(layer), 1), :]
        xh1[layer, dst, :] = xh.astype(BF)
        rs1[layer, dst, :] = jnp.broadcast_to(rstd, (CH, 128))
        ul[dst, :] = u.astype(BF)
        hu[dst, :] = h + u

    def enter():
        for i in range(tiles):
            for j in range(RT // CH):
                dst = chunk(i, j)
                norm1(0, dst, x_ref[dst, :].astype(F32))

    def block(f):
        f()

    loads[0].wait()
    enter()
    loads[3].wait()
    loads[4].wait()
    loads[5].wait()

    def lanes(x, times):
        return jnp.concatenate([x] * times, 1)

    def analyse(layer, t, p):
        sl = slice(t * ST, (t + 1) * ST)
        h = p % 2
        hs = slice(h * 256, (h + 1) * 256)
        if p < 2:
            zr = nn(at[sl, :], ul[:, hs]).astype(BF)
            for e in range(2):
                c0 = (2 * h + e) * 256
                z[layer, 0, sl, c0 : c0 + 128] = zr[:, e * 128 : e * 128 + 128]
        else:
            n, nbar = nm[sl, :], nb[sl, :]
            zi = nn(at[slots + t * ST : slots + (t + 1) * ST, :], ul[:, hs]).astype(BF)
            for e in range(2):
                c0 = (2 * h + e) * 256
                zie = zi[:, e * 128 : e * 128 + 128]
                zin = zie * n
                z[layer, 0, sl, c0 + 128 : c0 + 256] = zin
                z[layer, 1, sl, c0 + 128 : c0 + 256] = -zin
                z[layer, 1, sl, c0 : c0 + 128] = z[layer, 0, sl, c0 : c0 + 128] * n + zie * nbar

    def both(ref, layer, sl, gl):
        return ref[layer, :, sl, gl].reshape(2 * ST, 256)

    def put(ref, layer, sl, gl, x, c=None):
        if c is None:
            ref[layer, :, sl, gl] = x.reshape(2, ST, 256)
        else:
            r0 = sl.start + c % ST
            ref[layer, c // ST, r0 : r0 + CE, gl] = x

    def combine(dst, sl, cs, x, signed):
        n, nbar = nm[sl, :], nb[sl, :]
        rp, ip = x[0:ST, 0:128], x[0:ST, 128:256]
        rm, im = x[ST : 2 * ST, 0:128], x[ST : 2 * ST, 128:256]
        dst[sl, cs] = rp + rm * n
        q = ip + im if signed else (ip - im) * n
        dst[slots + sl.start : slots + sl.stop, cs] = q + rm * nbar

    def mix_forward(layer):
        def cut(k):
            t, g = k // 4, k % 4
            return slice(t * ST, (t + 1) * ST), slice(g * 128, (g + 1) * 128), slice(g * 256, (g + 1) * 256), g

        def dot_a(k):
            sl, cs, gl, g = cut(k)
            return nn(both(z, layer, sl, gl), w1g[layer, g])

        def gelu_a(k, a):
            sl, cs, gl, g = cut(k)
            bias = lanes2(b1[layer, 0:1, cs], b1[layer, 1:2, cs])
            ys = []
            for c in range(0, 2 * ST, CE):
                og, dag = gelu_split(a[c : c + CE] + bias)
                ys.append(og)
                put(o, layer, sl, gl, og, c)
                put(da, layer, sl, gl, dag, c)
            return nn(jnp.concatenate(ys, 0), w2g[layer, g])

        def shrink_e(k, ew):
            sl, cs, gl, g = cut(k)
            bias = lanes2(b2[layer, 0:1, cs], b2[layer, 1:2, cs])
            for c in range(0, ST, CE):
                rs = slice(sl.start + c, sl.start + c + CE)
                ss = []
                for sign in range(2):
                    e = ew[sign * ST + c : sign * ST + c + CE] + bias
                    r = lax.rsqrt(e * e + 0.0025)
                    c1 = k1[sign, rs, :]
                    ss.append((e - 0.05 * (e * r)).astype(BF) * c1)
                    r = r.astype(BF)
                    ds[layer, sign, rs, gl] = c1 - k3[sign, rs, :] * (r * r * r)
                n, nbar = nm[rs, :], nb[rs, :]
                rm = ss[1][:, 0:128]
                pq[rs, cs] = ss[0][:, 0:128] + rm * n
                pq[slots + rs.start : slots + rs.stop, cs] = ss[0][:, 128:256] + ss[1][:, 128:256] + rm * nbar

        steps = stiles * 4
        for p in range(4):
            analyse(layer, 0, p)
        a = dot_a(0)
        e_prev = None
        for k in range(steps):
            t, g = k // 4, k % 4
            if t + 1 < stiles:
                analyse(layer, t + 1, g)
            nxt = dot_a(k + 1) if k + 1 < steps else None
            e = gelu_a(k, a)
            if e_prev is not None:
                shrink_e(k - 1, e_prev)
            a, e_prev = nxt, e
        shrink_e(steps - 1, e_prev)

    def ff_forward(layer):
        def norm2(i, y):
            for j in range(RT // CH):
                cd = chunk(i, j)
                mid = y[j * CH : (j + 1) * CH] + hu[cd, :]
                mean = jnp.mean(mid, -1, keepdims=True)
                cent = mid - mean
                rstd = lax.rsqrt(jnp.mean(cent * cent, -1, keepdims=True) + 1e-05)
                xh = cent * rstd
                xh2[layer, cd, :] = xh.astype(BF)
                rs2[layer, cd, :] = jnp.broadcast_to(rstd, (CH, 128))
                v[layer, cd, :] = (xh * n2g[pl.ds(layer, 1), :] + n2b[pl.ds(layer, 1), :]).astype(BF)
                hu[cd, :] = mid
            return nn(v[layer, tile(i), :], fc1[layer])

        def gelu_f(i, pre):
            for j in range(0, RT, CF):
                cd = slice(i * RT + j, i * RT + j + CF)
                act[layer, cd, :], dp[layer, cd, :] = gelu_split(pre[j : j + CF] + fb1[pl.ds(layer, 1), :])
            return nn(act[layer, tile(i), :], fc2[layer])

        def leave(i, br):
            for j in range(RT // CH):
                cd = chunk(i, j)
                h = hu[cd, :] + (br[j * CH : (j + 1) * CH] + fb2[pl.ds(layer, 1), :])
                out_ref[cd, :] = h.astype(BF)
                norm1(layer + 1, cd, h)

        def dot_y(i):
            return nn(st[tile(i), :], pq[...])

        y = dot_y(0)
        pre = None
        for i in range(tiles + 1):
            nxt = dot_y(i + 1) if i + 1 < tiles else None
            br = gelu_f(i - 1, pre) if i >= 1 else None
            pre = norm2(i, y) if i < tiles else None
            if i >= 1:
                leave(i - 1, br)
            y = nxt

    @partial(lax.fori_loop, 0, LAYERS, init_val=0)
    def _(layer, carry):
        block(lambda: mix_forward(layer))
        block(lambda: ff_forward(layer))
        return carry

    out_copy = copy(6, out_ref, out_hbm)
    out_copy.start()
    for i in range(tiles):
        g_s[tile(i), :] = cot_ref[tile(i), :].astype(F32)

    def norm_back(gv, xh, rstd, gain):
        t = gv * gain
        mt = jnp.mean(t, -1, keepdims=True)
        mx = jnp.mean(t * xh, -1, keepdims=True)
        return rstd * (t - mt - xh * mx)

    def with_sums(left, right):
        ones = jnp.ones((16, left.shape[0]), BF)
        return nn(jnp.concatenate([left.T, ones], 0), right)

    def ff_backward(layer):
        def load_g(rs):
            return g_s[rs, :]

        def dot_a(i):
            dst = tile(i)
            gmt = g_s[dst, :].astype(BF)
            gm[dst, :] = gmt
            return nt(gmt, fc2[layer])

        def mul(i, ga_):
            dst = tile(i)
            dp[layer, dst, :] = ga_.astype(BF) * dp[layer, dst, :]
            return nt(dp[layer, dst, :], fc1[layer])

        def leave(i, gv):
            for j in range(RT // CH):
                cd = chunk(i, j)
                gvc = gv[j * CH : (j + 1) * CH]
                xh = xh2[layer, cd, :].astype(F32)
                add_to(layer, 6, gvc * xh)
                add_to(layer, 7, gvc)
                rstd = lanes(rs2[layer, cd, :], 4)
                gmc = load_g(cd) + norm_back(gvc, xh, rstd, n2g[pl.ds(layer, 1), :])
                gmid[cd, :] = gmc
                gy[cd, :] = gmc.astype(BF)

        cur = dot_a(0)
        prev = None
        for i in range(tiles + 1):
            nxt = dot_a(i + 1) if i + 1 < tiles else None
            gv = mul(i, cur) if i < tiles else None
            if i >= 1:
                leave(i - 1, prev)
            cur, prev = nxt, gv
        base = pl.multiple_of((layer ^ core_ref[0]) * PER, PER)
        for left, right, off, vec in ((v, dp[layer], 0, 8), (act, gm[...], 512, 9)):
            for h in range(2):
                hs = slice(h * 256, (h + 1) * 256)
                r = base + off + h * 256
                if h == 0:
                    p = with_sums(left[layer, :, hs], right)
                    acc[layer, vec, 0:1, :] = p[256:257]
                else:
                    p = tn(left[layer, :, hs], right)
                grads_ref[pl.ds(r, 256), :] = p[0:256].astype(BF)

    def mix_backward(layer):
        def cut(k):
            t, g = k // 4, k % 4
            return slice(t * ST, (t + 1) * ST), slice(g * 128, (g + 1) * 128), slice(g * 256, (g + 1) * 256), g

        def spectrum(t, h):
            hs = slice(h * 256, (h + 1) * 256)
            gr = nn(at[t * ST : (t + 1) * ST, :], gy[:, hs]).astype(BF)
            gi = nn(at[slots + t * ST : slots + (t + 1) * ST, :], gy[:, hs]).astype(BF)
            return gr, gi

        def dot_o(k, gr, gi):
            sl, cs, gl, g = cut(k)
            n, nbar = nm[sl, :], nb[sl, :]
            hs = slice(g % 2 * 128, g % 2 * 128 + 128)
            grc, gic = gr[:, hs], gi[:, hs]
            ds[layer, 0, sl, gl] = lanes2(grc, gic) * ds[layer, 0, sl, gl]
            ds[layer, 1, sl, gl] = lanes2(grc * n + gic * nbar, gic) * ds[layer, 1, sl, gl]
            return nt(both(ds, layer, sl, gl), w2g[layer, g])

        def dot_z(k, go):
            sl, cs, gl, g = cut(k)
            put(da, layer, sl, gl, go.astype(BF) * both(da, layer, sl, gl))
            return nt(both(da, layer, sl, gl), w1g[layer, g])

        def leave(k, gz):
            sl, cs, gl, g = cut(k)
            combine(pq, sl, cs, gz.astype(BF), False)

        steps = stiles * 4
        sp = {0: spectrum(0, 0)}
        go = dot_o(0, *sp[0])
        prev = None
        for k in range(steps + 1):
            if k % 2 == 0 and k + 2 < steps:
                sp[k // 2 + 1] = spectrum((k + 2) // 4, (k + 2) // 2 % 2)
            nxt = dot_o(k + 1, *sp[(k + 1) // 2]) if k + 1 < steps else None
            gz = dot_z(k, go) if k < steps else None
            if k >= 1:
                leave(k - 1, prev)
            go, prev = nxt, gz
        base = pl.multiple_of((layer ^ core_ref[0]) * PER, PER) + 1024
        low = lax.broadcasted_iota(jnp.int32, (64, 128), 1) < 64
        for left, right, off, vec in ((o, ds, base + 128, 4), (z, da, base, 2)):
            for g in range(4):
                cs = slice(g * 128, (g + 1) * 128)
                gl = slice(g * 256, (g + 1) * 256)
                lf = left[layer, :, :, gl].reshape(rows, 256)
                rt = right[layer, :, :, gl].reshape(rows, 256)
                p = with_sums(lf, rt)
                acc[layer, vec, 0:1, cs] = p[256:257, 0:128]
                acc[layer, vec + 1, 0:1, cs] = p[256:257, 128:256]
                re = p[0:128, 0:128] + p[128:256, 128:256]
                im = p[0:128, 128:256] - p[128:256, 0:128]
                grads_ref[pl.ds(off, 64), cs] = jnp.where(low, re[0:64], re[64:128]).astype(BF)
                grads_ref[pl.ds(off + 64, 64), cs] = jnp.where(low, im[0:64], im[64:128]).astype(BF)

    def in_backward(layer):
        def leave(i, y):
            for j in range(RT // CH):
                cd = chunk(i, j)
                gmc = gmid[cd, :]
                gu = y[j * CH : (j + 1) * CH] + gmc
                xh = xh1[layer, cd, :].astype(F32)
                add_to(layer, 0, gu * xh)
                add_to(layer, 1, gu)
                rstd = lanes(rs1[layer, cd, :], 4)
                gh = gmc + norm_back(gu, xh, rstd, n1g[pl.ds(min_layer(layer), 1), :])
                xg_ref[cd, :] = gh.astype(BF)
                g_s[cd, :] = gh

        y = nn(st[tile(0), :], pq[...])
        for i in range(tiles):
            nxt = nn(st[tile(i + 1), :], pq[...]) if i + 1 < tiles else None
            leave(i, y)
            y = nxt

    @partial(lax.fori_loop, 0, LAYERS, init_val=0)
    def _(step, carry):
        layer = LAYERS - 1 - step
        block(lambda: ff_backward(layer))
        block(lambda: mix_backward(layer))
        block(lambda: in_backward(layer))
        return carry

    def vectors(layer):
        t = jnp.sum(acc[layer], 1)
        t = jnp.concatenate([t, jnp.zeros((PER - 1290, 512), F32)], 0)
        grads_ref[pl.ds(pl.multiple_of((layer ^ core_ref[0]) * PER, PER) + 1280, PER - 1280), :] = t.astype(BF)

    vectors(1)
    sends = [
        copy(8 + k, grads_ref.at[pl.ds(row, PER // 3)], dst)
        for k, (row, dst) in enumerate(
            (((3 * half + c) * (PER // 3), dst) for half, refs in ((1, (t0, t1, t2)), (0, (m0, m1, m2))) for c, dst in enumerate(refs))
        )
    ]
    xg_copy = copy(7, xg_ref, xg_hbm)
    vectors(0)
    for c in sends:
        c.start()
    xg_copy.start()
    out_copy.wait()
    for c in sends:
        c.wait()
    xg_copy.wait()


def lanes2(a, b):
    return jnp.concatenate([a, b], 1)


def local_step(core, x_in, cotangent, block_grid, keep_modes, n1g, n1b, w1, b1, w2, b2, n2g, n2b, fc1, fb1, fc2, fb2):
    rows, d = x_in.shape
    slots = rows // 2
    vm = pl.BlockSpec(memory_space=pltpu.VMEM)
    sm = pl.BlockSpec(memory_space=pltpu.SMEM)
    hbm = pl.BlockSpec(memory_space=pl.ANY)
    w1r = w1.reshape(LAYERS, 2, 512, 64)
    w2r = w2.reshape(LAYERS, 2, 512, 64)
    scratch = [
        pltpu.VMEM((rows, d), BF), pltpu.VMEM((rows, d), BF),
        pltpu.VMEM(w1r.shape, BF), pltpu.VMEM(w2r.shape, BF), pltpu.VMEM(fc1.shape, BF), pltpu.VMEM(fc2.shape, BF),
        pltpu.VMEM((rows, d), BF), pltpu.VMEM((LAYERS * PER, d), BF),
        pltpu.SemaphoreType.DMA((14,)),
        pltpu.VMEM((rows, rows), BF), pltpu.VMEM((rows, rows), BF),
        pltpu.VMEM((2, slots, 256), BF), pltpu.VMEM((2, slots, 256), BF),
        pltpu.VMEM((slots, 128), BF), pltpu.VMEM((slots, 128), BF),
        pltpu.VMEM((LAYERS, 4, 256, 256), BF), pltpu.VMEM((LAYERS, 4, 256, 256), BF),
        pltpu.VMEM((LAYERS + 1, rows, d), BF), pltpu.VMEM((LAYERS + 1, rows, 128), F32),
        pltpu.VMEM((rows, d), F32), pltpu.VMEM((rows, d), BF),
        pltpu.VMEM((LAYERS, 2, slots, 2 * d), BF), pltpu.VMEM((LAYERS, 2, slots, 2 * d), BF),
        pltpu.VMEM((LAYERS, 2, slots, 2 * d), BF), pltpu.VMEM((LAYERS, 2, slots, 2 * d), BF),
        pltpu.VMEM((rows, d), BF),
        pltpu.VMEM((LAYERS, rows, d), BF), pltpu.VMEM((LAYERS, rows, 128), F32),
        pltpu.VMEM((LAYERS, rows, d), BF), pltpu.VMEM((LAYERS, rows, d), BF), pltpu.VMEM((LAYERS, rows, d), BF),
        pltpu.VMEM((rows, d), F32),
        pltpu.VMEM((LAYERS, 10, 8, d), F32),
    ]
    return pl.pallas_call(
        kernel,
        out_shape=(
            jax.ShapeDtypeStruct((rows, d), BF),
            jax.ShapeDtypeStruct((rows, d), BF),
        )
        + (jax.ShapeDtypeStruct((PER // 3, d), BF),) * 6,
        in_specs=[sm, sm, sm, hbm, hbm, vm, vm, hbm, vm, hbm, vm, vm, vm, hbm, vm, hbm, vm],
        out_specs=(hbm,) * 8,
        scratch_shapes=scratch,
        compiler_params=pltpu.CompilerParams(vmem_limit_bytes=58 * 1024 * 1024),
        name="slab_step",
    )(block_grid, keep_modes, core, x_in, cotangent, n1g, n1b, w1r, b1, w2r, b2, n2g, n2b, fc1, fb1, fc2, fb2)


AXES = ("dp", "modes")


def spread_layer(layer, parts, outs, bufs, sems):
    fc1, fc2, w1, w2 = bufs
    p0, p1, p2 = parts
    n = PER // 3
    copies = [pltpu.make_async_copy(buf, out.at[layer], sems.at[k]) for k, (buf, out) in enumerate(zip(bufs, outs))]
    fc1[0:n, :] = p0[...].astype(F32)
    fc1[n:512, :] = p1[0 : 512 - n, :].astype(F32)
    copies[0].start()
    fc2[0 : 2 * n - 512, :] = p1[512 - n : n, :].astype(F32)
    fc2[2 * n - 512 : 512, :] = p2[0 : 1024 - 2 * n, :].astype(F32)
    copies[1].start()
    for k, (ref, base) in enumerate(((w1, 1024 - 2 * n), (w2, 1152 - 2 * n))):
        for part in range(2):
            block = p2[base + part * 64 : base + part * 64 + 64, :].astype(F32)
            for j in range(8):
                ref[part, j] = block[:, j * 64 : j * 64 + 64]
        copies[2 + k].start()
    return copies


def spread_mine(core_ref, a0, a1, a2, fc1_out, fc2_out, w1_out, w2_out, fc1, fc2, w1, w2, sems):
    for c in spread_layer(core_ref[0], (a0, a1, a2), (fc1_out, fc2_out, w1_out, w2_out), (fc1, fc2, w1, w2), sems):
        c.wait()


def spread_other(
    core_ref, a0, a1, a2, c0, c1, c2, fc1_in, fc2_in, w1_in, w2_in,
    fc1_out, fc2_out, w1_out, w2_out, n1g, n1b, b1, b2, n2g, n2b, fb1, fb2, fc1, fc2, w1, w2, sems,
):
    copies = spread_layer(1 - core_ref[0], (c0, c1, c2), (fc1_out, fc2_out, w1_out, w2_out), (fc1, fc2, w1, w2), sems)
    row = 1280 - 2 * (PER // 3)
    here = a2[row : row + 16, :].astype(F32)
    there = c2[row : row + 16, :].astype(F32)
    for layer in range(LAYERS):
        vec = jnp.where(core_ref[0] == layer, here, there)
        for row, ref in ((0, n1g), (1, n1b), (6, n2g), (7, n2b), (8, fb1), (9, fb2)):
            ref[layer : layer + 1, :] = vec[row : row + 1]
        b1[layer] = vec[2:4]
        b2[layer] = vec[4:6]
    for c in copies:
        c.wait()


def unpack_shapes(d):
    mix = jax.ShapeDtypeStruct((LAYERS, 2, 8, 64, 64), F32)
    full = jax.ShapeDtypeStruct((LAYERS, d, d), F32)
    big = (full, full, mix, mix)
    scratch = [pltpu.VMEM(s.shape[1:], F32) for s in big] + [pltpu.SemaphoreType.DMA((4,))]
    return big, scratch


def unpack_mine(core, mine, d):
    vm = pl.BlockSpec(memory_space=pltpu.VMEM)
    hbm = pl.BlockSpec(memory_space=pl.ANY)
    big, scratch = unpack_shapes(d)
    return pl.pallas_call(
        spread_mine,
        out_shape=big,
        in_specs=[pl.BlockSpec(memory_space=pltpu.SMEM), vm, vm, vm],
        out_specs=(hbm,) * 4,
        scratch_shapes=scratch,
        compiler_params=pltpu.CompilerParams(vmem_limit_bytes=16 * 1024 * 1024),
        cost_estimate=pl.CostEstimate(flops=1 << 20, bytes_accessed=4 << 20, transcendentals=0),
        name="spread_mine",
    )(core, *mine)


def unpack(core, mine, other, d, big_in=None):
    vm = pl.BlockSpec(memory_space=pltpu.VMEM)
    hbm = pl.BlockSpec(memory_space=pl.ANY)
    big, scratch = unpack_shapes(d)
    vec = jax.ShapeDtypeStruct((LAYERS, d), F32)
    pair = jax.ShapeDtypeStruct((LAYERS, 2, d), F32)
    if big_in is None:
        big_in = unpack_mine(core, mine, d)
    fc1, fc2, w1, w2, n1g, n1b, b1, b2, n2g, n2b, fb1, fb2 = pl.pallas_call(
        spread_other,
        out_shape=big + (vec, vec, pair, pair, vec, vec, vec, vec),
        in_specs=[pl.BlockSpec(memory_space=pltpu.SMEM)] + [vm] * 6 + [hbm] * 4,
        out_specs=(hbm,) * 4 + (vm,) * 8,
        scratch_shapes=scratch,
        input_output_aliases={7: 0, 8: 1, 9: 2, 10: 3},
        compiler_params=pltpu.CompilerParams(vmem_limit_bytes=16 * 1024 * 1024),
        name="spread_other",
    )(core, *mine, *other, *big_in)
    return n1g, n1b, w1, b1, w2, b2, n2g, n2b, fc1, fb1, fc2, fb2


def exchange(a, bit, count):
    return lax.ppermute(a, AXES, [(i, i ^ bit) for i in range(count)])


def add(a, b):
    return (a.astype(F32) + b.astype(F32)).astype(BF)


def all_sum(mine, other, count):
    me = lax.axis_index(AXES)
    top = count // 2
    bits = [1 << k for k in range(top.bit_length() - 1)]
    orders = [[bits[(c + k) % 3] for k in range(3)] for c in range(3)]
    gots = [exchange(t, top, count) for t in other]
    parts = [add(m, got) for m, got in zip(mine, gots)]
    for k in range(3):
        moved = []
        for c in range(3):
            n = parts[c].shape[0] // 2
            high = (me & orders[c][k]) != 0
            keep = jnp.where(high, parts[c][n:], parts[c][:n])
            send = jnp.where(high, parts[c][:n], parts[c][n:])
            moved.append((keep, exchange(send, orders[c][k], count)))
        parts = [add(keep, got) for keep, got in moved]
    for bit in bits[3:]:
        parts = [add(p, exchange(p, bit, count)) for p in parts]
    for k in reversed(range(3)):
        gots = [exchange(parts[c], orders[c][k], count) for c in range(3)]
        for c in range(3):
            high = (me & orders[c][k]) != 0
            low_part = jnp.where(high, gots[c], parts[c])
            high_part = jnp.where(high, parts[c], gots[c])
            parts[c] = jnp.concatenate([low_part, high_part])
    return parts, [exchange(p, top, count) for p in parts]


def solution(mesh):
    count = mesh.shape["dp"] * mesh.shape["modes"]

    def on_device(*args):
        core = lax.axis_index("dp").astype(jnp.int32).reshape(1)
        out, x_grad, *parts = local_step(core, *args)
        mine, other = all_sum(parts[:3], parts[3:], count)
        return (out, x_grad) + tuple(unpack(core, mine, other, out.shape[1]))

    rows = P(AXES, None)
    return jax.shard_map(
        on_device,
        mesh=mesh,
        in_specs=(rows, rows, P(AXES)) + (P(),) * 13,
        out_specs=(rows, rows) + (P(),) * 12,
        check_vma=False,
    )
```

```python
import math
from functools import partial

import jax
import jax.numpy as jnp
from jax import lax
from jax.experimental import pallas as pl
from jax.experimental.pallas import tpu as pltpu
from jax.sharding import PartitionSpec as P

LAYERS = 2
NBLK = 16
F32 = jnp.float32
BF = jnp.bfloat16
C0 = math.sqrt(2.0 / math.pi)
C1 = 0.044715 * C0
PER = 1344
RT = 256
ST = 256
NH = 512
CH = 64
CE = 32
CF = 16


def nn(a, b):
    return jnp.dot(a, b, preferred_element_type=F32)


def nt(a, b):
    return lax.dot_general(a, b, (((1,), (1,)), ((), ())), preferred_element_type=F32)


def tn(a, b):
    return lax.dot_general(a, b, (((0,), (0,)), ((), ())), preferred_element_type=F32)


def gelu_pair(x):
    x2 = x * x
    p = 0.5 + 0.5 * jnp.tanh(x * (C0 + C1 * x2))
    y = x * p
    return y, p + y * (1.0 - p) * (2.0 * C0 + (6.0 * C1) * x2)


def gelu_split(x):
    p = 0.5 + 0.5 * jnp.tanh(x * (C0 + C1 * (x * x)))
    y = (x * p).astype(BF)
    xb, pb, qb = x.astype(BF), p.astype(BF), (1.0 - p).astype(BF)
    return y, pb + y * qb * (2.0 * C0 + (6.0 * C1) * (xb * xb))


def cos_of(t):
    x = t - 0.5
    w = (2.0 * math.pi * x) ** 2
    c = jnp.full_like(w, 1.0 / math.factorial(16))
    for k in range(7, -1, -1):
        c = c * w + (-1.0) ** k / math.factorial(2 * k)
    return -c


def cos_sin(t):
    x = t - 0.5
    w = (2.0 * math.pi * x) ** 2
    c = jnp.full_like(w, 1.0 / math.factorial(16))
    s = jnp.full_like(w, -1.0 / math.factorial(15))
    for k in range(7, -1, -1):
        c = c * w + (-1.0) ** k / math.factorial(2 * k)
        if k < 7:
            s = s * w + (-1.0) ** k / math.factorial(2 * k + 1)
    return -c, -s * (2.0 * math.pi * x)


def pick(values, block):
    out = jnp.zeros(block.shape, jnp.int32)
    for j in range(NBLK):
        out = jnp.where(block == j, values[j], out)
    return out


def log_of(grid):
    return jnp.where(grid == 8, 3, jnp.where(grid == 16, 4, 5))


def slot_of(slot, grid):
    half = grid * grid // 2
    local = slot & (half - 1)
    pp = lax.shift_right_logical(local, log_of(grid))
    qq = local & (grid - 1)
    mid = lax.shift_right_logical(grid, 1)
    first = pp == 0
    special = first & ((qq == 0) | (qq == mid))
    p = jnp.where(first & (qq >= mid), mid, pp)
    q = jnp.where(first & (qq == mid), 0, qq)
    pm = jnp.where(special, p, (grid - p) & (grid - 1))
    qm = jnp.where(special, mid, (grid - q) & (grid - 1))
    return 2 * (slot - local), p, q, special, pm, qm


def build_tables(grid_ref, keep_ref, at, k1, k3, nm, nb):
    rows = at.shape[1]
    slots = rows // 2
    unit = slots // NBLK
    vals = [grid_ref[j] for j in range(NBLK)]
    lane = lax.broadcasted_iota(jnp.int32, (8, rows), 1)
    sub = lax.broadcasted_iota(jnp.int32, (8, rows), 0)
    gc = pick(vals, lane // (2 * unit))
    span = gc * gc
    start_c = lane & ~(span - 1)
    local = lane & (span - 1)
    p_c = lax.shift_right_logical(local, log_of(gc))
    q_c = local & (gc - 1)
    ginv = 1.0 / gc.astype(F32)
    bcs = []
    for j in range(4):
        q_r = (sub + 8 * j) & (gc - 1)
        bcs.append(cos_sin(((q_r * q_c) & (gc - 1)).astype(F32) * ginv))

    def two(x):
        return jnp.concatenate([x, x], 0)

    gc2, start2, p2, q2, ginv2, sub2 = two(gc), two(start_c), two(p_c), two(q_c), two(ginv), lax.broadcasted_iota(jnp.int32, (16, rows), 0)

    def step(i, carry):
        slot = (sub + 8 * i) * 8
        gb = jnp.where(sub < 4, grid_ref[2 * i], grid_ref[2 * i + 1])
        half = gb * gb // 2
        loc = slot & (half - 1)
        p_b = lax.shift_right_logical(loc, log_of(gb))
        ac, as_ = cos_sin(((p_b * p_c) & (gc - 1)).astype(F32) * ginv)
        same = jnp.where(2 * (slot - loc) == start_c, ginv, 0.0)
        ac = ac * same
        as_ = as_ * same
        for j in range(0, 8, 2):
            re, im = [], []
            for d in range(2):
                bc, bs = bcs[(j + d) % 4]
                a1 = ac[j + d : j + d + 1, :]
                a2 = as_[j + d : j + d + 1, :]
                re.append(a1 * bc - a2 * bs)
                im.append(-(a2 * bc + a1 * bs))
            s0 = pl.multiple_of(i * 64 + j * 8, 16)
            at[pl.ds(s0, 16), :] = jnp.concatenate(re, 0).astype(BF)
            at[pl.ds(slots + s0, 16), :] = jnp.concatenate(im, 0).astype(BF)
            g = grid_ref[2 * i + j // 4]
            first = (s0 & (g * g // 2 - 1)) < g

            @pl.when(first)
            def _():
                gv = jnp.full((16, rows), 0, jnp.int32) + g
                start, p, q, special, pm, qm = slot_of(sub2 + s0, gv)
                live = jnp.where(start == start2, ginv2, 0.0)
                t = ((p * p2 + q * q2) & (gc2 - 1)).astype(F32) * ginv2
                tm = ((pm * p2 + qm * q2) & (gc2 - 1)).astype(F32) * ginv2
                quarter = jnp.where(t >= 0.75, t - 0.75, t + 0.25)
                at[pl.ds(s0, 16), :] = (cos_of(t) * live).astype(BF)
                at[pl.ds(slots + s0, 16), :] = (cos_of(jnp.where(special, tm, quarter)) * live).astype(BF)

        return carry

    lax.fori_loop(0, slots // 64, step, 0)

    def mask(i, carry):
        slot = lax.broadcasted_iota(jnp.int32, (unit, 128), 0) + unit * i
        g = jnp.full((unit, 128), 0, jnp.int32) + grid_ref[i]
        _, p, q, special, pm, qm = slot_of(slot, g)
        k = jnp.where(g == 8, keep_ref[0], jnp.where(g == 16, keep_ref[1], keep_ref[2]))
        plus = jnp.where((p < k) & (q < k), 1.0, 0.0)
        minus = jnp.where((pm < k) & (qm < k), 1.0, 0.0)
        n = jnp.where(special, 0.0, 1.0)
        dst = pl.ds(pl.multiple_of(i * unit, unit), unit)
        nm[dst, :] = n.astype(BF)
        nb[dst, :] = (1.0 - n).astype(BF)
        for sign, (m, im) in enumerate(((plus, plus * n), (minus, -minus * n))):
            for ref, f in ((k1, 1.0), (k3, 0.05 * 0.0025)):
                ref[sign, dst, 0:128] = (m * f).astype(BF)
                ref[sign, dst, 128:256] = (im * f).astype(BF)
        return carry

    lax.fori_loop(0, NBLK, mask, 0)


def build_mix(w_ref, out_ref):
    i = lax.broadcasted_iota(jnp.int32, (64, 128), 0)
    j = lax.broadcasted_iota(jnp.int32, (64, 128), 1)
    dup = jnp.where((j & 63) == i, 1.0, 0.0).astype(BF)
    r = lax.broadcasted_iota(jnp.int32, (512, 128), 0)
    c = lax.broadcasted_iota(jnp.int32, (512, 128), 1)
    diag = ((r // 64) & 1) == (c // 64)
    for layer in range(LAYERS):
        re = jnp.where(diag, nn(w_ref[layer, 0], dup), 0.0)
        im = jnp.where(diag, nn(w_ref[layer, 1], dup), 0.0)
        for g in range(4):
            a = re[g * 128 : (g + 1) * 128].astype(BF)
            b = im[g * 128 : (g + 1) * 128]
            out_ref[layer, g, 0:128, 0:128] = a
            out_ref[layer, g, 128:256, 128:256] = a
            out_ref[layer, g, 0:128, 128:256] = b.astype(BF)
            out_ref[layer, g, 128:256, 0:128] = (-b).astype(BF)


def min_layer(layer):
    return layer if isinstance(layer, int) else jnp.minimum(layer, LAYERS - 1)


def fold(x):
    return jnp.sum(x.reshape(x.shape[0] // 8, 8, x.shape[1]), 0)


def kernel(
    grid_ref, keep_ref, core_ref, x_hbm, cot_hbm,
    n1g, n1b, w1_hbm, b1, w2_hbm, b2, n2g, n2b, fc1_hbm, fb1, fc2_hbm, fb2,
    out_hbm, xg_hbm, m0, m1, m2, t0, t1, t2,
    x_ref, cot_ref, w1, w2, fc1, fc2, out_ref, grads_ref, sems,
    at, st, k1, k3, nm, nb, w1g, w2g,
    xh1, rs1, hu, ul, z, o, da, ds, pq, xh2, rs2, v, act, dp,
    gmid, acc,
):
    g_s, gy, gm, xg_ref = hu, ul, x_ref, cot_ref

    def copy(k, src, dst):
        return pltpu.make_async_copy(src, dst, sems.at[k])

    loads = [
        copy(k, src, dst)
        for k, (src, dst) in enumerate(
            ((x_hbm, x_ref), (w1_hbm, w1), (w2_hbm, w2), (fc1_hbm, fc1), (fc2_hbm, fc2), (cot_hbm, cot_ref))
        )
    ]
    for c in loads:
        c.start()
    rows = x_ref.shape[0]
    slots = rows // 2
    tiles = rows // RT
    stiles = slots // ST
    build_tables(grid_ref, keep_ref, at, k1, k3, nm, nb)
    for i in range(4):
        st[:, i * 256 : (i + 1) * 256] = at[i * 256 : (i + 1) * 256, :].T
    loads[1].wait()
    loads[2].wait()
    build_mix(w1, w1g)
    build_mix(w2, w2g)
    acc[...] = jnp.zeros_like(acc)

    def tile(i):
        return slice(i * RT, (i + 1) * RT)

    def chunk(i, j):
        return slice(i * RT + j * CH, i * RT + (j + 1) * CH)

    def add_to(layer, k, x):
        acc[layer, k] = acc[layer, k] + fold(x)

    def norm1(layer, dst, h):
        mean = jnp.mean(h, -1, keepdims=True)
        cent = h - mean
        rstd = lax.rsqrt(jnp.mean(cent * cent, -1, keepdims=True) + 1e-05)
        xh = cent * rstd
        u = xh * n1g[pl.ds(min_layer(layer), 1), :] + n1b[pl.ds(min_layer(layer), 1), :]
        xh1[layer, dst, :] = xh.astype(BF)
        rs1[layer, dst, :] = jnp.broadcast_to(rstd, (CH, 128))
        ul[dst, :] = u.astype(BF)
        hu[dst, :] = h + u

    def enter():
        for i in range(tiles):
            for j in range(RT // CH):
                dst = chunk(i, j)
                norm1(0, dst, x_ref[dst, :].astype(F32))

    def block(f):
        f()

    loads[0].wait()
    enter()
    loads[3].wait()
    loads[4].wait()
    loads[5].wait()

    def lanes(x, times):
        return jnp.concatenate([x] * times, 1)

    def analyse(layer, t, p):
        sl = slice(t * ST, (t + 1) * ST)
        h = p % 2
        hs = slice(h * 256, (h + 1) * 256)
        if p < 2:
            zr = nn(at[sl, :], ul[:, hs]).astype(BF)
            for e in range(2):
                c0 = (2 * h + e) * 256
                z[layer, 0, sl, c0 : c0 + 128] = zr[:, e * 128 : e * 128 + 128]
        else:
            n, nbar = nm[sl, :], nb[sl, :]
            zi = nn(at[slots + t * ST : slots + (t + 1) * ST, :], ul[:, hs]).astype(BF)
            for e in range(2):
                c0 = (2 * h + e) * 256
                zie = zi[:, e * 128 : e * 128 + 128]
                zin = zie * n
                z[layer, 0, sl, c0 + 128 : c0 + 256] = zin
                z[layer, 1, sl, c0 + 128 : c0 + 256] = -zin
                z[layer, 1, sl, c0 : c0 + 128] = z[layer, 0, sl, c0 : c0 + 128] * n + zie * nbar

    def both(ref, layer, sl, gl):
        return ref[layer, :, sl, gl].reshape(2 * ST, 256)

    def put(ref, layer, sl, gl, x, c=None):
        if c is None:
            ref[layer, :, sl, gl] = x.reshape(2, ST, 256)
        else:
            r0 = sl.start + c % ST
            ref[layer, c // ST, r0 : r0 + CE, gl] = x

    def combine(dst, sl, cs, x, signed):
        n, nbar = nm[sl, :], nb[sl, :]
        rp, ip = x[0:ST, 0:128], x[0:ST, 128:256]
        rm, im = x[ST : 2 * ST, 0:128], x[ST : 2 * ST, 128:256]
        dst[sl, cs] = rp + rm * n
        q = ip + im if signed else (ip - im) * n
        dst[slots + sl.start : slots + sl.stop, cs] = q + rm * nbar

    def mix_forward(layer):
        def cut(k):
            t, g = k // 4, k % 4
            return slice(t * ST, (t + 1) * ST), slice(g * 128, (g + 1) * 128), slice(g * 256, (g + 1) * 256), g

        def dot_a(k):
            sl, cs, gl, g = cut(k)
            return nn(both(z, layer, sl, gl), w1g[layer, g])

        def gelu_a(k, a):
            sl, cs, gl, g = cut(k)
            bias = lanes2(b1[layer, 0:1, cs], b1[layer, 1:2, cs])
            ys = []
            for c in range(0, 2 * ST, CE):
                og, dag = gelu_split(a[c : c + CE] + bias)
                ys.append(og)
                put(o, layer, sl, gl, og, c)
                put(da, layer, sl, gl, dag, c)
            return nn(jnp.concatenate(ys, 0), w2g[layer, g])

        def shrink_e(k, ew):
            sl, cs, gl, g = cut(k)
            bias = lanes2(b2[layer, 0:1, cs], b2[layer, 1:2, cs])
            for c in range(0, ST, CE):
                rs = slice(sl.start + c, sl.start + c + CE)
                ss = []
                for sign in range(2):
                    e = ew[sign * ST + c : sign * ST + c + CE] + bias
                    r = lax.rsqrt(e * e + 0.0025)
                    c1 = k1[sign, rs, :]
                    ss.append((e - 0.05 * (e * r)).astype(BF) * c1)
                    r = r.astype(BF)
                    ds[layer, sign, rs, gl] = c1 - k3[sign, rs, :] * (r * r * r)
                n, nbar = nm[rs, :], nb[rs, :]
                rm = ss[1][:, 0:128]
                pq[rs, cs] = ss[0][:, 0:128] + rm * n
                pq[slots + rs.start : slots + rs.stop, cs] = ss[0][:, 128:256] + ss[1][:, 128:256] + rm * nbar

        steps = stiles * 4
        for p in range(4):
            analyse(layer, 0, p)
        a = dot_a(0)
        e_prev = None
        for k in range(steps):
            t, g = k // 4, k % 4
            if t + 1 < stiles:
                analyse(layer, t + 1, g)
            nxt = dot_a(k + 1) if k + 1 < steps else None
            e = gelu_a(k, a)
            if e_prev is not None:
                shrink_e(k - 1, e_prev)
            a, e_prev = nxt, e
        shrink_e(steps - 1, e_prev)

    def ff_forward(layer):
        def norm2(i, y):
            for j in range(RT // CH):
                cd = chunk(i, j)
                mid = y[j * CH : (j + 1) * CH] + hu[cd, :]
                mean = jnp.mean(mid, -1, keepdims=True)
                cent = mid - mean
                rstd = lax.rsqrt(jnp.mean(cent * cent, -1, keepdims=True) + 1e-05)
                xh = cent * rstd
                xh2[layer, cd, :] = xh.astype(BF)
                rs2[layer, cd, :] = jnp.broadcast_to(rstd, (CH, 128))
                v[layer, cd, :] = (xh * n2g[pl.ds(layer, 1), :] + n2b[pl.ds(layer, 1), :]).astype(BF)
                hu[cd, :] = mid
            return nn(v[layer, tile(i), :], fc1[layer])

        def gelu_f(i, pre):
            for j in range(0, RT, CF):
                cd = slice(i * RT + j, i * RT + j + CF)
                act[layer, cd, :], dp[layer, cd, :] = gelu_pair((pre[j : j + CF] + fb1[pl.ds(layer, 1), :]).astype(BF))
            return nn(act[layer, tile(i), :], fc2[layer])

        def leave(i, br):
            for j in range(RT // CH):
                cd = chunk(i, j)
                h = hu[cd, :] + (br[j * CH : (j + 1) * CH] + fb2[pl.ds(layer, 1), :])
                out_ref[cd, :] = h.astype(BF)
                norm1(layer + 1, cd, h)

        def dot_y(i):
            return nn(st[tile(i), :], pq[...])

        y = dot_y(0)
        pre = None
        for i in range(tiles + 1):
            nxt = dot_y(i + 1) if i + 1 < tiles else None
            br = gelu_f(i - 1, pre) if i >= 1 else None
            pre = norm2(i, y) if i < tiles else None
            if i >= 1:
                leave(i - 1, br)
            y = nxt

    @partial(lax.fori_loop, 0, LAYERS, init_val=0)
    def _(layer, carry):
        block(lambda: mix_forward(layer))
        block(lambda: ff_forward(layer))
        return carry

    out_copy = copy(6, out_ref, out_hbm)
    out_copy.start()
    for i in range(tiles):
        g_s[tile(i), :] = cot_ref[tile(i), :].astype(F32)

    def norm_back(gv, xh, rstd, gain):
        t = gv * gain
        mt = jnp.mean(t, -1, keepdims=True)
        mx = jnp.mean(t * xh, -1, keepdims=True)
        return rstd * (t - mt - xh * mx)

    def with_sums(left, right):
        ones = jnp.ones((16, left.shape[0]), BF)
        return nn(jnp.concatenate([left.T, ones], 0), right)

    def ff_backward(layer):
        def load_g(rs):
            return g_s[rs, :]

        def dot_a(i):
            dst = tile(i)
            gmt = g_s[dst, :].astype(BF)
            gm[dst, :] = gmt
            return nt(gmt, fc2[layer])

        def mul(i, ga_):
            dst = tile(i)
            dp[layer, dst, :] = ga_.astype(BF) * dp[layer, dst, :]
            return nt(dp[layer, dst, :], fc1[layer])

        def leave(i, gv):
            for j in range(RT // CH):
                cd = chunk(i, j)
                gvc = gv[j * CH : (j + 1) * CH]
                xh = xh2[layer, cd, :].astype(F32)
                add_to(layer, 6, gvc * xh)
                add_to(layer, 7, gvc)
                rstd = lanes(rs2[layer, cd, :], 4)
                gmc = load_g(cd) + norm_back(gvc, xh, rstd, n2g[pl.ds(layer, 1), :])
                gmid[cd, :] = gmc
                gy[cd, :] = gmc.astype(BF)

        cur = dot_a(0)
        prev = None
        for i in range(tiles + 1):
            nxt = dot_a(i + 1) if i + 1 < tiles else None
            gv = mul(i, cur) if i < tiles else None
            if i >= 1:
                leave(i - 1, prev)
            cur, prev = nxt, gv
        base = pl.multiple_of((layer ^ core_ref[0]) * PER, PER)
        for left, right, off, vec in ((v, dp[layer], 0, 8), (act, gm[...], 512, 9)):
            for h in range(2):
                hs = slice(h * 256, (h + 1) * 256)
                r = base + off + h * 256
                if h == 0:
                    p = with_sums(left[layer, :, hs], right)
                    acc[layer, vec, 0:1, :] = p[256:257]
                else:
                    p = tn(left[layer, :, hs], right)
                grads_ref[pl.ds(r, 256), :] = p[0:256].astype(BF)

    def mix_backward(layer):
        def cut(k):
            t, g = k // 4, k % 4
            return slice(t * ST, (t + 1) * ST), slice(g * 128, (g + 1) * 128), slice(g * 256, (g + 1) * 256), g

        def spectrum(t, h):
            hs = slice(h * 256, (h + 1) * 256)
            gr = nn(at[t * ST : (t + 1) * ST, :], gy[:, hs]).astype(BF)
            gi = nn(at[slots + t * ST : slots + (t + 1) * ST, :], gy[:, hs]).astype(BF)
            return gr, gi

        def dot_o(k, gr, gi):
            sl, cs, gl, g = cut(k)
            n, nbar = nm[sl, :], nb[sl, :]
            hs = slice(g % 2 * 128, g % 2 * 128 + 128)
            grc, gic = gr[:, hs], gi[:, hs]
            ds[layer, 0, sl, gl] = lanes2(grc, gic) * ds[layer, 0, sl, gl]
            ds[layer, 1, sl, gl] = lanes2(grc * n + gic * nbar, gic) * ds[layer, 1, sl, gl]
            return nt(both(ds, layer, sl, gl), w2g[layer, g])

        def dot_z(k, go):
            sl, cs, gl, g = cut(k)
            put(da, layer, sl, gl, go.astype(BF) * both(da, layer, sl, gl))
            return nt(both(da, layer, sl, gl), w1g[layer, g])

        def leave(k, gz):
            sl, cs, gl, g = cut(k)
            combine(pq, sl, cs, gz.astype(BF), False)

        steps = stiles * 4
        sp = {0: spectrum(0, 0)}
        go = dot_o(0, *sp[0])
        prev = None
        for k in range(steps + 1):
            if k % 2 == 0 and k + 2 < steps:
                sp[k // 2 + 1] = spectrum((k + 2) // 4, (k + 2) // 2 % 2)
            nxt = dot_o(k + 1, *sp[(k + 1) // 2]) if k + 1 < steps else None
            gz = dot_z(k, go) if k < steps else None
            if k >= 1:
                leave(k - 1, prev)
            go, prev = nxt, gz
        base = pl.multiple_of((layer ^ core_ref[0]) * PER, PER) + 1024
        low = lax.broadcasted_iota(jnp.int32, (64, 128), 1) < 64
        for left, right, off, vec in ((o, ds, base + 128, 4), (z, da, base, 2)):
            for g in range(4):
                cs = slice(g * 128, (g + 1) * 128)
                gl = slice(g * 256, (g + 1) * 256)
                lf = left[layer, :, :, gl].reshape(rows, 256)
                rt = right[layer, :, :, gl].reshape(rows, 256)
                p = with_sums(lf, rt)
                acc[layer, vec, 0:1, cs] = p[256:257, 0:128]
                acc[layer, vec + 1, 0:1, cs] = p[256:257, 128:256]
                re = p[0:128, 0:128] + p[128:256, 128:256]
                im = p[0:128, 128:256] - p[128:256, 0:128]
                grads_ref[pl.ds(off, 64), cs] = jnp.where(low, re[0:64], re[64:128]).astype(BF)
                grads_ref[pl.ds(off + 64, 64), cs] = jnp.where(low, im[0:64], im[64:128]).astype(BF)

    def in_backward(layer):
        def leave(i, y):
            for j in range(RT // CH):
                cd = chunk(i, j)
                gmc = gmid[cd, :]
                gu = y[j * CH : (j + 1) * CH] + gmc
                xh = xh1[layer, cd, :].astype(F32)
                add_to(layer, 0, gu * xh)
                add_to(layer, 1, gu)
                rstd = lanes(rs1[layer, cd, :], 4)
                gh = gmc + norm_back(gu, xh, rstd, n1g[pl.ds(min_layer(layer), 1), :])
                xg_ref[cd, :] = gh.astype(BF)
                g_s[cd, :] = gh

        y = nn(st[tile(0), :], pq[...])
        for i in range(tiles):
            nxt = nn(st[tile(i + 1), :], pq[...]) if i + 1 < tiles else None
            leave(i, y)
            y = nxt

    def vectors(layer):
        t = jnp.sum(acc[layer], 1)
        t = jnp.concatenate([t, jnp.zeros((PER - 1290, 512), F32)], 0)
        grads_ref[pl.ds(pl.multiple_of((layer ^ core_ref[0]) * PER, PER) + 1280, PER - 1280), :] = t.astype(BF)

    sends = [
        copy(8 + k, grads_ref.at[pl.ds(row, PER // 3)], dst)
        for k, (row, dst) in enumerate(
            (((3 * half + c) * (PER // 3), dst) for half, refs in ((1, (t0, t1, t2)), (0, (m0, m1, m2))) for c, dst in enumerate(refs))
        )
    ]

    def start_half(half):
        for h in range(2):

            @pl.when(half == h)
            def _():
                for c in sends[3 - 3 * h : 6 - 3 * h]:
                    c.start()

    @partial(lax.fori_loop, 0, LAYERS, init_val=0)
    def _(step, carry):
        layer = LAYERS - 1 - step
        block(lambda: ff_backward(layer))
        block(lambda: mix_backward(layer))
        block(lambda: in_backward(layer))

        @pl.when(step == 0)
        def _():
            vectors(1)
            start_half(1 - core_ref[0])

        return carry

    xg_copy = copy(7, xg_ref, xg_hbm)
    vectors(0)
    start_half(core_ref[0])
    xg_copy.start()
    out_copy.wait()
    for c in sends:
        c.wait()
    xg_copy.wait()


def lanes2(a, b):
    return jnp.concatenate([a, b], 1)


def local_step(core, x_in, cotangent, block_grid, keep_modes, n1g, n1b, w1, b1, w2, b2, n2g, n2b, fc1, fb1, fc2, fb2):
    rows, d = x_in.shape
    slots = rows // 2
    vm = pl.BlockSpec(memory_space=pltpu.VMEM)
    sm = pl.BlockSpec(memory_space=pltpu.SMEM)
    hbm = pl.BlockSpec(memory_space=pl.ANY)
    w1r = w1.reshape(LAYERS, 2, 512, 64)
    w2r = w2.reshape(LAYERS, 2, 512, 64)
    scratch = [
        pltpu.VMEM((rows, d), BF), pltpu.VMEM((rows, d), BF),
        pltpu.VMEM(w1r.shape, BF), pltpu.VMEM(w2r.shape, BF), pltpu.VMEM(fc1.shape, BF), pltpu.VMEM(fc2.shape, BF),
        pltpu.VMEM((rows, d), BF), pltpu.VMEM((LAYERS * PER, d), BF),
        pltpu.SemaphoreType.DMA((14,)),
        pltpu.VMEM((rows, rows), BF), pltpu.VMEM((rows, rows), BF),
        pltpu.VMEM((2, slots, 256), BF), pltpu.VMEM((2, slots, 256), BF),
        pltpu.VMEM((slots, 128), BF), pltpu.VMEM((slots, 128), BF),
        pltpu.VMEM((LAYERS, 4, 256, 256), BF), pltpu.VMEM((LAYERS, 4, 256, 256), BF),
        pltpu.VMEM((LAYERS + 1, rows, d), BF), pltpu.VMEM((LAYERS + 1, rows, 128), F32),
        pltpu.VMEM((rows, d), F32), pltpu.VMEM((rows, d), BF),
        pltpu.VMEM((LAYERS, 2, slots, 2 * d), BF), pltpu.VMEM((LAYERS, 2, slots, 2 * d), BF),
        pltpu.VMEM((LAYERS, 2, slots, 2 * d), BF), pltpu.VMEM((LAYERS, 2, slots, 2 * d), BF),
        pltpu.VMEM((rows, d), BF),
        pltpu.VMEM((LAYERS, rows, d), BF), pltpu.VMEM((LAYERS, rows, 128), F32),
        pltpu.VMEM((LAYERS, rows, d), BF), pltpu.VMEM((LAYERS, rows, d), BF), pltpu.VMEM((LAYERS, rows, d), BF),
        pltpu.VMEM((rows, d), F32),
        pltpu.VMEM((LAYERS, 10, 8, d), F32),
    ]
    return pl.pallas_call(
        kernel,
        out_shape=(
            jax.ShapeDtypeStruct((rows, d), BF),
            jax.ShapeDtypeStruct((rows, d), BF),
        )
        + (jax.ShapeDtypeStruct((PER // 3, d), BF),) * 6,
        in_specs=[sm, sm, sm, hbm, hbm, vm, vm, hbm, vm, hbm, vm, vm, vm, hbm, vm, hbm, vm],
        out_specs=(hbm,) * 8,
        scratch_shapes=scratch,
        compiler_params=pltpu.CompilerParams(vmem_limit_bytes=58 * 1024 * 1024),
        name="slab_step",
    )(block_grid, keep_modes, core, x_in, cotangent, n1g, n1b, w1r, b1, w2r, b2, n2g, n2b, fc1, fb1, fc2, fb2)


AXES = ("dp", "modes")


def spread_layer(layer, parts, outs, bufs, sems):
    fc1, fc2, w1, w2 = bufs
    p0, p1, p2 = parts
    n = PER // 3
    copies = [pltpu.make_async_copy(buf, out.at[layer], sems.at[k]) for k, (buf, out) in enumerate(zip(bufs, outs))]
    fc1[0:n, :] = p0[...].astype(F32)
    fc1[n:512, :] = p1[0 : 512 - n, :].astype(F32)
    copies[0].start()
    fc2[0 : 2 * n - 512, :] = p1[512 - n : n, :].astype(F32)
    fc2[2 * n - 512 : 512, :] = p2[0 : 1024 - 2 * n, :].astype(F32)
    copies[1].start()
    for k, (ref, base) in enumerate(((w1, 1024 - 2 * n), (w2, 1152 - 2 * n))):
        for part in range(2):
            block = p2[base + part * 64 : base + part * 64 + 64, :].astype(F32)
            for j in range(8):
                ref[part, j] = block[:, j * 64 : j * 64 + 64]
        copies[2 + k].start()
    return copies


def spread_mine(core_ref, a0, a1, a2, fc1_out, fc2_out, w1_out, w2_out, fc1, fc2, w1, w2, sems):
    for c in spread_layer(core_ref[0], (a0, a1, a2), (fc1_out, fc2_out, w1_out, w2_out), (fc1, fc2, w1, w2), sems):
        c.wait()


def spread_other(
    core_ref, a0, a1, a2, c0, c1, c2, fc1_in, fc2_in, w1_in, w2_in,
    fc1_out, fc2_out, w1_out, w2_out, n1g, n1b, b1, b2, n2g, n2b, fb1, fb2, fc1, fc2, w1, w2, sems,
):
    copies = spread_layer(1 - core_ref[0], (c0, c1, c2), (fc1_out, fc2_out, w1_out, w2_out), (fc1, fc2, w1, w2), sems)
    row = 1280 - 2 * (PER // 3)
    here = a2[row : row + 16, :].astype(F32)
    there = c2[row : row + 16, :].astype(F32)
    for layer in range(LAYERS):
        vec = jnp.where(core_ref[0] == layer, here, there)
        for row, ref in ((0, n1g), (1, n1b), (6, n2g), (7, n2b), (8, fb1), (9, fb2)):
            ref[layer : layer + 1, :] = vec[row : row + 1]
        b1[layer] = vec[2:4]
        b2[layer] = vec[4:6]
    for c in copies:
        c.wait()


def unpack_shapes(d):
    mix = jax.ShapeDtypeStruct((LAYERS, 2, 8, 64, 64), F32)
    full = jax.ShapeDtypeStruct((LAYERS, d, d), F32)
    big = (full, full, mix, mix)
    scratch = [pltpu.VMEM(s.shape[1:], F32) for s in big] + [pltpu.SemaphoreType.DMA((4,))]
    return big, scratch


def unpack_mine(core, mine, d):
    vm = pl.BlockSpec(memory_space=pltpu.VMEM)
    hbm = pl.BlockSpec(memory_space=pl.ANY)
    big, scratch = unpack_shapes(d)
    return pl.pallas_call(
        spread_mine,
        out_shape=big,
        in_specs=[pl.BlockSpec(memory_space=pltpu.SMEM), vm, vm, vm],
        out_specs=(hbm,) * 4,
        scratch_shapes=scratch,
        compiler_params=pltpu.CompilerParams(vmem_limit_bytes=16 * 1024 * 1024),
        cost_estimate=pl.CostEstimate(flops=1 << 20, bytes_accessed=4 << 20, transcendentals=0),
        name="spread_mine",
    )(core, *mine)


def unpack(core, mine, other, d, big_in=None):
    vm = pl.BlockSpec(memory_space=pltpu.VMEM)
    hbm = pl.BlockSpec(memory_space=pl.ANY)
    big, scratch = unpack_shapes(d)
    vec = jax.ShapeDtypeStruct((LAYERS, d), F32)
    pair = jax.ShapeDtypeStruct((LAYERS, 2, d), F32)
    if big_in is None:
        big_in = unpack_mine(core, mine, d)
    fc1, fc2, w1, w2, n1g, n1b, b1, b2, n2g, n2b, fb1, fb2 = pl.pallas_call(
        spread_other,
        out_shape=big + (vec, vec, pair, pair, vec, vec, vec, vec),
        in_specs=[pl.BlockSpec(memory_space=pltpu.SMEM)] + [vm] * 6 + [hbm] * 4,
        out_specs=(hbm,) * 4 + (vm,) * 8,
        scratch_shapes=scratch,
        input_output_aliases={7: 0, 8: 1, 9: 2, 10: 3},
        compiler_params=pltpu.CompilerParams(vmem_limit_bytes=16 * 1024 * 1024),
        name="spread_other",
    )(core, *mine, *other, *big_in)
    return n1g, n1b, w1, b1, w2, b2, n2g, n2b, fc1, fb1, fc2, fb2


def exchange(a, bit, count):
    return lax.ppermute(a, AXES, [(i, i ^ bit) for i in range(count)])


def add(a, b):
    return (a.astype(F32) + b.astype(F32)).astype(BF)


def all_sum(mine, other, count):
    me = lax.axis_index(AXES)
    top = count // 2
    bits = [1 << k for k in range(top.bit_length() - 1)]
    orders = [[bits[(c + k) % 3] for k in range(3)] for c in range(3)]
    gots = [exchange(t, top, count) for t in other]
    parts = [add(m, got) for m, got in zip(mine, gots)]
    for k in range(3):
        moved = []
        for c in range(3):
            n = parts[c].shape[0] // 2
            high = (me & orders[c][k]) != 0
            keep = jnp.where(high, parts[c][n:], parts[c][:n])
            send = jnp.where(high, parts[c][:n], parts[c][n:])
            moved.append((keep, exchange(send, orders[c][k], count)))
        parts = [add(keep, got) for keep, got in moved]
    for bit in bits[3:]:
        parts = [add(p, exchange(p, bit, count)) for p in parts]
    for k in reversed(range(3)):
        gots = [exchange(parts[c], orders[c][k], count) for c in range(3)]
        for c in range(3):
            high = (me & orders[c][k]) != 0
            low_part = jnp.where(high, gots[c], parts[c])
            high_part = jnp.where(high, parts[c], gots[c])
            parts[c] = jnp.concatenate([low_part, high_part])
    return parts, [exchange(p, top, count) for p in parts]


def solution(mesh):
    count = mesh.shape["dp"] * mesh.shape["modes"]

    def on_device(*args):
        core = lax.axis_index("dp").astype(jnp.int32).reshape(1)
        out, x_grad, *parts = local_step(core, *args)
        mine, other = all_sum(parts[:3], parts[3:], count)
        return (out, x_grad) + tuple(unpack(core, mine, other, out.shape[1]))

    rows = P(AXES, None)
    return jax.shard_map(
        on_device,
        mesh=mesh,
        in_specs=(rows, rows, P(AXES)) + (P(),) * 13,
        out_specs=(rows, rows) + (P(),) * 12,
        check_vma=False,
    )
```

```python
import math
from functools import partial

import jax
import jax.numpy as jnp
from jax import lax
from jax.experimental import pallas as pl
from jax.experimental.pallas import tpu as pltpu
from jax.sharding import PartitionSpec as P

LAYERS = 2
NBLK = 16
F32 = jnp.float32
BF = jnp.bfloat16
C0 = math.sqrt(2.0 / math.pi)
C1 = 0.044715 * C0
PER = 1344
RT = 256
ST = 256
NH = 512
CH = 64
CE = 32
CF = 16


def nn(a, b):
    return jnp.dot(a, b, preferred_element_type=F32)


def nt(a, b):
    return lax.dot_general(a, b, (((1,), (1,)), ((), ())), preferred_element_type=F32)


def tn(a, b):
    return lax.dot_general(a, b, (((0,), (0,)), ((), ())), preferred_element_type=F32)


def gelu_pair(x):
    x2 = x * x
    p = 0.5 + 0.5 * jnp.tanh(x * (C0 + C1 * x2))
    y = x * p
    return y, p + y * (1.0 - p) * (2.0 * C0 + (6.0 * C1) * x2)


def gelu_split(x):
    p = 0.5 + 0.5 * jnp.tanh(x * (C0 + C1 * (x * x)))
    y = (x * p).astype(BF)
    xb, pb = x.astype(BF), p.astype(BF)
    qb = 1.0 - pb
    return y, pb + y * qb * (2.0 * C0 + (6.0 * C1) * (xb * xb))


def cos_of(t):
    x = t - 0.5
    w = (2.0 * math.pi * x) ** 2
    c = jnp.full_like(w, 1.0 / math.factorial(16))
    for k in range(7, -1, -1):
        c = c * w + (-1.0) ** k / math.factorial(2 * k)
    return -c


def cos_sin(t):
    x = t - 0.5
    w = (2.0 * math.pi * x) ** 2
    c = jnp.full_like(w, 1.0 / math.factorial(16))
    s = jnp.full_like(w, -1.0 / math.factorial(15))
    for k in range(7, -1, -1):
        c = c * w + (-1.0) ** k / math.factorial(2 * k)
        if k < 7:
            s = s * w + (-1.0) ** k / math.factorial(2 * k + 1)
    return -c, -s * (2.0 * math.pi * x)


def pick(values, block):
    out = jnp.zeros(block.shape, jnp.int32)
    for j in range(NBLK):
        out = jnp.where(block == j, values[j], out)
    return out


def log_of(grid):
    return jnp.where(grid == 8, 3, jnp.where(grid == 16, 4, 5))


def slot_of(slot, grid):
    half = grid * grid // 2
    local = slot & (half - 1)
    pp = lax.shift_right_logical(local, log_of(grid))
    qq = local & (grid - 1)
    mid = lax.shift_right_logical(grid, 1)
    first = pp == 0
    special = first & ((qq == 0) | (qq == mid))
    p = jnp.where(first & (qq >= mid), mid, pp)
    q = jnp.where(first & (qq == mid), 0, qq)
    pm = jnp.where(special, p, (grid - p) & (grid - 1))
    qm = jnp.where(special, mid, (grid - q) & (grid - 1))
    return 2 * (slot - local), p, q, special, pm, qm


def build_tables(grid_ref, keep_ref, at, k1, k3, nm, nb):
    rows = at.shape[1]
    slots = rows // 2
    unit = slots // NBLK
    vals = [grid_ref[j] for j in range(NBLK)]
    lane = lax.broadcasted_iota(jnp.int32, (8, rows), 1)
    sub = lax.broadcasted_iota(jnp.int32, (8, rows), 0)
    gc = pick(vals, lane // (2 * unit))
    span = gc * gc
    start_c = lane & ~(span - 1)
    local = lane & (span - 1)
    p_c = lax.shift_right_logical(local, log_of(gc))
    q_c = local & (gc - 1)
    ginv = 1.0 / gc.astype(F32)
    bcs = []
    for j in range(4):
        q_r = (sub + 8 * j) & (gc - 1)
        bcs.append(cos_sin(((q_r * q_c) & (gc - 1)).astype(F32) * ginv))

    def two(x):
        return jnp.concatenate([x, x], 0)

    gc2, start2, p2, q2, ginv2, sub2 = two(gc), two(start_c), two(p_c), two(q_c), two(ginv), lax.broadcasted_iota(jnp.int32, (16, rows), 0)

    def step(i, carry):
        slot = (sub + 8 * i) * 8
        gb = jnp.where(sub < 4, grid_ref[2 * i], grid_ref[2 * i + 1])
        half = gb * gb // 2
        loc = slot & (half - 1)
        p_b = lax.shift_right_logical(loc, log_of(gb))
        ac, as_ = cos_sin(((p_b * p_c) & (gc - 1)).astype(F32) * ginv)
        same = jnp.where(2 * (slot - loc) == start_c, ginv, 0.0)
        ac = ac * same
        as_ = as_ * same
        for j in range(0, 8, 2):
            re, im = [], []
            for d in range(2):
                bc, bs = bcs[(j + d) % 4]
                a1 = ac[j + d : j + d + 1, :]
                a2 = as_[j + d : j + d + 1, :]
                re.append(a1 * bc - a2 * bs)
                im.append(-(a2 * bc + a1 * bs))
            s0 = pl.multiple_of(i * 64 + j * 8, 16)
            at[pl.ds(s0, 16), :] = jnp.concatenate(re, 0).astype(BF)
            at[pl.ds(slots + s0, 16), :] = jnp.concatenate(im, 0).astype(BF)
            g = grid_ref[2 * i + j // 4]
            first = (s0 & (g * g // 2 - 1)) < g

            @pl.when(first)
            def _():
                gv = jnp.full((16, rows), 0, jnp.int32) + g
                start, p, q, special, pm, qm = slot_of(sub2 + s0, gv)
                live = jnp.where(start == start2, ginv2, 0.0)
                t = ((p * p2 + q * q2) & (gc2 - 1)).astype(F32) * ginv2
                tm = ((pm * p2 + qm * q2) & (gc2 - 1)).astype(F32) * ginv2
                quarter = jnp.where(t >= 0.75, t - 0.75, t + 0.25)
                at[pl.ds(s0, 16), :] = (cos_of(t) * live).astype(BF)
                at[pl.ds(slots + s0, 16), :] = (cos_of(jnp.where(special, tm, quarter)) * live).astype(BF)

        return carry

    lax.fori_loop(0, slots // 64, step, 0)

    def mask(i, carry):
        slot = lax.broadcasted_iota(jnp.int32, (unit, 128), 0) + unit * i
        g = jnp.full((unit, 128), 0, jnp.int32) + grid_ref[i]
        _, p, q, special, pm, qm = slot_of(slot, g)
        k = jnp.where(g == 8, keep_ref[0], jnp.where(g == 16, keep_ref[1], keep_ref[2]))
        plus = jnp.where((p < k) & (q < k), 1.0, 0.0)
        minus = jnp.where((pm < k) & (qm < k), 1.0, 0.0)
        n = jnp.where(special, 0.0, 1.0)
        dst = pl.ds(pl.multiple_of(i * unit, unit), unit)
        nm[dst, :] = n.astype(BF)
        nb[dst, :] = (1.0 - n).astype(BF)
        for sign, (m, im) in enumerate(((plus, plus * n), (minus, -minus * n))):
            for ref, f in ((k1, 1.0), (k3, 0.05 * 0.0025)):
                ref[sign, dst, 0:128] = (m * f).astype(BF)
                ref[sign, dst, 128:256] = (im * f).astype(BF)
        return carry

    lax.fori_loop(0, NBLK, mask, 0)


def build_mix(w_ref, out_ref):
    i = lax.broadcasted_iota(jnp.int32, (64, 128), 0)
    j = lax.broadcasted_iota(jnp.int32, (64, 128), 1)
    dup = jnp.where((j & 63) == i, 1.0, 0.0).astype(BF)
    r = lax.broadcasted_iota(jnp.int32, (512, 128), 0)
    c = lax.broadcasted_iota(jnp.int32, (512, 128), 1)
    diag = ((r // 64) & 1) == (c // 64)
    for layer in range(LAYERS):
        re = jnp.where(diag, nn(w_ref[layer, 0], dup), 0.0)
        im = jnp.where(diag, nn(w_ref[layer, 1], dup), 0.0)
        for g in range(4):
            a = re[g * 128 : (g + 1) * 128].astype(BF)
            b = im[g * 128 : (g + 1) * 128]
            out_ref[layer, g, 0:128, 0:128] = a
            out_ref[layer, g, 128:256, 128:256] = a
            out_ref[layer, g, 0:128, 128:256] = b.astype(BF)
            out_ref[layer, g, 128:256, 0:128] = (-b).astype(BF)


def min_layer(layer):
    return layer if isinstance(layer, int) else jnp.minimum(layer, LAYERS - 1)


def fold(x):
    return jnp.sum(x.reshape(x.shape[0] // 8, 8, x.shape[1]), 0)


def kernel(
    grid_ref, keep_ref, core_ref, x_hbm, cot_hbm,
    n1g, n1b, w1_hbm, b1, w2_hbm, b2, n2g, n2b, fc1_hbm, fb1, fc2_hbm, fb2,
    out_hbm, xg_hbm, m0, m1, m2, t0, t1, t2,
    x_ref, cot_ref, w1, w2, fc1, fc2, out_ref, grads_ref, sems,
    at, st, k1, k3, nm, nb, w1g, w2g,
    xh1, rs1, hu, ul, z, o, da, ds, pq, xh2, rs2, v, act, dp,
    gmid, acc,
):
    g_s, gy, gm, xg_ref = hu, ul, x_ref, cot_ref

    def copy(k, src, dst):
        return pltpu.make_async_copy(src, dst, sems.at[k])

    loads = [
        copy(k, src, dst)
        for k, (src, dst) in enumerate(
            ((x_hbm, x_ref), (w1_hbm, w1), (w2_hbm, w2), (fc1_hbm, fc1), (fc2_hbm, fc2), (cot_hbm, cot_ref))
        )
    ]
    for c in loads:
        c.start()
    rows = x_ref.shape[0]
    slots = rows // 2
    tiles = rows // RT
    stiles = slots // ST
    build_tables(grid_ref, keep_ref, at, k1, k3, nm, nb)
    for i in range(4):
        st[:, i * 256 : (i + 1) * 256] = at[i * 256 : (i + 1) * 256, :].T
    loads[1].wait()
    loads[2].wait()
    build_mix(w1, w1g)
    build_mix(w2, w2g)
    acc[...] = jnp.zeros_like(acc)

    def tile(i):
        return slice(i * RT, (i + 1) * RT)

    def chunk(i, j):
        return slice(i * RT + j * CH, i * RT + (j + 1) * CH)

    def add_to(layer, k, x):
        acc[layer, k] = acc[layer, k] + fold(x)

    def norm1(layer, dst, h):
        mean = jnp.mean(h, -1, keepdims=True)
        cent = h - mean
        rstd = lax.rsqrt(jnp.mean(cent * cent, -1, keepdims=True) + 1e-05)
        xh = cent * rstd
        u = xh * n1g[pl.ds(min_layer(layer), 1), :] + n1b[pl.ds(min_layer(layer), 1), :]
        xh1[layer, dst, :] = xh.astype(BF)
        rs1[layer, dst, :] = jnp.broadcast_to(rstd, (CH, 128))
        ul[dst, :] = u.astype(BF)
        hu[dst, :] = h + u

    def enter():
        for i in range(tiles):
            for j in range(RT // CH):
                dst = chunk(i, j)
                norm1(0, dst, x_ref[dst, :].astype(F32))

    def block(f):
        f()

    loads[0].wait()
    enter()
    loads[3].wait()
    loads[4].wait()
    loads[5].wait()

    def lanes(x, times):
        return jnp.concatenate([x] * times, 1)

    def analyse(layer, t, p):
        sl = slice(t * ST, (t + 1) * ST)
        h = p % 2
        hs = slice(h * 256, (h + 1) * 256)
        if p < 2:
            zr = nn(at[sl, :], ul[:, hs]).astype(BF)
            for e in range(2):
                c0 = (2 * h + e) * 256
                z[layer, 0, sl, c0 : c0 + 128] = zr[:, e * 128 : e * 128 + 128]
        else:
            n, nbar = nm[sl, :], nb[sl, :]
            zi = nn(at[slots + t * ST : slots + (t + 1) * ST, :], ul[:, hs]).astype(BF)
            for e in range(2):
                c0 = (2 * h + e) * 256
                zie = zi[:, e * 128 : e * 128 + 128]
                zin = zie * n
                z[layer, 0, sl, c0 + 128 : c0 + 256] = zin
                z[layer, 1, sl, c0 + 128 : c0 + 256] = -zin
                z[layer, 1, sl, c0 : c0 + 128] = z[layer, 0, sl, c0 : c0 + 128] * n + zie * nbar

    def both(ref, layer, sl, gl):
        return ref[layer, :, sl, gl].reshape(2 * ST, 256)

    def put(ref, layer, sl, gl, x, c=None):
        if c is None:
            ref[layer, :, sl, gl] = x.reshape(2, ST, 256)
        else:
            r0 = sl.start + c % ST
            ref[layer, c // ST, r0 : r0 + CE, gl] = x

    def combine(dst, sl, cs, x, signed):
        n, nbar = nm[sl, :], nb[sl, :]
        rp, ip = x[0:ST, 0:128], x[0:ST, 128:256]
        rm, im = x[ST : 2 * ST, 0:128], x[ST : 2 * ST, 128:256]
        dst[sl, cs] = rp + rm * n
        q = ip + im if signed else (ip - im) * n
        dst[slots + sl.start : slots + sl.stop, cs] = q + rm * nbar

    def mix_forward(layer):
        def cut(k):
            t, g = k // 4, k % 4
            return slice(t * ST, (t + 1) * ST), slice(g * 128, (g + 1) * 128), slice(g * 256, (g + 1) * 256), g

        def dot_a(k):
            sl, cs, gl, g = cut(k)
            return nn(both(z, layer, sl, gl), w1g[layer, g])

        def gelu_a(k, a):
            sl, cs, gl, g = cut(k)
            bias = lanes2(b1[layer, 0:1, cs], b1[layer, 1:2, cs])
            ys = []
            for c in range(0, 2 * ST, CE):
                og, dag = gelu_split(a[c : c + CE] + bias)
                ys.append(og)
                put(o, layer, sl, gl, og, c)
                put(da, layer, sl, gl, dag, c)
            return nn(jnp.concatenate(ys, 0), w2g[layer, g])

        def shrink_e(k, ew):
            sl, cs, gl, g = cut(k)
            bias = lanes2(b2[layer, 0:1, cs], b2[layer, 1:2, cs])
            for c in range(0, ST, CE):
                rs = slice(sl.start + c, sl.start + c + CE)
                ss = []
                for sign in range(2):
                    e = ew[sign * ST + c : sign * ST + c + CE] + bias
                    r = lax.rsqrt(e * e + 0.0025)
                    c1 = k1[sign, rs, :]
                    ss.append((e - 0.05 * (e * r)).astype(BF) * c1)
                    r = r.astype(BF)
                    ds[layer, sign, rs, gl] = c1 - k3[sign, rs, :] * (r * r * r)
                n, nbar = nm[rs, :], nb[rs, :]
                rm = ss[1][:, 0:128]
                pq[rs, cs] = ss[0][:, 0:128] + rm * n
                pq[slots + rs.start : slots + rs.stop, cs] = ss[0][:, 128:256] + ss[1][:, 128:256] + rm * nbar

        steps = stiles * 4
        for p in range(4):
            analyse(layer, 0, p)
        a = dot_a(0)
        e_prev = None
        for k in range(steps):
            t, g = k // 4, k % 4
            if t + 1 < stiles:
                analyse(layer, t + 1, g)
            nxt = dot_a(k + 1) if k + 1 < steps else None
            e = gelu_a(k, a)
            if e_prev is not None:
                shrink_e(k - 1, e_prev)
            a, e_prev = nxt, e
        shrink_e(steps - 1, e_prev)

    def ff_forward(layer):
        def norm2(i, y):
            for j in range(RT // CH):
                cd = chunk(i, j)
                mid = y[j * CH : (j + 1) * CH] + hu[cd, :]
                mean = jnp.mean(mid, -1, keepdims=True)
                cent = mid - mean
                rstd = lax.rsqrt(jnp.mean(cent * cent, -1, keepdims=True) + 1e-05)
                xh = cent * rstd
                xh2[layer, cd, :] = xh.astype(BF)
                rs2[layer, cd, :] = jnp.broadcast_to(rstd, (CH, 128))
                v[layer, cd, :] = (xh * n2g[pl.ds(layer, 1), :] + n2b[pl.ds(layer, 1), :]).astype(BF)
                hu[cd, :] = mid
            return nn(v[layer, tile(i), :], fc1[layer])

        def gelu_f(i, pre):
            for j in range(0, RT, CF):
                cd = slice(i * RT + j, i * RT + j + CF)
                act[layer, cd, :], dp[layer, cd, :] = gelu_pair((pre[j : j + CF] + fb1[pl.ds(layer, 1), :]).astype(BF))
            return nn(act[layer, tile(i), :], fc2[layer])

        def leave(i, br):
            for j in range(RT // CH):
                cd = chunk(i, j)
                h = hu[cd, :] + (br[j * CH : (j + 1) * CH] + fb2[pl.ds(layer, 1), :])
                out_ref[cd, :] = h.astype(BF)
                norm1(layer + 1, cd, h)

        def dot_y(i):
            return nn(st[tile(i), :], pq[...])

        y = dot_y(0)
        pre = None
        for i in range(tiles + 1):
            nxt = dot_y(i + 1) if i + 1 < tiles else None
            br = gelu_f(i - 1, pre) if i >= 1 else None
            pre = norm2(i, y) if i < tiles else None
            if i >= 1:
                leave(i - 1, br)
            y = nxt

    @partial(lax.fori_loop, 0, LAYERS, init_val=0)
    def _(layer, carry):
        block(lambda: mix_forward(layer))
        block(lambda: ff_forward(layer))
        return carry

    out_copy = copy(6, out_ref, out_hbm)
    out_copy.start()
    for i in range(tiles):
        g_s[tile(i), :] = cot_ref[tile(i), :].astype(F32)

    def norm_back(gv, xh, rstd, gain):
        t = gv * gain
        mt = jnp.mean(t, -1, keepdims=True)
        mx = jnp.mean(t * xh, -1, keepdims=True)
        return rstd * (t - mt - xh * mx)

    def with_sums(left, right):
        ones = jnp.ones((16, left.shape[0]), BF)
        return nn(jnp.concatenate([left.T, ones], 0), right)

    def ff_backward(layer):
        def load_g(rs):
            return g_s[rs, :]

        def dot_a(i):
            dst = tile(i)
            gmt = g_s[dst, :].astype(BF)
            gm[dst, :] = gmt
            return nt(gmt, fc2[layer])

        def mul(i, ga_):
            dst = tile(i)
            dp[layer, dst, :] = ga_.astype(BF) * dp[layer, dst, :]
            return nt(dp[layer, dst, :], fc1[layer])

        def leave(i, gv):
            for j in range(RT // CH):
                cd = chunk(i, j)
                gvc = gv[j * CH : (j + 1) * CH]
                xh = xh2[layer, cd, :].astype(F32)
                add_to(layer, 6, gvc * xh)
                add_to(layer, 7, gvc)
                rstd = lanes(rs2[layer, cd, :], 4)
                gmc = load_g(cd) + norm_back(gvc, xh, rstd, n2g[pl.ds(layer, 1), :])
                gmid[cd, :] = gmc
                gy[cd, :] = gmc.astype(BF)

        cur = dot_a(0)
        prev = None
        for i in range(tiles + 1):
            nxt = dot_a(i + 1) if i + 1 < tiles else None
            gv = mul(i, cur) if i < tiles else None
            if i >= 1:
                leave(i - 1, prev)
            cur, prev = nxt, gv
        base = pl.multiple_of((layer ^ core_ref[0]) * PER, PER)
        for left, right, off, vec in ((v, dp[layer], 0, 8), (act, gm[...], 512, 9)):
            for h in range(2):
                hs = slice(h * 256, (h + 1) * 256)
                r = base + off + h * 256
                if h == 0:
                    p = with_sums(left[layer, :, hs], right)
                    acc[layer, vec, 0:1, :] = p[256:257]
                else:
                    p = tn(left[layer, :, hs], right)
                grads_ref[pl.ds(r, 256), :] = p[0:256].astype(BF)

    def mix_backward(layer):
        def cut(k):
            t, g = k // 4, k % 4
            return slice(t * ST, (t + 1) * ST), slice(g * 128, (g + 1) * 128), slice(g * 256, (g + 1) * 256), g

        def spectrum(t, h):
            hs = slice(h * 256, (h + 1) * 256)
            gr = nn(at[t * ST : (t + 1) * ST, :], gy[:, hs]).astype(BF)
            gi = nn(at[slots + t * ST : slots + (t + 1) * ST, :], gy[:, hs]).astype(BF)
            return gr, gi

        def dot_o(k, gr, gi):
            sl, cs, gl, g = cut(k)
            n, nbar = nm[sl, :], nb[sl, :]
            hs = slice(g % 2 * 128, g % 2 * 128 + 128)
            grc, gic = gr[:, hs], gi[:, hs]
            ds[layer, 0, sl, gl] = lanes2(grc, gic) * ds[layer, 0, sl, gl]
            ds[layer, 1, sl, gl] = lanes2(grc * n + gic * nbar, gic) * ds[layer, 1, sl, gl]
            return nt(both(ds, layer, sl, gl), w2g[layer, g])

        def dot_z(k, go):
            sl, cs, gl, g = cut(k)
            put(da, layer, sl, gl, go.astype(BF) * both(da, layer, sl, gl))
            return nt(both(da, layer, sl, gl), w1g[layer, g])

        def leave(k, gz):
            sl, cs, gl, g = cut(k)
            combine(pq, sl, cs, gz.astype(BF), False)

        steps = stiles * 4
        sp = {0: spectrum(0, 0)}
        go = dot_o(0, *sp[0])
        prev = None
        for k in range(steps + 1):
            if k % 2 == 0 and k + 2 < steps:
                sp[k // 2 + 1] = spectrum((k + 2) // 4, (k + 2) // 2 % 2)
            nxt = dot_o(k + 1, *sp[(k + 1) // 2]) if k + 1 < steps else None
            gz = dot_z(k, go) if k < steps else None
            if k >= 1:
                leave(k - 1, prev)
            go, prev = nxt, gz
        base = pl.multiple_of((layer ^ core_ref[0]) * PER, PER) + 1024
        low = lax.broadcasted_iota(jnp.int32, (64, 128), 1) < 64
        for left, right, off, vec in ((o, ds, base + 128, 4), (z, da, base, 2)):
            for g in range(4):
                cs = slice(g * 128, (g + 1) * 128)
                gl = slice(g * 256, (g + 1) * 256)
                lf = left[layer, :, :, gl].reshape(rows, 256)
                rt = right[layer, :, :, gl].reshape(rows, 256)
                p = with_sums(lf, rt)
                acc[layer, vec, 0:1, cs] = p[256:257, 0:128]
                acc[layer, vec + 1, 0:1, cs] = p[256:257, 128:256]
                re = p[0:128, 0:128] + p[128:256, 128:256]
                im = p[0:128, 128:256] - p[128:256, 0:128]
                grads_ref[pl.ds(off, 64), cs] = jnp.where(low, re[0:64], re[64:128]).astype(BF)
                grads_ref[pl.ds(off + 64, 64), cs] = jnp.where(low, im[0:64], im[64:128]).astype(BF)

    def in_backward(layer):
        def leave(i, y):
            for j in range(RT // CH):
                cd = chunk(i, j)
                gmc = gmid[cd, :]
                gu = y[j * CH : (j + 1) * CH] + gmc
                xh = xh1[layer, cd, :].astype(F32)
                add_to(layer, 0, gu * xh)
                add_to(layer, 1, gu)
                rstd = lanes(rs1[layer, cd, :], 4)
                gh = gmc + norm_back(gu, xh, rstd, n1g[pl.ds(min_layer(layer), 1), :])
                xg_ref[cd, :] = gh.astype(BF)
                g_s[cd, :] = gh

        y = nn(st[tile(0), :], pq[...])
        for i in range(tiles):
            nxt = nn(st[tile(i + 1), :], pq[...]) if i + 1 < tiles else None
            leave(i, y)
            y = nxt

    def vectors(layer):
        t = jnp.sum(acc[layer], 1)
        t = jnp.concatenate([t, jnp.zeros((PER - 1290, 512), F32)], 0)
        grads_ref[pl.ds(pl.multiple_of((layer ^ core_ref[0]) * PER, PER) + 1280, PER - 1280), :] = t.astype(BF)

    sends = [
        copy(8 + k, grads_ref.at[pl.ds(row, PER // 3)], dst)
        for k, (row, dst) in enumerate(
            (((3 * half + c) * (PER // 3), dst) for half, refs in ((1, (t0, t1, t2)), (0, (m0, m1, m2))) for c, dst in enumerate(refs))
        )
    ]

    def start_half(half):
        for h in range(2):

            @pl.when(half == h)
            def _():
                for c in sends[3 - 3 * h : 6 - 3 * h]:
                    c.start()

    @partial(lax.fori_loop, 0, LAYERS, init_val=0)
    def _(step, carry):
        layer = LAYERS - 1 - step
        block(lambda: ff_backward(layer))
        block(lambda: mix_backward(layer))
        block(lambda: in_backward(layer))

        @pl.when(step == 0)
        def _():
            vectors(1)
            start_half(1 - core_ref[0])

        return carry

    xg_copy = copy(7, xg_ref, xg_hbm)
    vectors(0)
    start_half(core_ref[0])
    xg_copy.start()
    out_copy.wait()
    for c in sends:
        c.wait()
    xg_copy.wait()


def lanes2(a, b):
    return jnp.concatenate([a, b], 1)


def local_step(core, x_in, cotangent, block_grid, keep_modes, n1g, n1b, w1, b1, w2, b2, n2g, n2b, fc1, fb1, fc2, fb2):
    rows, d = x_in.shape
    slots = rows // 2
    vm = pl.BlockSpec(memory_space=pltpu.VMEM)
    sm = pl.BlockSpec(memory_space=pltpu.SMEM)
    hbm = pl.BlockSpec(memory_space=pl.ANY)
    w1r = w1.reshape(LAYERS, 2, 512, 64)
    w2r = w2.reshape(LAYERS, 2, 512, 64)
    scratch = [
        pltpu.VMEM((rows, d), BF), pltpu.VMEM((rows, d), BF),
        pltpu.VMEM(w1r.shape, BF), pltpu.VMEM(w2r.shape, BF), pltpu.VMEM(fc1.shape, BF), pltpu.VMEM(fc2.shape, BF),
        pltpu.VMEM((rows, d), BF), pltpu.VMEM((LAYERS * PER, d), BF),
        pltpu.SemaphoreType.DMA((14,)),
        pltpu.VMEM((rows, rows), BF), pltpu.VMEM((rows, rows), BF),
        pltpu.VMEM((2, slots, 256), BF), pltpu.VMEM((2, slots, 256), BF),
        pltpu.VMEM((slots, 128), BF), pltpu.VMEM((slots, 128), BF),
        pltpu.VMEM((LAYERS, 4, 256, 256), BF), pltpu.VMEM((LAYERS, 4, 256, 256), BF),
        pltpu.VMEM((LAYERS + 1, rows, d), BF), pltpu.VMEM((LAYERS + 1, rows, 128), F32),
        pltpu.VMEM((rows, d), F32), pltpu.VMEM((rows, d), BF),
        pltpu.VMEM((LAYERS, 2, slots, 2 * d), BF), pltpu.VMEM((LAYERS, 2, slots, 2 * d), BF),
        pltpu.VMEM((LAYERS, 2, slots, 2 * d), BF), pltpu.VMEM((LAYERS, 2, slots, 2 * d), BF),
        pltpu.VMEM((rows, d), BF),
        pltpu.VMEM((LAYERS, rows, d), BF), pltpu.VMEM((LAYERS, rows, 128), F32),
        pltpu.VMEM((LAYERS, rows, d), BF), pltpu.VMEM((LAYERS, rows, d), BF), pltpu.VMEM((LAYERS, rows, d), BF),
        pltpu.VMEM((rows, d), F32),
        pltpu.VMEM((LAYERS, 10, 8, d), F32),
    ]
    return pl.pallas_call(
        kernel,
        out_shape=(
            jax.ShapeDtypeStruct((rows, d), BF),
            jax.ShapeDtypeStruct((rows, d), BF),
        )
        + (jax.ShapeDtypeStruct((PER // 3, d), BF),) * 6,
        in_specs=[sm, sm, sm, hbm, hbm, vm, vm, hbm, vm, hbm, vm, vm, vm, hbm, vm, hbm, vm],
        out_specs=(hbm,) * 8,
        scratch_shapes=scratch,
        compiler_params=pltpu.CompilerParams(vmem_limit_bytes=58 * 1024 * 1024),
        name="slab_step",
    )(block_grid, keep_modes, core, x_in, cotangent, n1g, n1b, w1r, b1, w2r, b2, n2g, n2b, fc1, fb1, fc2, fb2)


AXES = ("dp", "modes")


def spread_layer(layer, parts, outs, bufs, sems):
    fc1, fc2, w1, w2 = bufs
    p0, p1, p2 = parts
    n = PER // 3
    copies = [pltpu.make_async_copy(buf, out.at[layer], sems.at[k]) for k, (buf, out) in enumerate(zip(bufs, outs))]
    fc1[0:n, :] = p0[...].astype(F32)
    fc1[n:512, :] = p1[0 : 512 - n, :].astype(F32)
    copies[0].start()
    fc2[0 : 2 * n - 512, :] = p1[512 - n : n, :].astype(F32)
    fc2[2 * n - 512 : 512, :] = p2[0 : 1024 - 2 * n, :].astype(F32)
    copies[1].start()
    for k, (ref, base) in enumerate(((w1, 1024 - 2 * n), (w2, 1152 - 2 * n))):
        for part in range(2):
            block = p2[base + part * 64 : base + part * 64 + 64, :].astype(F32)
            for j in range(8):
                ref[part, j] = block[:, j * 64 : j * 64 + 64]
        copies[2 + k].start()
    return copies


def spread_mine(core_ref, a0, a1, a2, fc1_out, fc2_out, w1_out, w2_out, fc1, fc2, w1, w2, sems):
    for c in spread_layer(core_ref[0], (a0, a1, a2), (fc1_out, fc2_out, w1_out, w2_out), (fc1, fc2, w1, w2), sems):
        c.wait()


def spread_other(
    core_ref, a0, a1, a2, c0, c1, c2, fc1_in, fc2_in, w1_in, w2_in,
    fc1_out, fc2_out, w1_out, w2_out, n1g, n1b, b1, b2, n2g, n2b, fb1, fb2, fc1, fc2, w1, w2, sems,
):
    copies = spread_layer(1 - core_ref[0], (c0, c1, c2), (fc1_out, fc2_out, w1_out, w2_out), (fc1, fc2, w1, w2), sems)
    row = 1280 - 2 * (PER // 3)
    here = a2[row : row + 16, :].astype(F32)
    there = c2[row : row + 16, :].astype(F32)
    for layer in range(LAYERS):
        vec = jnp.where(core_ref[0] == layer, here, there)
        for row, ref in ((0, n1g), (1, n1b), (6, n2g), (7, n2b), (8, fb1), (9, fb2)):
            ref[layer : layer + 1, :] = vec[row : row + 1]
        b1[layer] = vec[2:4]
        b2[layer] = vec[4:6]
    for c in copies:
        c.wait()


def unpack_shapes(d):
    mix = jax.ShapeDtypeStruct((LAYERS, 2, 8, 64, 64), F32)
    full = jax.ShapeDtypeStruct((LAYERS, d, d), F32)
    big = (full, full, mix, mix)
    scratch = [pltpu.VMEM(s.shape[1:], F32) for s in big] + [pltpu.SemaphoreType.DMA((4,))]
    return big, scratch


def unpack_mine(core, mine, d):
    vm = pl.BlockSpec(memory_space=pltpu.VMEM)
    hbm = pl.BlockSpec(memory_space=pl.ANY)
    big, scratch = unpack_shapes(d)
    return pl.pallas_call(
        spread_mine,
        out_shape=big,
        in_specs=[pl.BlockSpec(memory_space=pltpu.SMEM), vm, vm, vm],
        out_specs=(hbm,) * 4,
        scratch_shapes=scratch,
        compiler_params=pltpu.CompilerParams(vmem_limit_bytes=16 * 1024 * 1024),
        cost_estimate=pl.CostEstimate(flops=1 << 20, bytes_accessed=4 << 20, transcendentals=0),
        name="spread_mine",
    )(core, *mine)


def unpack(core, mine, other, d, big_in=None):
    vm = pl.BlockSpec(memory_space=pltpu.VMEM)
    hbm = pl.BlockSpec(memory_space=pl.ANY)
    big, scratch = unpack_shapes(d)
    vec = jax.ShapeDtypeStruct((LAYERS, d), F32)
    pair = jax.ShapeDtypeStruct((LAYERS, 2, d), F32)
    if big_in is None:
        big_in = unpack_mine(core, mine, d)
    fc1, fc2, w1, w2, n1g, n1b, b1, b2, n2g, n2b, fb1, fb2 = pl.pallas_call(
        spread_other,
        out_shape=big + (vec, vec, pair, pair, vec, vec, vec, vec),
        in_specs=[pl.BlockSpec(memory_space=pltpu.SMEM)] + [vm] * 6 + [hbm] * 4,
        out_specs=(hbm,) * 4 + (vm,) * 8,
        scratch_shapes=scratch,
        input_output_aliases={7: 0, 8: 1, 9: 2, 10: 3},
        compiler_params=pltpu.CompilerParams(vmem_limit_bytes=16 * 1024 * 1024),
        name="spread_other",
    )(core, *mine, *other, *big_in)
    return n1g, n1b, w1, b1, w2, b2, n2g, n2b, fc1, fb1, fc2, fb2


def exchange(a, bit, count):
    return lax.ppermute(a, AXES, [(i, i ^ bit) for i in range(count)])


def add(a, b):
    return (a.astype(F32) + b.astype(F32)).astype(BF)


def all_sum(mine, other, count):
    me = lax.axis_index(AXES)
    top = count // 2
    bits = [1 << k for k in range(top.bit_length() - 1)]
    orders = [[bits[(c + k) % 3] for k in range(3)] for c in range(3)]
    gots = [exchange(t, top, count) for t in other]
    parts = [add(m, got) for m, got in zip(mine, gots)]
    for k in range(3):
        moved = []
        for c in range(3):
            n = parts[c].shape[0] // 2
            high = (me & orders[c][k]) != 0
            keep = jnp.where(high, parts[c][n:], parts[c][:n])
            send = jnp.where(high, parts[c][:n], parts[c][n:])
            moved.append((keep, exchange(send, orders[c][k], count)))
        parts = [add(keep, got) for keep, got in moved]
    for bit in bits[3:]:
        parts = [add(p, exchange(p, bit, count)) for p in parts]
    for k in reversed(range(3)):
        gots = [exchange(parts[c], orders[c][k], count) for c in range(3)]
        for c in range(3):
            high = (me & orders[c][k]) != 0
            low_part = jnp.where(high, gots[c], parts[c])
            high_part = jnp.where(high, parts[c], gots[c])
            parts[c] = jnp.concatenate([low_part, high_part])
    return parts, [exchange(p, top, count) for p in parts]


def solution(mesh):
    count = mesh.shape["dp"] * mesh.shape["modes"]

    def on_device(*args):
        core = lax.axis_index("dp").astype(jnp.int32).reshape(1)
        out, x_grad, *parts = local_step(core, *args)
        mine, other = all_sum(parts[:3], parts[3:], count)
        return (out, x_grad) + tuple(unpack(core, mine, other, out.shape[1]))

    rows = P(AXES, None)
    return jax.shard_map(
        on_device,
        mesh=mesh,
        in_specs=(rows, rows, P(AXES)) + (P(),) * 13,
        out_specs=(rows, rows) + (P(),) * 12,
        check_vma=False,
    )
```
